32 devices in a mesh: row: 8 (over y, x, core), col: 4 (over z).
Axes of the slice: x: 2, y: 2, z: 4, core: 2. Of those that a mesh axis runs over, the one named last changes fastest.
Arguments:
- density: bfloat16 [3072, 3072], P(('row', 'col')), may hold values from -0.6171875 to 0.6171875
- pattern: int32 [24, 24], replicated, may hold values 0 or 1
- filter_square: int32 [24, 24], replicated, may hold values 0 or 1
- filter_cube: int32 [24, 24], replicated, may hold values 0 or 1
Outputs:
- purified: float32 [3072, 3072], P('row', 'col')
The draws below stay inside these ranges and needn't reach their ends.
All inputs are finite; a program needn't handle non-finite values.
Results may differ from the reference program's by a relative error of at most 0.0027.
Values may be sent and summed in bfloat16 or wider, within the bound.
No kernel may reach another device: no remote copies, remote signals or barrier semaphores. Data moves between devices by JAX's collectives and lax.ppermute only.
A program may use at most 64 MiB of HBM per device.

```python
import jax
import jax.numpy as jnp

BLK = 128
ORDER = 3072
NBLOCKS = 24


def plant(result, rng, smallest, top_value):
    dims = result.shape
    spot = [jax.random.randint(jax.random.fold_in(rng, axis), (), 0, dims[axis]) for axis in range(len(dims))]
    result = result.at[tuple(spot)].set(smallest)
    longest = dims.index(max(dims))
    spot[longest] = (spot[longest] + 1) % dims[longest]
    return result.at[tuple(spot)].set(top_value)


def block_scale(rng, shape, shards, smallest, high):
    loudness, own = 1.0, jax.random.fold_in(rng, 6)
    for axis_at, blocks in shards:
        heights = jnp.exp(jax.random.uniform(jax.random.fold_in(own, axis_at), (blocks,), jnp.float32, smallest / len(shards), high / len(shards)))
        loudness = loudness * jnp.repeat(heights, shape[axis_at] // blocks).reshape([-1 if axis == axis_at else 1 for axis in range(len(shape))])
    return loudness


def gaussian(rng, extent, scale, bound, cuts=(), kind=jnp.bfloat16):
    loudness = block_scale(rng, extent, cuts, -0.22, 0.18) if cuts else 1.0
    values = jax.random.normal(rng, extent, jnp.float32) * scale * loudness
    return jnp.minimum(jnp.maximum(values, -bound), bound).astype(kind)


def setup_inputs(seed: int = 0) -> dict:
    key_of = jax.random.split(jax.random.key(seed), 5)
    density = gaussian(key_of[0], (ORDER, ORDER), (1.5 * ORDER ** -0.3333), 0.6171875, ((0, 32),))
    pattern = plant((jax.random.randint(key_of[1], (NBLOCKS, NBLOCKS), 0, 2) < 1).astype(jnp.int32), jax.random.fold_in(key_of[1], 1), 0, 1)
    filter_square = plant((jax.random.randint(key_of[2], (NBLOCKS, NBLOCKS), 0, 4) < 3).astype(jnp.int32), jax.random.fold_in(key_of[2], 1), 0, 1)
    filter_cube = plant((jax.random.randint(key_of[3], (NBLOCKS, NBLOCKS), 0, 4) < 3).astype(jnp.int32), jax.random.fold_in(key_of[3], 1), 0, 1)
    return {"density": density, "pattern": pattern, "filter_square": filter_square, "filter_cube": filter_cube}


def expand(mask):
    values = mask.astype(jnp.float32)
    return jnp.repeat(jnp.repeat(values, BLK, axis=0), BLK, axis=1)


def reference(density, pattern, filter_square, filter_cube):
    masked = (density.astype(jnp.float32) * expand(pattern)).astype(jnp.bfloat16)
    square = jnp.dot(masked, masked, preferred_element_type=jnp.float32) * expand(filter_square)
    square_half = square.astype(jnp.bfloat16)
    cube = jnp.dot(masked, square_half, preferred_element_type=jnp.float32) * expand(filter_cube)
    return 3.0 * square - 2.0 * cube
```

```python
import jax
import jax.numpy as jnp
from jax import lax
from jax.sharding import PartitionSpec as P

BLK = 128


def expand(mask, row_start, rows, col_start, cols, dtype):
    small = lax.dynamic_slice(
        mask, (row_start // BLK, col_start // BLK), (rows // BLK, cols // BLK)
    ).astype(dtype)
    return jnp.broadcast_to(
        small[:, None, :, None], (rows // BLK, BLK, cols // BLK, BLK)
    ).reshape(rows, cols)


def on_device(density, pattern, filter_square, filter_cube):
    row_count = lax.axis_size("row")
    col_count = lax.axis_size("col")
    row_id = lax.axis_index("row")
    col_id = lax.axis_index("col")
    order = density.shape[1]
    rows = order // row_count
    width = order // col_count
    row_at = row_id * rows
    col_at = col_id * width
    left = lax.all_gather(density, "col", axis=0, tiled=True)
    left = left * expand(pattern, row_at, rows, 0, order, jnp.bfloat16)
    tile = lax.dynamic_slice(left, (0, col_at), (rows, width))
    right = lax.all_gather(tile, "row", axis=0, tiled=True)
    square = jnp.dot(left, right, preferred_element_type=jnp.float32)
    square = square * expand(filter_square, row_at, rows, col_at, width, jnp.float32)
    half = lax.all_gather(square.astype(jnp.bfloat16), "row", axis=0, tiled=True)
    cube = jnp.dot(left, half, preferred_element_type=jnp.float32)
    cube = cube * expand(filter_cube, row_at, rows, col_at, width, jnp.float32)
    return 3.0 * square - 2.0 * cube


def solution(mesh):
    placed = (P(("row", "col"), None), P(), P(), P())
    return jax.shard_map(
        on_device, mesh=mesh, in_specs=placed, out_specs=P("row", "col"), check_vma=False
    )
```

```python
import functools

import jax
import jax.numpy as jnp
from jax import lax
from jax.experimental import pallas as pl
from jax.experimental.pallas import tpu as pltpu
from jax.sharding import PartitionSpec as P

BLK = 128


def expand(mask, row_start, rows, col_start, cols, dtype):
    small = lax.dynamic_slice(
        mask, (row_start // BLK, col_start // BLK), (rows // BLK, cols // BLK)
    ).astype(dtype)
    return jnp.broadcast_to(
        small[:, None, :, None], (rows // BLK, BLK, cols // BLK, BLK)
    ).reshape(rows, cols)


def xor_moved(block, axis, bit_of):
    size = lax.axis_size(axis)
    return lax.ppermute(block, axis, [(i, i ^ bit_of(i)) for i in range(size)])


def gather_row(tile):
    count = lax.axis_size("row")
    bits = [1 << b for b in range(1, count.bit_length() - 1)]
    pieces = [(tile, 0, 0)]
    for low, high in zip(bits, bits[::-1]):

        def bit_of(i, low=low, high=high):
            return high if i & 1 else low

        pieces = pieces + [
            (xor_moved(piece, "row", bit_of), even ^ low, odd ^ high)
            for piece, even, odd in pieces
        ]
    pieces = pieces + [
        (xor_moved(piece, "row", lambda i: 1), odd ^ 1, even ^ 1) for piece, even, odd in pieces
    ]
    odd_core = lax.axis_index("row") & 1
    places = [
        lax.axis_index("row") ^ jnp.where(odd_core == 1, odd, even) for _, even, odd in pieces
    ]
    return [piece for piece, _, _ in pieces], jnp.stack(places).astype(jnp.int32)


def product_kernel(count, places_ref, left_ref, *refs):
    right_refs = refs[:count]
    out_ref, left, right, sems = refs[count:]
    rows = right_refs[0].shape[0]
    copies = [pltpu.make_async_copy(left_ref, left, sems.at[count])]
    copies += [
        pltpu.make_async_copy(right_refs[j], right.at[j], sems.at[j]) for j in range(count)
    ]
    for copy in copies:
        copy.start()
    copies[0].wait()
    for j in range(count):
        copies[j + 1].wait()
        at = pl.multiple_of(places_ref[j] * rows, BLK)
        part = jnp.dot(
            left[:, pl.ds(at, rows)], right[j], preferred_element_type=jnp.float32
        )
        if j == 0:
            out_ref[...] = part
        else:
            out_ref[...] += part


def product(left, pieces, places):
    count = len(pieces)
    rows, width = pieces[0].shape
    order = left.shape[1]
    return pl.pallas_call(
        functools.partial(product_kernel, count),
        out_shape=jax.ShapeDtypeStruct((rows, width), jnp.float32),
        in_specs=[pl.BlockSpec(memory_space=pltpu.SMEM)]
        + [pl.BlockSpec(memory_space=pl.ANY)] * (count + 1),
        out_specs=pl.BlockSpec(memory_space=pltpu.VMEM),
        scratch_shapes=[
            pltpu.VMEM((rows, order), jnp.bfloat16),
            pltpu.VMEM((count, rows, width), jnp.bfloat16),
            pltpu.SemaphoreType.DMA((count + 1,)),
        ],
        compiler_params=pltpu.CompilerParams(vmem_limit_bytes=40 << 20),
        cost_estimate=pl.CostEstimate(
            flops=2 * rows * order * width,
            bytes_accessed=2 * order * (rows + width) + 4 * rows * width,
            transcendentals=0,
        ),
    )(places, left, *pieces)


def on_device(density, pattern, filter_square, filter_cube):
    row_count = lax.axis_size("row")
    col_count = lax.axis_size("col")
    row_id = lax.axis_index("row")
    col_id = lax.axis_index("col")
    order = density.shape[1]
    rows = order // row_count
    width = order // col_count
    row_at = row_id * rows
    col_at = col_id * width
    left = lax.all_gather(density, "col", axis=0, tiled=True)
    tile = lax.all_to_all(
        density.reshape(-1, 1, col_count, width), "col", split_axis=2, concat_axis=0, tiled=True
    ).reshape(rows, width)
    tile = tile * expand(pattern, row_at, rows, col_at, width, jnp.bfloat16)
    right, places = gather_row(tile)
    left = left * expand(pattern, row_at, rows, 0, order, jnp.bfloat16)
    square = product(left, right, places)
    square = square * expand(filter_square, row_at, rows, col_at, width, jnp.float32)
    half, places = gather_row(square.astype(jnp.bfloat16))
    cube = product(left, half, places)
    cube = cube * expand(filter_cube, row_at, rows, col_at, width, jnp.float32)
    return 3.0 * square - 2.0 * cube


def solution(mesh):
    placed = (P(("row", "col"), None), P(), P(), P())
    return jax.shard_map(
        on_device, mesh=mesh, in_specs=placed, out_specs=P("row", "col"), check_vma=False
    )
```

```python
import functools

import jax
import jax.numpy as jnp
from jax import lax
from jax.experimental import pallas as pl
from jax.experimental.pallas import tpu as pltpu
from jax.sharding import PartitionSpec as P

BLK = 128
VMEM = pl.BlockSpec(memory_space=pltpu.VMEM)


def shifted(block, axis, distance):
    size = lax.axis_size(axis)
    return lax.ppermute(block, axis, [(i, (i + distance) % size) for i in range(size)])


def xor_moved(block, axis, bit_of):
    size = lax.axis_size(axis)
    return lax.ppermute(block, axis, [(i, i ^ bit_of(i)) for i in range(size)])


def row_places(count):
    bits = [1 << b for b in range(1, count.bit_length() - 1)]
    places = [(0, 0)]
    for low, high in zip(bits, bits[::-1]):
        places = places + [(even ^ low, odd ^ high) for even, odd in places]
    return places + [(odd ^ 1, even ^ 1) for even, odd in places]


def gather_row(block):
    count = lax.axis_size("row")
    bits = [1 << b for b in range(1, count.bit_length() - 1)]
    pieces = [block]
    for low, high in zip(bits, bits[::-1]):

        def bit_of(i, low=low, high=high):
            return high if i & 1 else low

        pieces = pieces + [xor_moved(piece, "row", bit_of) for piece in pieces]
    return pieces + [xor_moved(piece, "row", lambda i: 1) for piece in pieces]


def iota(shape, axis):
    return lax.broadcasted_iota(jnp.int32, shape, axis)


def expand(mask, row_start, rows, col_start, cols):
    nblocks = mask.shape[0]
    pick_row = (row_start + iota((rows, nblocks), 0)) // BLK == iota((rows, nblocks), 1)
    pick_col = (col_start + iota((nblocks, cols), 1)) // BLK == iota((nblocks, cols), 0)
    lines = jnp.dot(
        pick_row.astype(jnp.bfloat16),
        mask.astype(jnp.float32).astype(jnp.bfloat16),
        preferred_element_type=jnp.float32,
    )
    return jnp.dot(
        lines.astype(jnp.bfloat16),
        pick_col.astype(jnp.bfloat16),
        preferred_element_type=jnp.float32,
    )


def mask_kernel(col_count, pattern_ref, density_ref, local_ref, *piece_refs):
    rows_one, order = density_ref.shape
    width = order // col_count
    col_id = lax.axis_index("col")
    first = (lax.axis_index("row") * col_count + col_id) * rows_one
    full = expand(pattern_ref[...], first, rows_one, 0, order).astype(jnp.bfloat16)
    local_ref[...] = density_ref[...] * full
    for shift, piece_ref in enumerate(piece_refs):
        at = pl.multiple_of(lax.rem(col_id + shift, col_count) * width, BLK)
        piece_ref[...] = local_ref[:, pl.ds(at, width)]


def masked_pieces(density, pattern):
    col_count = lax.axis_size("col")
    rows_one, order = density.shape
    whole = jax.ShapeDtypeStruct((rows_one, order), jnp.bfloat16)
    piece = jax.ShapeDtypeStruct((rows_one, order // col_count), jnp.bfloat16)
    local, *pieces = pl.pallas_call(
        functools.partial(mask_kernel, col_count),
        out_shape=[whole] + [piece] * col_count,
        in_specs=[VMEM] * 2,
        out_specs=[VMEM] * (col_count + 1),
        name="mask",
    )(pattern, density)
    return local, pieces


def sub_at(shift, col_count, rows_one):
    return pl.multiple_of(
        lax.rem(lax.axis_index("col") + (col_count - shift), col_count) * rows_one, 16
    )


def fill_left(left, left_refs, shifts, col_count):
    rows_one = left_refs[0].shape[0]
    for shift, left_ref in zip(shifts, left_refs):
        left[pl.ds(sub_at(shift, col_count, rows_one), rows_one), :] = left_ref[...]


def fill_right(right, chunk_refs, chunk_shifts, sizes):
    row_count, col_count = sizes
    order = right.shape[0]
    rows = order // row_count
    rows_one = rows // col_count
    row_id = lax.axis_index("row")
    odd_core = lax.rem(row_id, 2) == 1
    for refs, shifts in zip(chunk_refs, chunk_shifts):
        for ref, (even, odd) in zip(refs, row_places(row_count)):
            place = pl.multiple_of((row_id ^ jnp.where(odd_core, odd, even)) * rows, BLK)
            for slot, shift in enumerate(shifts):
                at = pl.multiple_of(place + sub_at(shift, col_count, rows_one), 16)
                right[pl.ds(at, rows_one), :] = ref[slot * rows_one : (slot + 1) * rows_one, :]


def split_refs(refs, counts):
    groups = []
    for count in counts:
        groups.append(refs[:count])
        refs = refs[count:]
    return groups + [refs]


def square_kernel(sizes, left_shifts, chunk_shifts, filter_ref, *refs):
    row_count, col_count = sizes
    counts = [len(left_shifts)] + [row_count] * len(chunk_shifts)
    left_refs, *chunk_refs, rest = split_refs(refs, counts)
    square_ref, half_ref, left, right = rest
    rows, width = square_ref.shape
    fill_left(left, left_refs, left_shifts, col_count)
    fill_right(right, chunk_refs, chunk_shifts, sizes)
    row_at = lax.axis_index("row") * rows
    col_at = lax.axis_index("col") * width
    keep = expand(filter_ref[...], row_at, rows, col_at, width)
    total = jnp.dot(left[...], right[...], preferred_element_type=jnp.float32) * keep
    square_ref[...] = total
    half_ref[...] = total.astype(jnp.bfloat16)


def cube_kernel(sizes, left_shifts, filter_ref, square_ref, *refs):
    row_count, col_count = sizes
    left_refs, right_refs, rest = split_refs(refs, [len(left_shifts), row_count])
    out_ref, left = rest
    rows, width = square_ref.shape
    fill_left(left, left_refs, left_shifts, col_count)
    row_id = lax.axis_index("row")
    odd_core = lax.rem(row_id, 2) == 1
    total = jnp.zeros((rows, width), jnp.float32)
    for ref, (even, odd) in zip(right_refs, row_places(row_count)):
        place = pl.multiple_of((row_id ^ jnp.where(odd_core, odd, even)) * rows, BLK)
        total = total + jnp.dot(
            left[:, pl.ds(place, rows)], ref[...], preferred_element_type=jnp.float32
        )
    row_at = row_id * rows
    col_at = lax.axis_index("col") * width
    keep = expand(filter_ref[...], row_at, rows, col_at, width)
    out_ref[...] = 3.0 * square_ref[...] - 2.0 * (total * keep)


def cost(rows, order, width):
    return pl.CostEstimate(
        flops=2 * rows * order * width,
        bytes_accessed=2 * order * (rows + width) + 4 * rows * width,
        transcendentals=0,
    )


def on_device(density, pattern, filter_square, filter_cube):
    sizes = (lax.axis_size("row"), lax.axis_size("col"))
    row_count, col_count = sizes
    order = density.shape[1]
    rows = order // row_count
    width = order // col_count
    tile32 = jax.ShapeDtypeStruct((rows, width), jnp.float32)
    tile16 = jax.ShapeDtypeStruct((rows, width), jnp.bfloat16)
    local, pieces = masked_pieces(density, pattern)

    early = gather_row(pieces[0])
    others = [shifted(pieces[shift], "col", shift) for shift in range(1, col_count)]
    late = gather_row(jnp.concatenate(others, axis=0))
    chunk_shifts = [[0], list(range(1, col_count))]

    source = lax.optimization_barrier((local, *others))[0]
    lefts, left_shifts = [local], [0]
    up, down = source, source
    for step in range(1, col_count // 2 + 1):
        up = shifted(up, "col", 1)
        lefts.append(up)
        left_shifts.append(step)
        if step < col_count // 2:
            down = shifted(down, "col", -1)
            lefts.append(down)
            left_shifts.append(col_count - step)

    params = pltpu.CompilerParams(vmem_limit_bytes=30 << 20)
    left_scratch = pltpu.VMEM((rows, order), jnp.bfloat16)
    square, half = pl.pallas_call(
        functools.partial(square_kernel, sizes, left_shifts, chunk_shifts),
        out_shape=[tile32, tile16],
        in_specs=[VMEM] * (1 + len(lefts) + 2 * row_count),
        out_specs=[VMEM] * 2,
        scratch_shapes=[left_scratch, pltpu.VMEM((order, width), jnp.bfloat16)],
        compiler_params=params,
        cost_estimate=cost(rows, order, width),
        name="square",
    )(filter_square, *lefts, *early, *late)
    halves = gather_row(half)
    return pl.pallas_call(
        functools.partial(cube_kernel, sizes, left_shifts),
        out_shape=tile32,
        in_specs=[VMEM] * (2 + len(lefts) + row_count),
        out_specs=VMEM,
        scratch_shapes=[left_scratch],
        compiler_params=params,
        cost_estimate=cost(rows, order, width),
        name="cube",
    )(filter_cube, square, *lefts, *halves)


def solution(mesh):
    placed = (P(("row", "col"), None), P(), P(), P())
    return jax.shard_map(
        on_device, mesh=mesh, in_specs=placed, out_specs=P("row", "col"), check_vma=False
    )
```

```python
import functools

import jax
import jax.numpy as jnp
from jax import lax
from jax.experimental import pallas as pl
from jax.experimental.pallas import tpu as pltpu
from jax.sharding import PartitionSpec as P

BLK = 128
VMEM = pl.BlockSpec(memory_space=pltpu.VMEM)


def shifted(block, axis, distance):
    size = lax.axis_size(axis)
    return lax.ppermute(block, axis, [(i, (i + distance) % size) for i in range(size)])


def xor_moved(block, axis, bit_of):
    size = lax.axis_size(axis)
    return lax.ppermute(block, axis, [(i, i ^ bit_of(i)) for i in range(size)])


def row_places(count):
    bits = [1 << b for b in range(1, count.bit_length() - 1)]
    places = [(0, 0)]
    for low, high in zip(bits, bits[::-1]):
        places = places + [(even ^ low, odd ^ high) for even, odd in places]
    return places + [(odd ^ 1, even ^ 1) for even, odd in places]


def gather_row(block):
    count = lax.axis_size("row")
    bits = [1 << b for b in range(1, count.bit_length() - 1)]
    pieces = [block]
    for low, high in zip(bits, bits[::-1]):

        def bit_of(i, low=low, high=high):
            return high if i & 1 else low

        pieces = pieces + [xor_moved(piece, "row", bit_of) for piece in pieces]
    return pieces + [xor_moved(piece, "row", lambda i: 1) for piece in pieces]


def iota(shape, axis):
    return lax.broadcasted_iota(jnp.int32, shape, axis)


def expand(mask, row_start, rows, col_start, cols):
    nblocks = mask.shape[0]
    pick_row = (row_start + iota((rows, nblocks), 0)) // BLK == iota((rows, nblocks), 1)
    pick_col = (col_start + iota((nblocks, cols), 1)) // BLK == iota((nblocks, cols), 0)
    lines = jnp.dot(
        pick_row.astype(jnp.bfloat16),
        mask.astype(jnp.float32).astype(jnp.bfloat16),
        preferred_element_type=jnp.float32,
    )
    return jnp.dot(
        lines.astype(jnp.bfloat16),
        pick_col.astype(jnp.bfloat16),
        preferred_element_type=jnp.float32,
    )


def mask_kernel(col_count, pattern_ref, density_ref, local_ref, up_ref, down_ref, *piece_refs):
    rows_one, order = density_ref.shape
    width = order // col_count
    col_id = lax.axis_index("col")
    first = (lax.axis_index("row") * col_count + col_id) * rows_one
    full = expand(pattern_ref[...], first, rows_one, 0, order).astype(jnp.bfloat16)
    local_ref[...] = density_ref[...] * full
    for shift, piece_ref in enumerate(piece_refs):
        piece = local_ref[:, pl.ds(block_at(shift, col_count, width), width)]
        piece_ref[...] = piece
        if shift != 1:
            slot = (shift - 2) % col_count
            up_ref[:, slot * width : (slot + 1) * width] = piece
        if shift != col_count - 1:
            down_ref[:, shift * width : (shift + 1) * width] = piece


def masked_pieces(density, pattern):
    col_count = lax.axis_size("col")
    rows_one, order = density.shape
    width = order // col_count
    shapes = [order, order - width, order - width] + [width] * col_count
    local, up, down, *pieces = pl.pallas_call(
        functools.partial(mask_kernel, col_count),
        out_shape=[jax.ShapeDtypeStruct((rows_one, cols), jnp.bfloat16) for cols in shapes],
        in_specs=[VMEM] * 2,
        out_specs=[VMEM] * len(shapes),
        name="mask",
    )(pattern, density)
    return local, up, down, pieces


def block_at(shift, col_count, width):
    return pl.multiple_of(lax.rem(lax.axis_index("col") + shift, col_count) * width, BLK)


def sub_at(shift, col_count, rows_one):
    return pl.multiple_of(
        lax.rem(lax.axis_index("col") + (col_count - shift), col_count) * rows_one, 16
    )


def fill_right(right, chunk_refs, chunk_shifts, sizes):
    row_count, col_count = sizes
    order = right.shape[0]
    rows = order // row_count
    rows_one = rows // col_count
    row_id = lax.axis_index("row")
    odd_core = lax.rem(row_id, 2) == 1
    for refs, shifts in zip(chunk_refs, chunk_shifts):
        for ref, (even, odd) in zip(refs, row_places(row_count)):
            place = pl.multiple_of((row_id ^ jnp.where(odd_core, odd, even)) * rows, BLK)
            for slot, shift in enumerate(shifts):
                at = pl.multiple_of(place + sub_at(shift, col_count, rows_one), 16)
                right[pl.ds(at, rows_one), :] = ref[slot * rows_one : (slot + 1) * rows_one, :]


def split_refs(refs, counts):
    groups = []
    for count in counts:
        groups.append(refs[:count])
        refs = refs[count:]
    return groups + [refs]


def fill_left(left, first, whole_refs, pair_refs, col_count, rows_one):
    at = first
    for ref in whole_refs:
        left[at : at + ref.shape[0], :] = ref[...]
        at += ref.shape[0]
    for most_ref, own_ref in zip(pair_refs[::2], pair_refs[1::2]):
        width = own_ref.shape[1]
        left[at : at + rows_one, pl.ds(block_at(0, col_count, width), width)] = own_ref[...]
        for slot in range(col_count - 1):
            left[at : at + rows_one, pl.ds(block_at(slot + 1, col_count, width), width)] = most_ref[
                :, slot * width : (slot + 1) * width
            ]
        at += rows_one


def keep_of(filter_ref, shift, col_count, rows_one, width):
    row_at = lax.axis_index("row") * (rows_one * col_count) + sub_at(shift, col_count, rows_one)
    col_at = lax.axis_index("col") * width
    return expand(filter_ref[...], row_at, rows_one, col_at, width)


def square_part(left, right, shifts, col_count, filter_ref, square_ref, half_ref):
    rows_one = square_ref.shape[0] // len(shifts)
    width = square_ref.shape[1]
    total = jnp.dot(left, right, preferred_element_type=jnp.float32)
    for slot, shift in enumerate(shifts):
        at = slice(slot * rows_one, (slot + 1) * rows_one)
        part = total[at] * keep_of(filter_ref, shift, col_count, rows_one, width)
        square_ref[at, :] = part
        half_ref[at, :] = part.astype(jnp.bfloat16)


def square_first_kernel(sizes, shifts, chunk_shifts, filter_ref, local_ref, *refs):
    row_count, col_count = sizes
    counts = [2 * len(shifts) - 2] + [row_count] * len(chunk_shifts)
    pair_refs, *chunk_refs, rest = split_refs(refs, counts)
    square_ref, half_ref, left_ref, right_ref = rest
    fill_left(left_ref, 0, [local_ref], pair_refs, col_count, local_ref.shape[0])
    fill_right(right_ref, chunk_refs, chunk_shifts, sizes)
    square_part(
        left_ref[...], right_ref[...], shifts, col_count, filter_ref, square_ref, half_ref
    )


def square_last_kernel(sizes, shifts, filter_ref, right_ref, before_ref, *refs):
    col_count = sizes[1]
    pair_refs, (square_ref, half_ref, left_ref) = refs[: 2 * len(shifts)], refs[2 * len(shifts) :]
    before = before_ref.shape[0]
    fill_left(left_ref, 0, [before_ref], pair_refs, col_count, pair_refs[0].shape[0])
    square_part(
        left_ref[before:, :], right_ref[...], shifts, col_count, filter_ref, square_ref, half_ref
    )


def cube_kernel(sizes, chunk_shifts, filter_ref, left_ref, *refs):
    row_count, col_count = sizes
    counts = [len(chunk_shifts)] + [row_count] * len(chunk_shifts)
    square_refs, *chunk_refs, rest = split_refs(refs, counts)
    out_ref, right = rest
    rows, width = out_ref.shape
    rows_one = rows // col_count
    fill_right(right, chunk_refs, chunk_shifts, sizes)
    total = jnp.dot(left_ref[...], right[...], preferred_element_type=jnp.float32)
    row = 0
    for square_ref, shifts in zip(square_refs, chunk_shifts):
        for slot, shift in enumerate(shifts):
            keep = keep_of(filter_ref, shift, col_count, rows_one, width)
            square = square_ref[slot * rows_one : (slot + 1) * rows_one, :]
            out_ref[pl.ds(sub_at(shift, col_count, rows_one), rows_one), :] = 3.0 * square - 2.0 * (
                total[row : row + rows_one] * keep
            )
            row += rows_one


def kernel_call(kernel, name, out_shape, inputs, product, scratch=()):
    rows, order, width = product
    return pl.pallas_call(
        kernel,
        out_shape=out_shape,
        in_specs=[VMEM] * len(inputs),
        out_specs=jax.tree.map(lambda shape: VMEM, out_shape),
        scratch_shapes=scratch,
        compiler_params=pltpu.CompilerParams(vmem_limit_bytes=24 << 20),
        cost_estimate=pl.CostEstimate(
            flops=2 * rows * order * width,
            bytes_accessed=2 * order * (rows + width) + 6 * rows * width,
            transcendentals=0,
        ),
        name=name,
    )(*inputs)


def on_device(density, pattern, filter_square, filter_cube):
    sizes = (lax.axis_size("row"), lax.axis_size("col"))
    row_count, col_count = sizes
    rows_one, order = density.shape
    rows = order // row_count
    width = order // col_count

    def shape(height, cols, dtype):
        return jax.ShapeDtypeStruct((height, cols), dtype)

    local, up, down, pieces = masked_pieces(density, pattern)

    early = gather_row(pieces[0])
    came = {shift: shifted(pieces[shift], "col", shift) for shift in range(1, col_count)}
    others = [came[shift] for shift in range(1, col_count)]
    up, down, *others = lax.optimization_barrier((up, down, *others, *early[: row_count // 2]))[
        : col_count + 1
    ]
    late = gather_row(jnp.concatenate(others, axis=0))

    steps = col_count // 2
    up_shifts, down_shifts = list(range(1, steps + 1)), list(range(col_count - 1, steps, -1))
    ups, downs = [], []
    for step in range(1, steps + 1):
        up = shifted(up, "col", 1)
        ups += [up, came[step]]
        if step == steps:
            break
        down = shifted(down, "col", -1)
        up, down = lax.optimization_barrier((up, down))
        downs += [down, came[col_count - step]]
        up = jnp.concatenate([up[:, width:], came[step]], axis=1)
        down = jnp.concatenate([came[col_count - step], down[:, :-width]], axis=1)
    first_shifts, last_shifts = [0] + up_shifts[:-1], down_shifts + up_shifts[-1:]
    first_pairs, last_pairs = ups[:-2], downs + ups[-2:]

    part = rows // 2
    square_first, half_first, left_first, right = kernel_call(
        functools.partial(
            square_first_kernel, sizes, first_shifts, [[0], list(range(1, col_count))]
        ),
        "square_first",
        [
            shape(part, width, jnp.float32),
            shape(part, width, jnp.bfloat16),
            shape(part, order, jnp.bfloat16),
            shape(order, width, jnp.bfloat16),
        ],
        [filter_square, local, *first_pairs, *early, *late],
        (part, order, width),
    )
    halves_first = gather_row(half_first)
    right = lax.optimization_barrier((right, *halves_first[1 : row_count // 2 - 1]))[0]
    square_last, half_last, left = kernel_call(
        functools.partial(square_last_kernel, sizes, last_shifts),
        "square_last",
        [
            shape(part, width, jnp.float32),
            shape(part, width, jnp.bfloat16),
            shape(rows, order, jnp.bfloat16),
        ],
        [filter_square, right, left_first, *last_pairs],
        (part, order, width),
    )
    halves_last = gather_row(half_last)
    return kernel_call(
        functools.partial(cube_kernel, sizes, [first_shifts, last_shifts]),
        "cube",
        shape(rows, width, jnp.float32),
        [filter_cube, left, square_first, square_last, *halves_first, *halves_last],
        (rows, order, width),
        [pltpu.VMEM((order, width), jnp.bfloat16)],
    )


def solution(mesh):
    placed = (P(("row", "col"), None), P(), P(), P())
    return jax.shard_map(
        on_device, mesh=mesh, in_specs=placed, out_specs=P("row", "col"), check_vma=False
    )
```

```python
import functools

import jax
import jax.numpy as jnp
from jax import lax
from jax.experimental import pallas as pl
from jax.experimental.pallas import tpu as pltpu
from jax.sharding import PartitionSpec as P

BLK = 128
VMEM = pl.BlockSpec(memory_space=pltpu.VMEM)


def shifted(block, axis, distance):
    size = lax.axis_size(axis)
    return lax.ppermute(block, axis, [(i, (i + distance) % size) for i in range(size)])


def xor_moved(block, axis, bit_of):
    size = lax.axis_size(axis)
    return lax.ppermute(block, axis, [(i, i ^ bit_of(i)) for i in range(size)])


def hops(block, shifts, hold=lambda piece: piece):
    count = lax.axis_size("row")
    bits = [1 << b for b in range(1, count.bit_length() - 1)]
    items = [(block, 0, 0)]
    for low, high in zip(bits, bits[::-1]):

        def bit_of(i, low=low, high=high):
            return high if i & 1 else low

        items = items + [
            (xor_moved(piece if even == 0 else hold(piece), "row", bit_of), even ^ low, odd ^ high)
            for piece, even, odd in items
        ]
    return [(piece, [(even, odd, shifts)]) for piece, even, odd in items]


def hint(flops):
    return pl.CostEstimate(flops=flops, bytes_accessed=0, transcendentals=0)


def join_kernel(*refs):
    *piece_refs, out_ref = refs
    row = 0
    for ref in piece_refs:
        out_ref[row : row + ref.shape[0], :] = ref[...]
        row += ref.shape[0]


def swap_cores(items, flops):
    pieces = [piece for piece, _ in items]
    joined = pieces[0]
    if len(pieces) > 1:
        rows = sum(piece.shape[0] for piece in pieces)
        joined = pl.pallas_call(
            join_kernel,
            out_shape=jax.ShapeDtypeStruct((rows, pieces[0].shape[1]), jnp.bfloat16),
            in_specs=[VMEM] * len(pieces),
            out_specs=VMEM,
            cost_estimate=hint(flops),
            name="join",
        )(*pieces)
    held = [(odd ^ 1, even ^ 1, shifts) for _, parts in items for even, odd, shifts in parts]
    return xor_moved(joined, "row", lambda i: 1), held


def iota(shape, axis):
    return lax.broadcasted_iota(jnp.int32, shape, axis)


def expand(mask, row_start, rows, col_start, cols):
    nblocks = mask.shape[0]
    pick_row = (row_start + iota((rows, nblocks), 0)) // BLK == iota((rows, nblocks), 1)
    pick_col = (col_start + iota((nblocks, cols), 1)) // BLK == iota((nblocks, cols), 0)
    lines = jnp.dot(
        pick_row.astype(jnp.bfloat16),
        mask.astype(jnp.float32).astype(jnp.bfloat16),
        preferred_element_type=jnp.float32,
    )
    return jnp.dot(
        lines.astype(jnp.bfloat16),
        pick_col.astype(jnp.bfloat16),
        preferred_element_type=jnp.float32,
    )


def mask_kernel(col_count, pattern_ref, density_ref, local_ref, up_ref, down_ref, *piece_refs):
    rows_one, order = density_ref.shape
    width = order // col_count
    col_id = lax.axis_index("col")
    first = (lax.axis_index("row") * col_count + col_id) * rows_one
    full = expand(pattern_ref[...], first, rows_one, 0, order).astype(jnp.bfloat16)
    local_ref[...] = density_ref[...] * full
    for shift, piece_ref in enumerate(piece_refs):
        piece = local_ref[:, pl.ds(block_at(shift, col_count, width), width)]
        piece_ref[...] = piece
        if shift != 1:
            slot = (shift - 2) % col_count
            up_ref[:, slot * width : (slot + 1) * width] = piece
        if shift != col_count - 1:
            down_ref[:, shift * width : (shift + 1) * width] = piece


def masked_pieces(density, pattern):
    col_count = lax.axis_size("col")
    rows_one, order = density.shape
    width = order // col_count
    shapes = [order, order - width, order - width] + [width] * col_count
    local, up, down, *pieces = pl.pallas_call(
        functools.partial(mask_kernel, col_count),
        out_shape=[jax.ShapeDtypeStruct((rows_one, cols), jnp.bfloat16) for cols in shapes],
        in_specs=[VMEM] * 2,
        out_specs=[VMEM] * len(shapes),
        name="mask",
    )(pattern, density)
    return local, up, down, pieces


def block_at(shift, col_count, width):
    return pl.multiple_of(lax.rem(lax.axis_index("col") + shift, col_count) * width, BLK)


def sub_at(shift, col_count, rows_one):
    return pl.multiple_of(
        lax.rem(lax.axis_index("col") + (col_count - shift), col_count) * rows_one, 16
    )


def fill_right(right, refs, layouts, sizes):
    row_count, col_count = sizes
    rows = right.shape[0] // row_count
    rows_one = rows // col_count
    row_id = lax.axis_index("row")
    odd_core = lax.rem(row_id, 2) == 1
    for ref, held in zip(refs, layouts):
        row = 0
        for even, odd, shifts in held:
            place = pl.multiple_of((row_id ^ jnp.where(odd_core, odd, even)) * rows, BLK)
            for shift in shifts:
                at = pl.multiple_of(place + sub_at(shift, col_count, rows_one), 16)
                right[pl.ds(at, rows_one), :] = ref[row : row + rows_one, :]
                row += rows_one


def split_refs(refs, counts):
    groups = []
    for count in counts:
        groups.append(refs[:count])
        refs = refs[count:]
    return groups + [refs]


def fill_left(left, first, whole_refs, pair_refs, col_count, rows_one):
    at = first
    for ref in whole_refs:
        left[at : at + ref.shape[0], :] = ref[...]
        at += ref.shape[0]
    for most_ref, own_ref in zip(pair_refs[::2], pair_refs[1::2]):
        width = own_ref.shape[1]
        left[at : at + rows_one, pl.ds(block_at(0, col_count, width), width)] = own_ref[...]
        for slot in range(col_count - 1):
            left[at : at + rows_one, pl.ds(block_at(slot + 1, col_count, width), width)] = most_ref[
                :, slot * width : (slot + 1) * width
            ]
        at += rows_one


def keep_kernel(square_filter_ref, cube_filter_ref, square_ref, cube_ref):
    rows, width = square_ref.shape
    row_at, col_at = lax.axis_index("row") * rows, lax.axis_index("col") * width
    for filter_ref, keep_ref in ((square_filter_ref, square_ref), (cube_filter_ref, cube_ref)):
        keep_ref[...] = expand(filter_ref[...], row_at, rows, col_at, width)


def keep_masks(filter_square, filter_cube, rows, width):
    return pl.pallas_call(
        keep_kernel,
        out_shape=[jax.ShapeDtypeStruct((rows, width), jnp.float32)] * 2,
        in_specs=[VMEM] * 2,
        out_specs=[VMEM] * 2,
        cost_estimate=hint(2 * 10**10),
        name="keep",
    )(filter_square, filter_cube)


def square_part(left, right, shifts, col_count, keep_ref, square_ref, half_ref):
    rows_one = square_ref.shape[0] // len(shifts)
    total = jnp.dot(left, right, preferred_element_type=jnp.float32)
    for slot, shift in enumerate(shifts):
        at = slice(slot * rows_one, (slot + 1) * rows_one)
        part = total[at] * keep_ref[pl.ds(sub_at(shift, col_count, rows_one), rows_one), :]
        square_ref[at, :] = part
        half_ref[at, :] = part.astype(jnp.bfloat16)


def square_first_kernel(sizes, shifts, layouts, keep_ref, local_ref, *refs):
    col_count = sizes[1]
    pair_refs, piece_refs, rest = split_refs(refs, [2 * len(shifts) - 2, len(layouts)])
    square_ref, half_ref, left_ref, right_ref = rest
    fill_left(left_ref, 0, [local_ref], pair_refs, col_count, local_ref.shape[0])
    fill_right(right_ref, piece_refs, layouts, sizes)
    square_part(
        left_ref[...], right_ref[...], shifts, col_count, keep_ref, square_ref, half_ref
    )


def square_last_kernel(sizes, shifts, keep_ref, right_ref, before_ref, *refs):
    col_count = sizes[1]
    pair_refs, (square_ref, half_ref, left_ref) = refs[: 2 * len(shifts)], refs[2 * len(shifts) :]
    before = before_ref.shape[0]
    fill_left(left_ref, 0, [before_ref], pair_refs, col_count, pair_refs[0].shape[0])
    square_part(
        left_ref[before:, :], right_ref[...], shifts, col_count, keep_ref, square_ref, half_ref
    )


def cube_kernel(sizes, chunk_shifts, layouts, keep_ref, left_ref, *refs):
    col_count = sizes[1]
    square_refs, piece_refs, rest = split_refs(refs, [len(chunk_shifts), len(layouts)])
    out_ref, right = rest
    rows, width = out_ref.shape
    rows_one = rows // col_count
    fill_right(right, piece_refs, layouts, sizes)
    total = jnp.dot(left_ref[...], right[...], preferred_element_type=jnp.float32)
    row = 0
    for square_ref, shifts in zip(square_refs, chunk_shifts):
        for slot, shift in enumerate(shifts):
            at = pl.ds(sub_at(shift, col_count, rows_one), rows_one)
            square = square_ref[slot * rows_one : (slot + 1) * rows_one, :]
            out_ref[at, :] = 3.0 * square - 2.0 * (total[row : row + rows_one] * keep_ref[at, :])
            row += rows_one


def kernel_call(kernel, name, out_shape, inputs, product, scratch=()):
    rows, order, width = product
    return pl.pallas_call(
        kernel,
        out_shape=out_shape,
        in_specs=[VMEM] * len(inputs),
        out_specs=jax.tree.map(lambda shape: VMEM, out_shape),
        scratch_shapes=scratch,
        compiler_params=pltpu.CompilerParams(vmem_limit_bytes=24 << 20),
        cost_estimate=pl.CostEstimate(
            flops=2 * rows * order * width,
            bytes_accessed=2 * order * (rows + width) + 6 * rows * width,
            transcendentals=0,
        ),
        name=name,
    )(*inputs)


def on_device(density, pattern, filter_square, filter_cube):
    sizes = (lax.axis_size("row"), lax.axis_size("col"))
    row_count, col_count = sizes
    rows_one, order = density.shape
    rows = order // row_count
    width = order // col_count

    def shape(height, cols, dtype):
        return jax.ShapeDtypeStruct((height, cols), dtype)

    local, up, down, pieces = masked_pieces(density, pattern)

    near = sorted({1, col_count - 1})
    far = list(range(2, col_count - 1))
    came = {shift: shifted(pieces[shift], "col", shift) for shift in near}
    up, down, *ready = lax.optimization_barrier(
        (up, down, *[pieces[shift] for shift in far], *[came[shift] for shift in near])
    )
    came.update({shift: shifted(piece, "col", shift) for shift, piece in zip(far, ready)})
    came.update(zip(near, ready[len(far) :]))
    early = jnp.concatenate([pieces[0]] + [came[shift] for shift in near], axis=0)
    keep_square, keep_cube = keep_masks(filter_square, filter_cube, rows, width)
    ready = (came[far[0]], keep_square) if far else (keep_square,)
    early = hops(early, [0] + near, lambda piece: lax.optimization_barrier((piece, *ready))[0])
    late = jnp.concatenate([came[shift] for shift in far], axis=0)
    late = hops(lax.optimization_barrier((late, early[1][0], early[2][0]))[0], far)
    cut = len(early) * 3 // 4
    begin = lax.optimization_barrier((*[piece for piece, _ in early[:cut]], late[1][0], late[2][0]))
    begin = [(piece, held) for piece, (_, held) in zip(begin, early[:cut])]
    columns = early + late + [swap_cores(begin, 10**9)]

    steps = col_count // 2
    up_shifts, down_shifts = list(range(1, steps + 1)), list(range(col_count - 1, steps, -1))
    ups, downs = [], []
    for step in range(1, steps + 1):
        up = shifted(up, "col", 1)
        ups += [up, came[step]]
        if step == steps:
            break
        down = shifted(down, "col", -1)
        rest = early[cut:] + late if step == 1 else []
        up, down, *ready = lax.optimization_barrier((up, down, *[piece for piece, _ in rest]))
        if step == 1:
            rest = [(piece, held) for piece, (_, held) in zip(ready, rest)]
            columns = columns + [swap_cores(rest, 10**9)]
        downs += [down, came[col_count - step]]
        up = jnp.concatenate([up[:, width:], came[step]], axis=1)
        down = jnp.concatenate([came[col_count - step], down[:, :-width]], axis=1)
    first_shifts, last_shifts = [0] + up_shifts[:-1], down_shifts + up_shifts[-1:]
    first_pairs, last_pairs = ups[:-2], downs + ups[-2:]

    part = rows // 2
    square_first, half_first, left_first, right = kernel_call(
        functools.partial(
            square_first_kernel, sizes, first_shifts, [held for _, held in columns]
        ),
        "square_first",
        [
            shape(part, width, jnp.float32),
            shape(part, width, jnp.bfloat16),
            shape(part, order, jnp.bfloat16),
            shape(order, width, jnp.bfloat16),
        ],
        [keep_square, local, *first_pairs, *[piece for piece, _ in columns]],
        (part, order, width),
    )
    first = hops(half_first, first_shifts, lambda piece: lax.optimization_barrier((piece, up))[0])
    right = lax.optimization_barrier((right, first[1][0], first[2][0]))[0]
    square_last, half_last, left = kernel_call(
        functools.partial(square_last_kernel, sizes, last_shifts),
        "square_last",
        [
            shape(part, width, jnp.float32),
            shape(part, width, jnp.bfloat16),
            shape(rows, order, jnp.bfloat16),
        ],
        [keep_square, right, left_first, *last_pairs],
        (part, order, width),
    )
    last = hops(half_last, last_shifts)
    halves = first + last
    halves += [swap_cores(items, 10**10) for items in (first, last[:cut], last[cut:])]
    return kernel_call(
        functools.partial(
            cube_kernel, sizes, [first_shifts, last_shifts], [held for _, held in halves]
        ),
        "cube",
        shape(rows, width, jnp.float32),
        [keep_cube, left, square_first, square_last, *[piece for piece, _ in halves]],
        (rows, order, width),
        [pltpu.VMEM((order, width), jnp.bfloat16)],
    )


def solution(mesh):
    placed = (P(("row", "col"), None), P(), P(), P())
    return jax.shard_map(
        on_device, mesh=mesh, in_specs=placed, out_specs=P("row", "col"), check_vma=False
    )
```

```python
import functools

import jax
import jax.numpy as jnp
from jax import lax
from jax.experimental import pallas as pl
from jax.experimental.pallas import tpu as pltpu
from jax.sharding import PartitionSpec as P

BLK = 128
VMEM = pl.BlockSpec(memory_space=pltpu.VMEM)
SMALL = pltpu.CompilerParams(vmem_limit_bytes=4 << 20)


def shifted(block, axis, distance):
    size = lax.axis_size(axis)
    return lax.ppermute(block, axis, [(i, (i + distance) % size) for i in range(size)])


def xor_moved(block, axis, bit_of):
    size = lax.axis_size(axis)
    return lax.ppermute(block, axis, [(i, i ^ bit_of(i)) for i in range(size)])


def hops(block, shifts, hold=lambda piece: piece):
    count = lax.axis_size("row")
    bits = [1 << b for b in range(1, count.bit_length() - 1)]
    items = [(block, 0, 0)]
    for low, high in zip(bits, bits[::-1]):

        def bit_of(i, low=low, high=high):
            return high if i & 1 else low

        items = items + [
            (xor_moved(piece if even == 0 else hold(piece), "row", bit_of), even ^ low, odd ^ high)
            for piece, even, odd in items
        ]
    return [(piece, [(even, odd, shifts)]) for piece, even, odd in items]


def hint(flops):
    return pl.CostEstimate(flops=flops, bytes_accessed=0, transcendentals=0)


def join_kernel(*refs):
    *piece_refs, out_ref = refs
    row = 0
    for ref in piece_refs:
        out_ref[row : row + ref.shape[0], :] = ref[...]
        row += ref.shape[0]


def swap_cores(items, flops):
    pieces = [piece for piece, _ in items]
    joined = pieces[0]
    if len(pieces) > 1:
        rows = sum(piece.shape[0] for piece in pieces)
        joined = pl.pallas_call(
            join_kernel,
            out_shape=jax.ShapeDtypeStruct((rows, pieces[0].shape[1]), jnp.bfloat16),
            in_specs=[VMEM] * len(pieces),
            out_specs=VMEM,
            compiler_params=SMALL,
            cost_estimate=hint(flops),
            name="join",
        )(*pieces)
    held = [(odd ^ 1, even ^ 1, shifts) for _, parts in items for even, odd, shifts in parts]
    return xor_moved(joined, "row", lambda i: 1), held


def iota(shape, axis):
    return lax.broadcasted_iota(jnp.int32, shape, axis)


def expand(mask, row_start, rows, col_start, cols):
    nblocks = mask.shape[0]
    pick_row = (row_start + iota((rows, nblocks), 0)) // BLK == iota((rows, nblocks), 1)
    pick_col = (col_start + iota((nblocks, cols), 1)) // BLK == iota((nblocks, cols), 0)
    lines = jnp.dot(
        pick_row.astype(jnp.bfloat16),
        mask.astype(jnp.float32).astype(jnp.bfloat16),
        preferred_element_type=jnp.float32,
    )
    return jnp.dot(
        lines.astype(jnp.bfloat16),
        pick_col.astype(jnp.bfloat16),
        preferred_element_type=jnp.float32,
    )


def mask_kernel(col_count, pattern_ref, density_ref, local_ref, up_ref, down_ref, *piece_refs):
    rows_one, order = density_ref.shape
    width = order // col_count
    col_id = lax.axis_index("col")
    first = (lax.axis_index("row") * col_count + col_id) * rows_one
    full = expand(pattern_ref[...], first, rows_one, 0, order).astype(jnp.bfloat16)
    local_ref[...] = density_ref[...] * full
    for shift, piece_ref in enumerate(piece_refs):
        piece = local_ref[:, pl.ds(block_at(shift, col_count, width), width)]
        piece_ref[...] = piece
        if shift != 1:
            slot = (shift - 2) % col_count
            up_ref[:, slot * width : (slot + 1) * width] = piece
        if shift != col_count - 1:
            down_ref[:, shift * width : (shift + 1) * width] = piece


def masked_pieces(density, pattern):
    col_count = lax.axis_size("col")
    rows_one, order = density.shape
    width = order // col_count
    shapes = [order, order - width, order - width] + [width] * col_count
    local, up, down, *pieces = pl.pallas_call(
        functools.partial(mask_kernel, col_count),
        out_shape=[jax.ShapeDtypeStruct((rows_one, cols), jnp.bfloat16) for cols in shapes],
        in_specs=[VMEM] * 2,
        out_specs=[VMEM] * len(shapes),
        compiler_params=SMALL,
        name="mask",
    )(pattern, density)
    return local, up, down, pieces


def block_at(shift, col_count, width):
    return pl.multiple_of(lax.rem(lax.axis_index("col") + shift, col_count) * width, BLK)


def sub_at(shift, col_count, rows_one):
    return pl.multiple_of(
        lax.rem(lax.axis_index("col") + (col_count - shift), col_count) * rows_one, 16
    )


def fill_right(right, refs, layouts, sizes):
    row_count, col_count = sizes
    rows = right.shape[0] // row_count
    rows_one = rows // col_count
    row_id = lax.axis_index("row")
    odd_core = lax.rem(row_id, 2) == 1
    for ref, held in zip(refs, layouts):
        row = 0
        for even, odd, shifts in held:
            place = pl.multiple_of((row_id ^ jnp.where(odd_core, odd, even)) * rows, BLK)
            for shift in shifts:
                at = pl.multiple_of(place + sub_at(shift, col_count, rows_one), 16)
                right[pl.ds(at, rows_one), :] = ref[row : row + rows_one, :]
                row += rows_one


def split_refs(refs, counts):
    groups = []
    for count in counts:
        groups.append(refs[:count])
        refs = refs[count:]
    return groups + [refs]


def fill_left(left, first, whole_refs, pair_refs, col_count, rows_one):
    at = first
    for ref in whole_refs:
        left[at : at + ref.shape[0], :] = ref[...]
        at += ref.shape[0]
    for most_ref, own_ref in zip(pair_refs[::2], pair_refs[1::2]):
        width = own_ref.shape[1]
        left[at : at + rows_one, pl.ds(block_at(0, col_count, width), width)] = own_ref[...]
        for slot in range(col_count - 1):
            left[at : at + rows_one, pl.ds(block_at(slot + 1, col_count, width), width)] = most_ref[
                :, slot * width : (slot + 1) * width
            ]
        at += rows_one


def keep_kernel(square_filter_ref, cube_filter_ref, square_ref, cube_ref):
    rows, width = square_ref.shape
    row_at, col_at = lax.axis_index("row") * rows, lax.axis_index("col") * width
    for filter_ref, keep_ref in ((square_filter_ref, square_ref), (cube_filter_ref, cube_ref)):
        keep_ref[...] = expand(filter_ref[...], row_at, rows, col_at, width).astype(jnp.bfloat16)


def keep_masks(filter_square, filter_cube, rows, width):
    return pl.pallas_call(
        keep_kernel,
        out_shape=[jax.ShapeDtypeStruct((rows, width), jnp.bfloat16)] * 2,
        in_specs=[VMEM] * 2,
        out_specs=[VMEM] * 2,
        compiler_params=SMALL,
        cost_estimate=hint(2 * 10**10),
        name="keep",
    )(filter_square, filter_cube)


def square_part(left, right, shifts, col_count, keep_ref, square_ref, half_ref):
    rows_one = square_ref.shape[0] // len(shifts)
    total = jnp.dot(left, right, preferred_element_type=jnp.float32)
    for slot, shift in enumerate(shifts):
        at = slice(slot * rows_one, (slot + 1) * rows_one)
        keep = keep_ref[pl.ds(sub_at(shift, col_count, rows_one), rows_one), :]
        part = total[at] * keep.astype(jnp.float32)
        square_ref[at, :] = part
        half_ref[at, :] = part.astype(jnp.bfloat16)


def square_first_kernel(sizes, shifts, layouts, keep_ref, local_ref, *refs):
    col_count = sizes[1]
    pair_refs, piece_refs, rest = split_refs(refs, [2 * len(shifts) - 2, len(layouts)])
    square_ref, half_ref, left_ref, right_ref = rest
    fill_left(left_ref, 0, [local_ref], pair_refs, col_count, local_ref.shape[0])
    fill_right(right_ref, piece_refs, layouts, sizes)
    square_part(
        left_ref[...], right_ref[...], shifts, col_count, keep_ref, square_ref, half_ref
    )


def square_last_kernel(sizes, shifts, keep_ref, right_ref, before_ref, *refs):
    col_count = sizes[1]
    pair_refs, (square_ref, half_ref, left_ref) = refs[: 2 * len(shifts)], refs[2 * len(shifts) :]
    before = before_ref.shape[0]
    fill_left(left_ref, 0, [before_ref], pair_refs, col_count, pair_refs[0].shape[0])
    square_part(
        left_ref[before:, :], right_ref[...], shifts, col_count, keep_ref, square_ref, half_ref
    )


def cube_kernel(sizes, chunk_shifts, layouts, keep_ref, left_ref, *refs):
    col_count = sizes[1]
    square_refs, piece_refs, rest = split_refs(refs, [len(chunk_shifts), len(layouts)])
    out_ref, right = rest
    rows, width = out_ref.shape
    rows_one = rows // col_count
    fill_right(right, piece_refs, layouts, sizes)
    total = jnp.dot(left_ref[...], right[...], preferred_element_type=jnp.float32)
    row = 0
    for square_ref, shifts in zip(square_refs, chunk_shifts):
        for slot, shift in enumerate(shifts):
            at = pl.ds(sub_at(shift, col_count, rows_one), rows_one)
            square = square_ref[slot * rows_one : (slot + 1) * rows_one, :]
            keep = keep_ref[at, :].astype(jnp.float32)
            out_ref[at, :] = 3.0 * square - 2.0 * (total[row : row + rows_one] * keep)
            row += rows_one


def kernel_call(kernel, name, out_shape, inputs, product, scratch=()):
    rows, order, width = product
    return pl.pallas_call(
        kernel,
        out_shape=out_shape,
        in_specs=[VMEM] * len(inputs),
        out_specs=jax.tree.map(lambda shape: VMEM, out_shape),
        scratch_shapes=scratch,
        compiler_params=pltpu.CompilerParams(vmem_limit_bytes=16 << 20),
        cost_estimate=pl.CostEstimate(
            flops=2 * rows * order * width,
            bytes_accessed=2 * order * (rows + width) + 6 * rows * width,
            transcendentals=0,
        ),
        name=name,
    )(*inputs)


def on_device(density, pattern, filter_square, filter_cube):
    sizes = (lax.axis_size("row"), lax.axis_size("col"))
    row_count, col_count = sizes
    rows_one, order = density.shape
    rows = order // row_count
    width = order // col_count

    def shape(height, cols, dtype):
        return jax.ShapeDtypeStruct((height, cols), dtype)

    local, up, down, pieces = masked_pieces(density, pattern)

    near = sorted({1, col_count - 1})
    far = list(range(2, col_count - 1))
    came = {shift: shifted(pieces[shift], "col", shift) for shift in near}
    up, down, *ready = lax.optimization_barrier(
        (up, down, *[pieces[shift] for shift in far], *[came[shift] for shift in near])
    )
    came.update({shift: shifted(piece, "col", shift) for shift, piece in zip(far, ready)})
    came.update(zip(near, ready[len(far) :]))
    early = jnp.concatenate([pieces[0]] + [came[shift] for shift in near], axis=0)
    keep_square, keep_cube = keep_masks(filter_square, filter_cube, rows, width)
    ready = (came[far[0]], keep_square) if far else (keep_square,)
    early = hops(early, [0] + near, lambda piece: lax.optimization_barrier((piece, *ready))[0])
    late = jnp.concatenate([came[shift] for shift in far], axis=0)
    late = hops(lax.optimization_barrier((late, early[1][0], early[2][0]))[0], far)
    cut = len(early) * 3 // 4
    begin = lax.optimization_barrier((*[piece for piece, _ in early[:cut]], late[1][0], late[2][0]))
    begin = [(piece, held) for piece, (_, held) in zip(begin, early[:cut])]
    columns = early + late + [swap_cores(begin, 10**9)]

    steps = col_count // 2
    up_shifts, down_shifts = list(range(1, steps + 1)), list(range(col_count - 1, steps, -1))
    ups, downs = [], []
    for step in range(1, steps + 1):
        up = shifted(up, "col", 1)
        ups += [up, came[step]]
        if step == steps:
            break
        down = shifted(down, "col", -1)
        rest = early[cut:] + late if step == 1 else []
        up, down, *ready = lax.optimization_barrier((up, down, *[piece for piece, _ in rest]))
        if step == 1:
            rest = [(piece, held) for piece, (_, held) in zip(ready, rest)]
            columns = columns + [swap_cores(rest, 10**9)]
        downs += [down, came[col_count - step]]
        up = jnp.concatenate([up[:, width:], came[step]], axis=1)
        down = jnp.concatenate([came[col_count - step], down[:, :-width]], axis=1)
    first_shifts, last_shifts = [0] + up_shifts[:-1], down_shifts + up_shifts[-1:]
    first_pairs, last_pairs = ups[:-2], downs + ups[-2:]

    part = rows // 2
    square_first, half_first, left_first, right = kernel_call(
        functools.partial(
            square_first_kernel, sizes, first_shifts, [held for _, held in columns]
        ),
        "square_first",
        [
            shape(part, width, jnp.float32),
            shape(part, width, jnp.bfloat16),
            shape(part, order, jnp.bfloat16),
            shape(order, width, jnp.bfloat16),
        ],
        [keep_square, local, *first_pairs, *[piece for piece, _ in columns]],
        (part, order, width),
    )
    first = hops(half_first, first_shifts, lambda piece: lax.optimization_barrier((piece, up))[0])
    right = lax.optimization_barrier((right, first[1][0], first[2][0]))[0]
    square_last, half_last, left = kernel_call(
        functools.partial(square_last_kernel, sizes, last_shifts),
        "square_last",
        [
            shape(part, width, jnp.float32),
            shape(part, width, jnp.bfloat16),
            shape(rows, order, jnp.bfloat16),
        ],
        [keep_square, right, left_first, *last_pairs],
        (part, order, width),
    )
    last = hops(half_last, last_shifts)
    halves = first + last
    halves += [swap_cores(items, 10**10) for items in (first, last[:cut], last[cut:])]
    return kernel_call(
        functools.partial(
            cube_kernel, sizes, [first_shifts, last_shifts], [held for _, held in halves]
        ),
        "cube",
        shape(rows, width, jnp.float32),
        [keep_cube, left, square_first, square_last, *[piece for piece, _ in halves]],
        (rows, order, width),
        [pltpu.VMEM((order, width), jnp.bfloat16)],
    )


def solution(mesh):
    placed = (P(("row", "col"), None), P(), P(), P())
    return jax.shard_map(
        on_device, mesh=mesh, in_specs=placed, out_specs=P("row", "col"), check_vma=False
    )
```

```python
import functools

import jax
import jax.numpy as jnp
from jax import lax
from jax.experimental import pallas as pl
from jax.experimental.pallas import tpu as pltpu
from jax.sharding import PartitionSpec as P

BLK = 128
VMEM = pl.BlockSpec(memory_space=pltpu.VMEM)
SMALL = pltpu.CompilerParams(vmem_limit_bytes=4 << 20)


def shifted(block, axis, distance):
    size = lax.axis_size(axis)
    return lax.ppermute(block, axis, [(i, (i + distance) % size) for i in range(size)])


def xor_moved(block, axis, bit_of):
    size = lax.axis_size(axis)
    return lax.ppermute(block, axis, [(i, i ^ bit_of(i)) for i in range(size)])


def hops(block, shifts, hold_base=lambda piece: piece, hold=lambda piece: piece):
    count = lax.axis_size("row")
    bits = [1 << b for b in range(1, count.bit_length() - 1)]
    items = [(block, 0, 0)]
    for low, high in zip(bits, bits[::-1]):

        def bit_of(i, low=low, high=high):
            return high if i & 1 else low

        items = items + [
            (xor_moved(piece if even == 0 else hold(piece), "row", bit_of), even ^ low, odd ^ high)
            for piece, even, odd in items
        ]
        items[0] = (hold_base(block), 0, 0)
    return [(piece, [(even, odd, shifts)]) for piece, even, odd in items]


def hint(flops):
    return pl.CostEstimate(flops=flops, bytes_accessed=0, transcendentals=0)


def join_kernel(*refs):
    *piece_refs, out_ref = refs
    row = 0
    for ref in piece_refs:
        out_ref[row : row + ref.shape[0], :] = ref[...]
        row += ref.shape[0]


def swap_cores(items, flops):
    pieces = [piece for piece, _ in items]
    joined = pieces[0]
    if len(pieces) > 1:
        rows = sum(piece.shape[0] for piece in pieces)
        joined = pl.pallas_call(
            join_kernel,
            out_shape=jax.ShapeDtypeStruct((rows, pieces[0].shape[1]), jnp.bfloat16),
            in_specs=[VMEM] * len(pieces),
            out_specs=VMEM,
            compiler_params=SMALL,
            cost_estimate=hint(flops),
            name="join",
        )(*pieces)
    held = [(odd ^ 1, even ^ 1, shifts) for _, parts in items for even, odd, shifts in parts]
    return xor_moved(joined, "row", lambda i: 1), held


def iota(shape, axis):
    return lax.broadcasted_iota(jnp.int32, shape, axis)


def expand(mask, row_start, rows, col_start, cols):
    nblocks = mask.shape[0]
    pick_row = (row_start + iota((rows, nblocks), 0)) // BLK == iota((rows, nblocks), 1)
    pick_col = (col_start + iota((nblocks, cols), 1)) // BLK == iota((nblocks, cols), 0)
    lines = jnp.dot(
        pick_row.astype(jnp.bfloat16),
        mask.astype(jnp.float32).astype(jnp.bfloat16),
        preferred_element_type=jnp.float32,
    )
    return jnp.dot(
        lines.astype(jnp.bfloat16),
        pick_col.astype(jnp.bfloat16),
        preferred_element_type=jnp.float32,
    )


def mask_kernel(col_count, pattern_ref, density_ref, local_ref, up_ref, down_ref, *piece_refs):
    rows_one, order = density_ref.shape
    width = order // col_count
    col_id = lax.axis_index("col")
    first = (lax.axis_index("row") * col_count + col_id) * rows_one
    full = expand(pattern_ref[...], first, rows_one, 0, order).astype(jnp.bfloat16)
    local_ref[...] = density_ref[...] * full
    for shift, piece_ref in enumerate(piece_refs):
        piece = local_ref[:, pl.ds(block_at(shift, col_count, width), width)]
        piece_ref[...] = piece
        if shift != 1:
            slot = (shift - 2) % col_count
            up_ref[:, slot * width : (slot + 1) * width] = piece
        if shift != col_count - 1:
            down_ref[:, shift * width : (shift + 1) * width] = piece


def masked_pieces(density, pattern):
    col_count = lax.axis_size("col")
    rows_one, order = density.shape
    width = order // col_count
    shapes = [order, order - width, order - width] + [width] * col_count
    local, up, down, *pieces = pl.pallas_call(
        functools.partial(mask_kernel, col_count),
        out_shape=[jax.ShapeDtypeStruct((rows_one, cols), jnp.bfloat16) for cols in shapes],
        in_specs=[VMEM] * 2,
        out_specs=[VMEM] * len(shapes),
        compiler_params=SMALL,
        name="mask",
    )(pattern, density)
    return local, up, down, pieces


def block_at(shift, col_count, width):
    return pl.multiple_of(lax.rem(lax.axis_index("col") + shift, col_count) * width, BLK)


def sub_at(shift, col_count, rows_one):
    return pl.multiple_of(
        lax.rem(lax.axis_index("col") + (col_count - shift), col_count) * rows_one, 16
    )


def fill_right(right, refs, layouts, sizes):
    row_count, col_count = sizes
    rows = right.shape[0] // row_count
    rows_one = rows // col_count
    row_id = lax.axis_index("row")
    odd_core = lax.rem(row_id, 2) == 1
    for ref, held in zip(refs, layouts):
        row = 0
        for even, odd, shifts in held:
            place = pl.multiple_of((row_id ^ jnp.where(odd_core, odd, even)) * rows, BLK)
            for shift in shifts:
                at = pl.multiple_of(place + sub_at(shift, col_count, rows_one), 16)
                right[pl.ds(at, rows_one), :] = ref[row : row + rows_one, :]
                row += rows_one


def split_refs(refs, counts):
    groups = []
    for count in counts:
        groups.append(refs[:count])
        refs = refs[count:]
    return groups + [refs]


def fill_left(left, first, whole_refs, pair_refs, col_count, rows_one):
    at = first
    for ref in whole_refs:
        left[at : at + ref.shape[0], :] = ref[...]
        at += ref.shape[0]
    for most_ref, own_ref in zip(pair_refs[::2], pair_refs[1::2]):
        width = own_ref.shape[1]
        left[at : at + rows_one, pl.ds(block_at(0, col_count, width), width)] = own_ref[...]
        for slot in range(col_count - 1):
            left[at : at + rows_one, pl.ds(block_at(slot + 1, col_count, width), width)] = most_ref[
                :, slot * width : (slot + 1) * width
            ]
        at += rows_one


def keep_kernel(filter_ref, keep_ref):
    rows, width = keep_ref.shape
    row_at, col_at = lax.axis_index("row") * rows, lax.axis_index("col") * width
    keep_ref[...] = expand(filter_ref[...], row_at, rows, col_at, width).astype(jnp.bfloat16)


def keep_mask(mask, rows, width, flops):
    return pl.pallas_call(
        keep_kernel,
        out_shape=jax.ShapeDtypeStruct((rows, width), jnp.bfloat16),
        in_specs=[VMEM],
        out_specs=VMEM,
        compiler_params=SMALL,
        cost_estimate=hint(flops),
        name="keep",
    )(mask)


def square_part(left, right, shifts, col_count, keep_ref, square_ref, half_ref):
    rows_one = square_ref.shape[0] // len(shifts)
    total = jnp.dot(left, right, preferred_element_type=jnp.float32)
    for slot, shift in enumerate(shifts):
        at = slice(slot * rows_one, (slot + 1) * rows_one)
        keep = keep_ref[pl.ds(sub_at(shift, col_count, rows_one), rows_one), :]
        part = total[at] * keep.astype(jnp.float32)
        square_ref[at, :] = part
        half_ref[at, :] = part.astype(jnp.bfloat16)


def square_first_kernel(sizes, shifts, layouts, keep_ref, local_ref, *refs):
    col_count = sizes[1]
    pair_refs, piece_refs, rest = split_refs(refs, [2 * len(shifts) - 2, len(layouts)])
    square_ref, half_ref, left_ref, right_ref = rest
    fill_left(left_ref, 0, [local_ref], pair_refs, col_count, local_ref.shape[0])
    fill_right(right_ref, piece_refs, layouts, sizes)
    square_part(
        left_ref[...], right_ref[...], shifts, col_count, keep_ref, square_ref, half_ref
    )


def square_last_kernel(sizes, shifts, keep_ref, right_ref, before_ref, *refs):
    col_count = sizes[1]
    pair_refs, (square_ref, half_ref, left_ref) = refs[: 2 * len(shifts)], refs[2 * len(shifts) :]
    before = before_ref.shape[0]
    fill_left(left_ref, 0, [before_ref], pair_refs, col_count, pair_refs[0].shape[0])
    square_part(
        left_ref[before:, :], right_ref[...], shifts, col_count, keep_ref, square_ref, half_ref
    )


def cube_kernel(sizes, chunk_shifts, layouts, keep_ref, left_ref, *refs):
    col_count = sizes[1]
    square_refs, piece_refs, rest = split_refs(refs, [len(chunk_shifts), len(layouts)])
    out_ref, right = rest
    rows, width = out_ref.shape
    rows_one = rows // col_count
    fill_right(right, piece_refs, layouts, sizes)
    total = jnp.dot(left_ref[...], right[...], preferred_element_type=jnp.float32)
    row = 0
    for square_ref, shifts in zip(square_refs, chunk_shifts):
        for slot, shift in enumerate(shifts):
            at = pl.ds(sub_at(shift, col_count, rows_one), rows_one)
            square = square_ref[slot * rows_one : (slot + 1) * rows_one, :]
            keep = keep_ref[at, :].astype(jnp.float32)
            out_ref[at, :] = 3.0 * square - 2.0 * (total[row : row + rows_one] * keep)
            row += rows_one


def kernel_call(kernel, name, out_shape, inputs, product, scratch=()):
    rows, order, width = product
    return pl.pallas_call(
        kernel,
        out_shape=out_shape,
        in_specs=[VMEM] * len(inputs),
        out_specs=jax.tree.map(lambda shape: VMEM, out_shape),
        scratch_shapes=scratch,
        compiler_params=pltpu.CompilerParams(vmem_limit_bytes=16 << 20),
        cost_estimate=pl.CostEstimate(
            flops=2 * rows * order * width,
            bytes_accessed=2 * order * (rows + width) + 6 * rows * width,
            transcendentals=0,
        ),
        name=name,
    )(*inputs)


def on_device(density, pattern, filter_square, filter_cube):
    sizes = (lax.axis_size("row"), lax.axis_size("col"))
    row_count, col_count = sizes
    rows_one, order = density.shape
    rows = order // row_count
    width = order // col_count

    def shape(height, cols, dtype):
        return jax.ShapeDtypeStruct((height, cols), dtype)

    local, up, down, pieces = masked_pieces(density, pattern)

    near = sorted({1, col_count - 1})
    far = list(range(2, col_count - 1))
    came = {shift: shifted(pieces[shift], "col", shift) for shift in near + far}
    up, down, *ready = lax.optimization_barrier((up, down, *[came[shift] for shift in near + far]))
    keep_square = keep_mask(filter_square, rows, width, 10**9)
    keep_cube = keep_mask(filter_cube, rows, width, 2 * 10**10)
    early = jnp.concatenate([pieces[0]] + [came[shift] for shift in near], axis=0)
    early = hops(
        lax.optimization_barrier((early, keep_square))[0],
        [0] + near,
        lambda piece: lax.optimization_barrier((piece, *ready))[0],
        lambda piece: lax.optimization_barrier((piece, keep_cube))[0],
    )
    came = dict(zip(near + far, ready))
    late = jnp.concatenate([came[shift] for shift in far], axis=0)
    late = hops(lax.optimization_barrier((late, early[1][0], early[2][0]))[0], far)
    cut = len(early) * 3 // 4
    begin = lax.optimization_barrier((*[piece for piece, _ in early[:cut]], late[1][0], late[2][0]))
    begin = [(piece, held) for piece, (_, held) in zip(begin, early[:cut])]
    columns = early + late + [swap_cores(begin, 10**9)]

    steps = col_count // 2
    up_shifts, down_shifts = list(range(1, steps + 1)), list(range(col_count - 1, steps, -1))
    ups, downs = [], []
    for step in range(1, steps + 1):
        up = shifted(up, "col", 1)
        ups += [up, came[step]]
        if step == steps:
            break
        down = shifted(down, "col", -1)
        rest = early[cut:] + late if step == 1 else []
        up, down, *ready = lax.optimization_barrier((up, down, *[piece for piece, _ in rest]))
        if step == 1:
            rest = [(piece, held) for piece, (_, held) in zip(ready, rest)]
            columns = columns + [swap_cores(rest, 10**9)]
        downs += [down, came[col_count - step]]
        up = jnp.concatenate([up[:, width:], came[step]], axis=1)
        down = jnp.concatenate([came[col_count - step], down[:, :-width]], axis=1)
    first_shifts, last_shifts = [0] + up_shifts[:-1], down_shifts + up_shifts[-1:]
    first_pairs, last_pairs = ups[:-2], downs + ups[-2:]

    part = rows // 2
    square_first, half_first, left_first, right = kernel_call(
        functools.partial(
            square_first_kernel, sizes, first_shifts, [held for _, held in columns]
        ),
        "square_first",
        [
            shape(part, width, jnp.float32),
            shape(part, width, jnp.bfloat16),
            shape(part, order, jnp.bfloat16),
            shape(order, width, jnp.bfloat16),
        ],
        [keep_square, local, *first_pairs, *[piece for piece, _ in columns]],
        (part, order, width),
    )
    first = hops(
        half_first, first_shifts, hold=lambda piece: lax.optimization_barrier((piece, up))[0]
    )
    right = lax.optimization_barrier((right, first[1][0], first[2][0]))[0]
    square_last, half_last, left = kernel_call(
        functools.partial(square_last_kernel, sizes, last_shifts),
        "square_last",
        [
            shape(part, width, jnp.float32),
            shape(part, width, jnp.bfloat16),
            shape(rows, order, jnp.bfloat16),
        ],
        [keep_square, right, left_first, *last_pairs],
        (part, order, width),
    )
    last = hops(half_last, last_shifts)
    halves = first + last
    halves += [swap_cores(items, 10**10) for items in (first, last[:cut], last[cut:])]
    return kernel_call(
        functools.partial(
            cube_kernel, sizes, [first_shifts, last_shifts], [held for _, held in halves]
        ),
        "cube",
        shape(rows, width, jnp.float32),
        [keep_cube, left, square_first, square_last, *[piece for piece, _ in halves]],
        (rows, order, width),
        [pltpu.VMEM((order, width), jnp.bfloat16)],
    )


def solution(mesh):
    placed = (P(("row", "col"), None), P(), P(), P())
    return jax.shard_map(
        on_device, mesh=mesh, in_specs=placed, out_specs=P("row", "col"), check_vma=False
    )
```

```python
import functools

import jax
import jax.numpy as jnp
from jax import lax
from jax.experimental import pallas as pl
from jax.experimental.pallas import tpu as pltpu
from jax.sharding import PartitionSpec as P

BLK = 128
VMEM = pl.BlockSpec(memory_space=pltpu.VMEM)


def shifted(block, axis, distance):
    size = lax.axis_size(axis)
    return lax.ppermute(block, axis, [(i, (i + distance) % size) for i in range(size)])


def xor_moved(block, axis, bit_of):
    size = lax.axis_size(axis)
    return lax.ppermute(block, axis, [(i, i ^ bit_of(i)) for i in range(size)])


def hops(block, held, hold_base=lambda piece: piece, hold=lambda piece: piece):
    count = lax.axis_size("row")
    bits = [1 << b for b in range(1, count.bit_length() - 1)]
    items = [(block, 0, 0)]
    for low, high in zip(bits, bits[::-1]):

        def bit_of(i, low=low, high=high):
            return high if i & 1 else low

        items = items + [
            (xor_moved(piece if even == 0 else hold(piece), "row", bit_of), even ^ low, odd ^ high)
            for piece, even, odd in items
        ]
        items[0] = (hold_base(block), 0, 0)
    return [(piece, [(even, odd, held)]) for piece, even, odd in items]


def hint(flops):
    return pl.CostEstimate(flops=flops, bytes_accessed=0, transcendentals=0)


def call(kernel, name, out_shape, inputs, flops, scratch=(), limit=4):
    return pl.pallas_call(
        kernel,
        out_shape=out_shape,
        in_specs=[VMEM] * len(inputs),
        out_specs=jax.tree.map(lambda shape: VMEM, out_shape),
        scratch_shapes=scratch,
        compiler_params=pltpu.CompilerParams(vmem_limit_bytes=limit << 20),
        cost_estimate=hint(flops),
        name=name,
    )(*inputs)


def half(*shape):
    return jax.ShapeDtypeStruct(shape, jnp.bfloat16)


def full(*shape):
    return jax.ShapeDtypeStruct(shape, jnp.float32)


def join_kernel(*refs):
    *piece_refs, out_ref = refs
    row = 0
    for ref in piece_refs:
        out_ref[row : row + ref.shape[0], :] = ref[...]
        row += ref.shape[0]


def swap_cores(items, flops):
    pieces = [piece for piece, _ in items]
    joined = pieces[0]
    if len(pieces) > 1:
        rows = sum(piece.shape[0] for piece in pieces)
        joined = call(join_kernel, "join", half(rows, pieces[0].shape[1]), pieces, flops)
    held = [(odd ^ 1, even ^ 1, shifts) for _, parts in items for even, odd, shifts in parts]
    return xor_moved(joined, "row", lambda i: 1), held


def tied(items, *others):
    ready = lax.optimization_barrier((*[piece for piece, _ in items], *others))
    return [(piece, held) for piece, (_, held) in zip(ready, items)]


def iota(shape, axis):
    return lax.broadcasted_iota(jnp.int32, shape, axis)


def expand(mask, row_start, rows, col_start, cols):
    nblocks = mask.shape[0]
    pick_row = (row_start + iota((rows, nblocks), 0)) // BLK == iota((rows, nblocks), 1)
    pick_col = (col_start + iota((nblocks, cols), 1)) // BLK == iota((nblocks, cols), 0)
    lines = jnp.dot(
        pick_row.astype(jnp.bfloat16),
        mask.astype(jnp.float32).astype(jnp.bfloat16),
        preferred_element_type=jnp.float32,
    )
    return jnp.dot(
        lines.astype(jnp.bfloat16),
        pick_col.astype(jnp.bfloat16),
        preferred_element_type=jnp.float32,
    ).astype(jnp.bfloat16)


def block_at(shift, col_count, width):
    return pl.multiple_of(lax.rem(lax.axis_index("col") + shift, col_count) * width, BLK)


def sub_at(shift, col_count, rows_one):
    return pl.multiple_of(
        lax.rem(lax.axis_index("col") + (col_count - shift), col_count) * rows_one, 16
    )


def masked_rows(pattern_ref, rows_ref, shift, col_count):
    rows_one, order = rows_ref.shape
    first = lax.axis_index("row") * (col_count * rows_one) + sub_at(shift, col_count, rows_one)
    return rows_ref[...] * expand(pattern_ref[...], first, rows_one, 0, order)


def cut_kernel(col_count, shifts, pattern_ref, density_ref, local_ref, *piece_refs):
    width = density_ref.shape[1] // col_count
    local_ref[...] = masked_rows(pattern_ref, density_ref, 0, col_count)
    for shift, piece_ref in zip(shifts, piece_refs):
        piece_ref[...] = local_ref[:, pl.ds(block_at(shift, col_count, width), width)]


def near_kernel(col_count, pattern_ref, raw_up_ref, raw_down_ref, up_ref, down_ref, near_ref, *go_refs):
    rows_one, order = up_ref.shape
    width = order // col_count
    up_ref[...] = masked_rows(pattern_ref, raw_up_ref, 1, col_count)
    down_ref[...] = masked_rows(pattern_ref, raw_down_ref, col_count - 1, col_count)
    own = pl.ds(block_at(0, col_count, width), width)
    near_ref[:rows_one, :] = up_ref[:, own]
    near_ref[rows_one:, :] = down_ref[:, own]
    for go_ref, ref, first in zip(go_refs, (up_ref, down_ref), (2, 0)):
        for slot in range(col_count - 1):
            at = block_at(first + slot, col_count, width)
            go_ref[:, slot * width : (slot + 1) * width] = ref[:, pl.ds(at, width)]


def keep_kernel(filter_ref, keep_ref):
    rows, width = keep_ref.shape
    row_at, col_at = lax.axis_index("row") * rows, lax.axis_index("col") * width
    keep_ref[...] = expand(filter_ref[...], row_at, rows, col_at, width)


def fill_left(left, whole_refs, whole_shifts, pair_refs, pair_shifts, col_count):
    rows_one = whole_refs[0].shape[0]
    for ref, shift in zip(whole_refs, whole_shifts):
        left[pl.ds(sub_at(shift, col_count, rows_one), rows_one), :] = ref[...]
    for most_ref, own_ref, shift in zip(pair_refs[::2], pair_refs[1::2], pair_shifts):
        width = own_ref.shape[1]
        rows = pl.ds(sub_at(shift, col_count, rows_one), rows_one)
        left[rows, pl.ds(block_at(0, col_count, width), width)] = own_ref[...]
        for slot in range(col_count - 1):
            columns = pl.ds(block_at(slot + 1, col_count, width), width)
            left[rows, columns] = most_ref[:, slot * width : (slot + 1) * width]


def fill_right(rights, refs, layouts, sizes):
    row_count, col_count = sizes
    rows = rights[0].shape[0] // row_count
    row_id = lax.axis_index("row")
    odd_core = lax.rem(row_id, 2) == 1
    for ref, held in zip(refs, layouts):
        row = 0
        for even, odd, shifts in held:
            place = pl.multiple_of((row_id ^ jnp.where(odd_core, odd, even)) * rows, BLK)
            height = rows if shifts is None else rows // col_count
            for shift in [0] if shifts is None else shifts:
                at = place
                if shifts is not None:
                    at = pl.multiple_of(place + sub_at(shift, col_count, height), 16)
                column = 0
                for right in rights:
                    stop = column + right.shape[1]
                    right[pl.ds(at, height), :] = ref[row : row + height, column:stop]
                    column = stop
                row += height


def split_refs(refs, counts):
    groups = []
    for count in counts:
        groups.append(refs[:count])
        refs = refs[count:]
    return groups + [refs]


def filtered(left, right, keep):
    return jnp.dot(left, right, preferred_element_type=jnp.float32) * keep.astype(jnp.float32)


def square_first_kernel(sizes, whole_shifts, pair_shifts, layouts, keep_ref, *refs):
    counts = [len(whole_shifts), 2 * len(pair_shifts), len(layouts)]
    whole_refs, pair_refs, piece_refs, rest = split_refs(refs, counts)
    square_ref, half_ref, left_ref, later_ref, right = rest
    fill_left(left_ref, whole_refs, whole_shifts, pair_refs, pair_shifts, sizes[1])
    fill_right([right, later_ref], piece_refs, layouts, sizes)
    total = filtered(left_ref[...], right[...], keep_ref[:, : right.shape[1]])
    square_ref[...] = total
    half_ref[...] = total.astype(jnp.bfloat16)


def square_later_kernel(keep_ref, left_ref, right_ref, square_ref, half_ref):
    total = filtered(left_ref[...], right_ref[...], keep_ref[:, -right_ref.shape[1] :])
    square_ref[...] = total
    half_ref[...] = total.astype(jnp.bfloat16)


def cube_first_kernel(sizes, layouts, keep_ref, left_ref, square_ref, *refs):
    *piece_refs, out_ref, right = refs
    fill_right([right], piece_refs, layouts, sizes)
    cube = filtered(left_ref[...], right[...], keep_ref[:, : right.shape[1]])
    out_ref[...] = 3.0 * square_ref[...] - 2.0 * cube


def cube_later_kernel(sizes, layouts, keep_ref, left_ref, square_ref, first_ref, *refs):
    *piece_refs, out_ref, right = refs
    cut = first_ref.shape[1]
    fill_right([right], piece_refs, layouts, sizes)
    out_ref[:, :cut] = first_ref[...]
    cube = filtered(left_ref[...], right[...], keep_ref[:, cut:])
    out_ref[:, cut:] = 3.0 * square_ref[...] - 2.0 * cube


def on_device(density, pattern, filter_square, filter_cube):
    sizes = (lax.axis_size("row"), lax.axis_size("col"))
    row_count, col_count = sizes
    rows_one, order = density.shape
    rows = order // row_count
    width = order // col_count
    steps = col_count // 2
    far = list(range(2, col_count - 1))

    raw_up = shifted(density, "col", 1)
    raw_down = shifted(density, "col", -1)
    local, *pieces = call(
        functools.partial(cut_kernel, col_count, [0] + far),
        "cut",
        [half(rows_one, order)] + [half(rows_one, width)] * (1 + len(far)),
        [pattern, density],
        10**10,
    )
    came = {shift: shifted(piece, "col", shift) for shift, piece in zip(far, pieces[1:])}
    keep_square, keep_cube = (
        call(keep_kernel, "keep", half(rows, width), [mask], 2 * 10**10)
        for mask in (filter_square, filter_cube)
    )
    start = jnp.concatenate([pieces[0]] + [came[shift] for shift in far], axis=0)
    start = hops(lax.optimization_barrier((start, keep_square))[0], [0] + far)
    raw_up, raw_down, *ready = lax.optimization_barrier(
        (raw_up, raw_down, *[piece for piece, _ in start])
    )
    start = [(piece, held) for piece, (_, held) in zip(ready, start)]
    most = order - width
    sent_on = 1 if col_count == 4 else 2
    up, down, near, *go = call(
        functools.partial(near_kernel, col_count),
        "near",
        [half(rows_one, order)] * 2 + [half(2 * rows_one, width)] + [half(rows_one, most)] * sent_on,
        [pattern, raw_up, raw_down],
        10**9,
    )
    near = hops(
        near,
        [1, col_count - 1],
        hold=lambda piece: lax.optimization_barrier((piece, keep_cube))[0],
    )
    cut = len(near) * 3 // 4
    swapped = [swap_cores(start, 10**9), swap_cores(near[:cut], 10**9)]

    pairs, pair_shifts = [], []
    for step in range(2, steps + 1):
        moved = shifted(go[0], "col", 1)
        pairs += [moved, came[step]]
        pair_shifts.append(step)
        ahead = jnp.concatenate([moved[:, width:], came[step]], axis=1)
        if step == steps:
            break
        moved = shifted(go[1], "col", -1)
        pairs += [moved, came[col_count - step]]
        pair_shifts.append(col_count - step)
        go = [ahead, jnp.concatenate([came[col_count - step], moved[:, :-width]], axis=1)]

    columns = start + near + swapped + [swap_cores(tied(near[cut:], pairs[-2]), 10**9)]

    first = width * 2 // 3 // BLK * BLK
    later = width - first
    flops = 2 * rows * order * width
    square_first, half_first, left, right_later = call(
        functools.partial(
            square_first_kernel,
            sizes,
            [0, 1, col_count - 1],
            pair_shifts,
            [held for _, held in columns],
        ),
        "square_first",
        [full(rows, first), half(rows, first), half(rows, order), half(order, later)],
        [keep_square, local, up, down, *pairs, *[piece for piece, _ in columns]],
        flops * 2 // 3,
        [pltpu.VMEM((order, first), jnp.bfloat16)],
        12,
    )
    square_later, half_later = call(
        square_later_kernel,
        "square_later",
        [full(rows, later), half(rows, later)],
        [keep_square, left, right_later],
        flops // 3,
        limit=8,
    )
    ahead = hops(
        half_first, None, hold=lambda piece: lax.optimization_barrier((piece, half_later))[0]
    )
    behind = hops(half_later, None)
    ahead = ahead + [swap_cores(tied(ahead, behind[1][0], behind[2][0]), 10**10)]
    behind = behind + [swap_cores(behind[:cut], 10**9), swap_cores(behind[cut:], 10**9)]
    out_first = call(
        functools.partial(cube_first_kernel, sizes, [held for _, held in ahead]),
        "cube_first",
        full(rows, first),
        [keep_cube, left, square_first, *[piece for piece, _ in ahead]],
        flops * 2 // 3,
        [pltpu.VMEM((order, first), jnp.bfloat16)],
        12,
    )
    return call(
        functools.partial(cube_later_kernel, sizes, [held for _, held in behind]),
        "cube_later",
        full(rows, width),
        [keep_cube, left, square_later, out_first, *[piece for piece, _ in behind]],
        flops // 3,
        [pltpu.VMEM((order, later), jnp.bfloat16)],
        12,
    )


def solution(mesh):
    placed = (P(("row", "col"), None), P(), P(), P())
    return jax.shard_map(
        on_device, mesh=mesh, in_specs=placed, out_specs=P("row", "col"), check_vma=False
    )
```

```python
import functools

import jax
import jax.numpy as jnp
from jax import lax
from jax.experimental import pallas as pl
from jax.experimental.pallas import tpu as pltpu
from jax.sharding import PartitionSpec as P

BLK = 128
VMEM = pl.BlockSpec(memory_space=pltpu.VMEM)


def shifted(block, axis, distance):
    size = lax.axis_size(axis)
    return lax.ppermute(block, axis, [(i, (i + distance) % size) for i in range(size)])


def xor_moved(block, axis, bit_of):
    size = lax.axis_size(axis)
    return lax.ppermute(block, axis, [(i, i ^ bit_of(i)) for i in range(size)])


def hops(block, held, hold_base=lambda piece: piece, hold=lambda piece: piece):
    count = lax.axis_size("row")
    bits = [1 << b for b in range(1, count.bit_length() - 1)]
    items = [(block, 0, 0)]
    for low, high in zip(bits, bits[::-1]):

        def bit_of(i, low=low, high=high):
            return high if i & 1 else low

        items = items + [
            (xor_moved(piece if even == 0 else hold(piece), "row", bit_of), even ^ low, odd ^ high)
            for piece, even, odd in items
        ]
        items[0] = (hold_base(block), 0, 0)
    return [(piece, [(even, odd, held)]) for piece, even, odd in items]


def hint(flops):
    return pl.CostEstimate(flops=flops, bytes_accessed=0, transcendentals=0)


def call(kernel, name, out_shape, inputs, flops, scratch=(), limit=4):
    return pl.pallas_call(
        kernel,
        out_shape=out_shape,
        in_specs=[VMEM] * len(inputs),
        out_specs=jax.tree.map(lambda shape: VMEM, out_shape),
        scratch_shapes=scratch,
        compiler_params=pltpu.CompilerParams(vmem_limit_bytes=limit << 20),
        cost_estimate=hint(flops),
        name=name,
    )(*inputs)


def half(*shape):
    return jax.ShapeDtypeStruct(shape, jnp.bfloat16)


def full(*shape):
    return jax.ShapeDtypeStruct(shape, jnp.float32)


def join_kernel(*refs):
    *piece_refs, out_ref = refs
    row = 0
    for ref in piece_refs:
        out_ref[row : row + ref.shape[0], :] = ref[...]
        row += ref.shape[0]


def swap_cores(items, flops):
    pieces = [piece for piece, _ in items]
    joined = pieces[0]
    if len(pieces) > 1:
        rows = sum(piece.shape[0] for piece in pieces)
        joined = call(join_kernel, "join", half(rows, pieces[0].shape[1]), pieces, flops)
    held = [(odd ^ 1, even ^ 1, shifts) for _, parts in items for even, odd, shifts in parts]
    return xor_moved(joined, "row", lambda i: 1), held


def tied(items, *others):
    ready = lax.optimization_barrier((*[piece for piece, _ in items], *others))
    return [(piece, held) for piece, (_, held) in zip(ready, items)]


def iota(shape, axis):
    return lax.broadcasted_iota(jnp.int32, shape, axis)


def expand(mask, row_start, rows, col_start, cols):
    nblocks = mask.shape[0]
    pick_row = (row_start + iota((rows, nblocks), 0)) // BLK == iota((rows, nblocks), 1)
    pick_col = (col_start + iota((nblocks, cols), 1)) // BLK == iota((nblocks, cols), 0)
    lines = jnp.dot(
        pick_row.astype(jnp.bfloat16),
        mask.astype(jnp.float32).astype(jnp.bfloat16),
        preferred_element_type=jnp.float32,
    )
    return jnp.dot(
        lines.astype(jnp.bfloat16),
        pick_col.astype(jnp.bfloat16),
        preferred_element_type=jnp.float32,
    ).astype(jnp.bfloat16)


def block_at(shift, col_count, width):
    return pl.multiple_of(lax.rem(lax.axis_index("col") + shift, col_count) * width, BLK)


def sub_at(shift, col_count, rows_one):
    return pl.multiple_of(
        lax.rem(lax.axis_index("col") + (col_count - shift), col_count) * rows_one, 16
    )


def cut_kernel(col_count, pattern_ref, density_ref, local_ref, up_ref, down_ref, *piece_refs):
    rows_one, order = density_ref.shape
    width = order // col_count
    first = lax.axis_index("row") * (col_count * rows_one) + sub_at(0, col_count, rows_one)
    local_ref[...] = density_ref[...] * expand(pattern_ref[...], first, rows_one, 0, order)
    for shift, piece_ref in enumerate(piece_refs):
        piece = local_ref[:, pl.ds(block_at(shift, col_count, width), width)]
        piece_ref[...] = piece
        if shift != 1:
            slot = (shift - 2) % col_count
            up_ref[:, slot * width : (slot + 1) * width] = piece
        if shift != col_count - 1:
            down_ref[:, shift * width : (shift + 1) * width] = piece


def keep_kernel(filter_ref, keep_ref):
    rows, width = keep_ref.shape
    row_at, col_at = lax.axis_index("row") * rows, lax.axis_index("col") * width
    keep_ref[...] = expand(filter_ref[...], row_at, rows, col_at, width)


def fill_left(left, first, whole_refs, pair_refs, col_count):
    at = first
    for ref in whole_refs:
        left[at : at + ref.shape[0], :] = ref[...]
        at += ref.shape[0]
    for most_ref, own_ref in zip(pair_refs[::2], pair_refs[1::2]):
        rows_one, width = own_ref.shape
        left[at : at + rows_one, pl.ds(block_at(0, col_count, width), width)] = own_ref[...]
        for slot in range(col_count - 1):
            columns = pl.ds(block_at(slot + 1, col_count, width), width)
            left[at : at + rows_one, columns] = most_ref[:, slot * width : (slot + 1) * width]
        at += rows_one


def fill_right(right, refs, layouts, sizes):
    row_count, col_count = sizes
    rows = right.shape[0] // row_count
    rows_one = rows // col_count
    row_id = lax.axis_index("row")
    odd_core = lax.rem(row_id, 2) == 1
    for ref, held in zip(refs, layouts):
        row = 0
        for even, odd, shifts in held:
            place = pl.multiple_of((row_id ^ jnp.where(odd_core, odd, even)) * rows, BLK)
            for shift in shifts:
                at = pl.multiple_of(place + sub_at(shift, col_count, rows_one), 16)
                right[pl.ds(at, rows_one), :] = ref[row : row + rows_one, :]
                row += rows_one


def split_refs(refs, counts):
    groups = []
    for count in counts:
        groups.append(refs[:count])
        refs = refs[count:]
    return groups + [refs]


def square_part(left, right, shifts, col_count, keep_ref, square_ref, half_ref):
    rows_one = square_ref.shape[0] // len(shifts)
    total = jnp.dot(left, right, preferred_element_type=jnp.float32)
    for slot, shift in enumerate(shifts):
        at = slice(slot * rows_one, (slot + 1) * rows_one)
        keep = keep_ref[pl.ds(sub_at(shift, col_count, rows_one), rows_one), :]
        part = total[at] * keep.astype(jnp.float32)
        square_ref[at, :] = part
        half_ref[at, :] = part.astype(jnp.bfloat16)


def square_first_kernel(sizes, shifts, layouts, keep_ref, local_ref, *refs):
    pair_refs, piece_refs, rest = split_refs(refs, [2 * len(shifts) - 2, len(layouts)])
    square_ref, half_ref, left_ref, right_ref = rest
    fill_left(left_ref, 0, [local_ref], pair_refs, sizes[1])
    fill_right(right_ref, piece_refs, layouts, sizes)
    square_part(left_ref[...], right_ref[...], shifts, sizes[1], keep_ref, square_ref, half_ref)


def square_last_kernel(sizes, shifts, keep_ref, right_ref, before_ref, *refs):
    pair_refs, (square_ref, half_ref, left_ref) = split_refs(refs, [2 * len(shifts)])
    before = before_ref.shape[0]
    fill_left(left_ref, 0, [before_ref], pair_refs, sizes[1])
    square_part(
        left_ref[before:, :], right_ref[...], shifts, sizes[1], keep_ref, square_ref, half_ref
    )


def cube_kernel(sizes, chunk_shifts, layouts, keep_ref, left_ref, *refs):
    square_refs, piece_refs, rest = split_refs(refs, [len(chunk_shifts), len(layouts)])
    out_ref, right = rest
    rows_one = out_ref.shape[0] // sizes[1]
    fill_right(right, piece_refs, layouts, sizes)
    total = jnp.dot(left_ref[...], right[...], preferred_element_type=jnp.float32)
    row = 0
    for square_ref, shifts in zip(square_refs, chunk_shifts):
        for slot, shift in enumerate(shifts):
            at = pl.ds(sub_at(shift, sizes[1], rows_one), rows_one)
            square = square_ref[slot * rows_one : (slot + 1) * rows_one, :]
            keep = keep_ref[at, :].astype(jnp.float32)
            out_ref[at, :] = 3.0 * square - 2.0 * (total[row : row + rows_one] * keep)
            row += rows_one


def after(value, *others):
    return lax.optimization_barrier((value, *others))[0]


def on_device(density, pattern, filter_square, filter_cube):
    sizes = (lax.axis_size("row"), lax.axis_size("col"))
    row_count, col_count = sizes
    rows_one, order = density.shape
    rows = order // row_count
    width = order // col_count
    steps = col_count // 2

    local, up, down, *pieces = call(
        functools.partial(cut_kernel, col_count),
        "cut",
        [half(rows_one, order)]
        + [half(rows_one, order - width)] * 2
        + [half(rows_one, width)] * col_count,
        [pattern, density],
        10**9,
    )
    keep_square, keep_cube = (
        call(keep_kernel, "keep", half(rows, width), [mask], 2 * 10**10)
        for mask in (filter_square, filter_cube)
    )
    others = list(range(1, col_count))
    came = {shift: shifted(pieces[shift], "col", shift) for shift in others}
    own = hops(after(pieces[0], keep_square), [0])
    up, down, *ready = lax.optimization_barrier((up, down, *came.values()))
    came = dict(zip(others, ready))
    rest = jnp.concatenate(ready, axis=0)
    rest = hops(after(rest, own[1][0], own[2][0]), others)

    ups, downs = [], []
    for step in range(1, steps + 1):
        up = shifted(up, "col", 1)
        ups += [up, came[step]]
        if step == 1:
            up = after(up, rest[1][0], rest[2][0])
        if step == steps:
            break
        down = shifted(down, "col", -1)
        downs += [down, came[col_count - step]]
        up = jnp.concatenate([up[:, width:], came[step]], axis=1)
        down = jnp.concatenate([came[col_count - step], down[:, :-width]], axis=1)
    first_shifts = list(range(steps))
    last_shifts = list(range(col_count - 1, steps - 1, -1))
    first_pairs, last_pairs = ups[:-2], downs + ups[-2:]

    cut = len(rest) * 3 // 4
    columns = own + rest
    columns = columns + [
        swap_cores(own, 10**9),
        swap_cores(rest[:cut], 10**9),
        swap_cores(tied(rest[cut:], first_pairs[0], last_pairs[0], keep_cube), 10**9),
    ]
    part = rows // 2
    flops = 2 * part * order * width
    square_first, half_first, left_first, right = call(
        functools.partial(square_first_kernel, sizes, first_shifts, [held for _, held in columns]),
        "square_first",
        [full(part, width), half(part, width), half(part, order), half(order, width)],
        [keep_square, local, *first_pairs, *[piece for piece, _ in columns]],
        flops,
        limit=12,
    )
    first = hops(half_first, first_shifts, hold=lambda piece: after(piece, last_pairs[-2]))
    square_last, half_last, left = call(
        functools.partial(square_last_kernel, sizes, last_shifts),
        "square_last",
        [full(part, width), half(part, width), half(rows, order)],
        [keep_square, after(right, first[1][0], first[2][0]), left_first, *last_pairs],
        flops,
        limit=12,
    )
    last = hops(half_last, last_shifts)
    halves = first + last
    halves = halves + [swap_cores(items, 10**10) for items in (first, last[:cut], last[cut:])]
    return call(
        functools.partial(
            cube_kernel, sizes, [first_shifts, last_shifts], [held for _, held in halves]
        ),
        "cube",
        full(rows, width),
        [keep_cube, left, square_first, square_last, *[piece for piece, _ in halves]],
        2 * flops,
        [pltpu.VMEM((order, width), jnp.bfloat16)],
        16,
    )


def solution(mesh):
    placed = (P(("row", "col"), None), P(), P(), P())
    return jax.shard_map(
        on_device, mesh=mesh, in_specs=placed, out_specs=P("row", "col"), check_vma=False
    )
```

```python
import functools

import jax
import jax.numpy as jnp
from jax import lax
from jax.experimental import pallas as pl
from jax.experimental.pallas import tpu as pltpu
from jax.sharding import PartitionSpec as P

BLK = 128
VMEM = pl.BlockSpec(memory_space=pltpu.VMEM)
HBM = pl.BlockSpec(memory_space=pltpu.HBM)


def shifted(block, axis, distance):
    size = lax.axis_size(axis)
    return lax.ppermute(block, axis, [(i, (i + distance) % size) for i in range(size)])


def xor_moved(block, axis, bit_of):
    size = lax.axis_size(axis)
    return lax.ppermute(block, axis, [(i, i ^ bit_of(i)) for i in range(size)])


def hops(block, held, hold_base=lambda piece: piece, hold=lambda piece: piece):
    count = lax.axis_size("row")
    bits = [1 << b for b in range(1, count.bit_length() - 1)]
    items = [(block, 0, 0)]
    for low, high in zip(bits, bits[::-1]):

        def bit_of(i, low=low, high=high):
            return high if i & 1 else low

        items = items + [
            (xor_moved(piece if even == 0 else hold(piece), "row", bit_of), even ^ low, odd ^ high)
            for piece, even, odd in items
        ]
        items[0] = (hold_base(block), 0, 0)
    return [(piece, [(even, odd, held)]) for piece, even, odd in items]


def hint(flops):
    return pl.CostEstimate(flops=flops, bytes_accessed=0, transcendentals=0)


def call(kernel, name, out_shape, inputs, flops, scratch=(), limit=4, source=VMEM, target=VMEM):
    return pl.pallas_call(
        kernel,
        out_shape=out_shape,
        in_specs=[source] * len(inputs),
        out_specs=jax.tree.map(lambda shape: target, out_shape),
        scratch_shapes=scratch,
        compiler_params=pltpu.CompilerParams(vmem_limit_bytes=limit << 20),
        cost_estimate=hint(flops),
        name=name,
    )(*inputs)


def half(*shape):
    return jax.ShapeDtypeStruct(shape, jnp.bfloat16)


def full(*shape):
    return jax.ShapeDtypeStruct(shape, jnp.float32)


def join_kernel(*refs):
    *piece_refs, out_ref = refs
    row = 0
    for ref in piece_refs:
        out_ref[row : row + ref.shape[0], :] = ref[...]
        row += ref.shape[0]


def swap_cores(items, flops):
    pieces = [piece for piece, _ in items]
    joined = pieces[0]
    if len(pieces) > 1:
        rows = sum(piece.shape[0] for piece in pieces)
        joined = call(join_kernel, "join", half(rows, pieces[0].shape[1]), pieces, flops)
    held = [(odd ^ 1, even ^ 1, shifts) for _, parts in items for even, odd, shifts in parts]
    return xor_moved(joined, "row", lambda i: 1), held


def tied(items, *others):
    ready = lax.optimization_barrier((*[piece for piece, _ in items], *others))
    return [(piece, held) for piece, (_, held) in zip(ready, items)]


def iota(shape, axis):
    return lax.broadcasted_iota(jnp.int32, shape, axis)


def expand(mask, row_start, rows, col_start, cols):
    nblocks = mask.shape[0]
    pick_row = (row_start + iota((rows, nblocks), 0)) // BLK == iota((rows, nblocks), 1)
    pick_col = (col_start + iota((nblocks, cols), 1)) // BLK == iota((nblocks, cols), 0)
    lines = jnp.dot(
        pick_row.astype(jnp.bfloat16),
        mask.astype(jnp.float32).astype(jnp.bfloat16),
        preferred_element_type=jnp.float32,
    )
    return jnp.dot(
        lines.astype(jnp.bfloat16),
        pick_col.astype(jnp.bfloat16),
        preferred_element_type=jnp.float32,
    ).astype(jnp.bfloat16)


def block_at(shift, col_count, width):
    return pl.multiple_of(lax.rem(lax.axis_index("col") + shift, col_count) * width, BLK)


def sub_at(shift, col_count, rows_one):
    return pl.multiple_of(
        lax.rem(lax.axis_index("col") + (col_count - shift), col_count) * rows_one, 16
    )


def cut_kernel(col_count, pattern_hbm, density_hbm, local_ref, up_ref, down_ref, *refs):
    *piece_refs, pattern_ref, density_ref, sems = refs
    fetches = [
        pltpu.make_async_copy(pattern_hbm, pattern_ref, sems.at[0]),
        pltpu.make_async_copy(density_hbm, density_ref, sems.at[1]),
    ]
    for fetch in fetches:
        fetch.start()
    rows_one, order = density_ref.shape
    width = order // col_count
    first = lax.axis_index("row") * (col_count * rows_one) + sub_at(0, col_count, rows_one)
    fetches[0].wait()
    keep = expand(pattern_ref[...], first, rows_one, 0, order)
    fetches[1].wait()
    local_ref[...] = density_ref[...] * keep
    for shift, piece_ref in enumerate(piece_refs):
        piece = local_ref[:, pl.ds(block_at(shift, col_count, width), width)]
        piece_ref[...] = piece
        if shift != 1:
            slot = (shift - 2) % col_count
            up_ref[:, slot * width : (slot + 1) * width] = piece
        if shift != col_count - 1:
            down_ref[:, shift * width : (shift + 1) * width] = piece


def keep_kernel(filter_ref, keep_ref):
    rows, width = keep_ref.shape
    row_at, col_at = lax.axis_index("row") * rows, lax.axis_index("col") * width
    keep_ref[...] = expand(filter_ref[...], row_at, rows, col_at, width)


def fill_left(left, first, whole_refs, pair_refs, col_count):
    at = first
    for ref in whole_refs:
        left[at : at + ref.shape[0], :] = ref[...]
        at += ref.shape[0]
    for most_ref, own_ref in zip(pair_refs[::2], pair_refs[1::2]):
        rows_one, width = own_ref.shape
        left[at : at + rows_one, pl.ds(block_at(0, col_count, width), width)] = own_ref[...]
        for slot in range(col_count - 1):
            columns = pl.ds(block_at(slot + 1, col_count, width), width)
            left[at : at + rows_one, columns] = most_ref[:, slot * width : (slot + 1) * width]
        at += rows_one


def fill_right(right, refs, layouts, sizes):
    row_count, col_count = sizes
    rows = right.shape[0] // row_count
    rows_one = rows // col_count
    row_id = lax.axis_index("row")
    odd_core = lax.rem(row_id, 2) == 1
    for ref, held in zip(refs, layouts):
        row = 0
        for even, odd, shifts in held:
            place = pl.multiple_of((row_id ^ jnp.where(odd_core, odd, even)) * rows, BLK)
            for shift in shifts:
                at = pl.multiple_of(place + sub_at(shift, col_count, rows_one), 16)
                right[pl.ds(at, rows_one), :] = ref[row : row + rows_one, :]
                row += rows_one


def split_refs(refs, counts):
    groups = []
    for count in counts:
        groups.append(refs[:count])
        refs = refs[count:]
    return groups + [refs]


def square_part(left, right, shifts, col_count, keep_ref, square_ref, half_ref):
    rows_one = square_ref.shape[0] // len(shifts)
    total = jnp.dot(left, right, preferred_element_type=jnp.float32)
    for slot, shift in enumerate(shifts):
        at = slice(slot * rows_one, (slot + 1) * rows_one)
        keep = keep_ref[pl.ds(sub_at(shift, col_count, rows_one), rows_one), :]
        part = total[at] * keep.astype(jnp.float32)
        square_ref[at, :] = part
        half_ref[at, :] = part.astype(jnp.bfloat16)


def square_first_kernel(sizes, shifts, layouts, keep_ref, local_ref, *refs):
    pair_refs, piece_refs, rest = split_refs(refs, [2 * len(shifts) - 2, len(layouts)])
    square_ref, half_ref, left_ref, right_ref = rest
    fill_left(left_ref, 0, [local_ref], pair_refs, sizes[1])
    fill_right(right_ref, piece_refs, layouts, sizes)
    square_part(left_ref[...], right_ref[...], shifts, sizes[1], keep_ref, square_ref, half_ref)


def square_last_kernel(sizes, shifts, keep_ref, right_ref, before_ref, *refs):
    pair_refs, (square_ref, half_ref, left_ref) = split_refs(refs, [2 * len(shifts)])
    before = before_ref.shape[0]
    fill_left(left_ref, 0, [before_ref], pair_refs, sizes[1])
    square_part(
        left_ref[before:, :], right_ref[...], shifts, sizes[1], keep_ref, square_ref, half_ref
    )


def cube_kernel(sizes, chunk_shifts, layouts, keep_ref, left_ref, *refs):
    square_refs, piece_refs, rest = split_refs(refs, [len(chunk_shifts), len(layouts)])
    out_hbm, right, out_ref, sems = rest
    rows, width = out_ref.shape
    rows_one = rows // sizes[1]
    fill_right(right, piece_refs, layouts, sizes)
    copies = []
    for number, start in enumerate(range(0, width, 2 * BLK)):
        cols = slice(start, start + 2 * BLK)
        total = jnp.dot(left_ref[...], right[:, cols], preferred_element_type=jnp.float32)
        row = 0
        for square_ref, shifts in zip(square_refs, chunk_shifts):
            for slot, shift in enumerate(shifts):
                at = pl.ds(sub_at(shift, sizes[1], rows_one), rows_one)
                square = square_ref[slot * rows_one : (slot + 1) * rows_one, cols]
                keep = keep_ref[at, cols].astype(jnp.float32)
                out_ref[at, cols] = 3.0 * square - 2.0 * (total[row : row + rows_one] * keep)
                row += rows_one
        copies.append(
            pltpu.make_async_copy(out_ref.at[:, cols], out_hbm.at[:, cols], sems.at[number])
        )
        copies[-1].start()
    for copy in copies:
        copy.wait()


def after(value, *others):
    return lax.optimization_barrier((value, *others))[0]


def on_device(density, pattern, filter_square, filter_cube):
    sizes = (lax.axis_size("row"), lax.axis_size("col"))
    row_count, col_count = sizes
    rows_one, order = density.shape
    rows = order // row_count
    width = order // col_count
    steps = col_count // 2

    local, up, down, *pieces = call(
        functools.partial(cut_kernel, col_count),
        "cut",
        [half(rows_one, order)]
        + [half(rows_one, order - width)] * 2
        + [half(rows_one, width)] * col_count,
        [pattern, density],
        10**9,
        [
            pltpu.VMEM(pattern.shape, pattern.dtype),
            pltpu.VMEM(density.shape, density.dtype),
            pltpu.SemaphoreType.DMA((2,)),
        ],
        source=HBM,
    )
    keep_square, keep_cube = (
        call(keep_kernel, "keep", half(rows, width), [mask], 2 * 10**10)
        for mask in (filter_square, filter_cube)
    )
    others = list(range(1, col_count))
    came = {shift: shifted(pieces[shift], "col", shift) for shift in others}
    own = hops(after(pieces[0], keep_square), [0])
    up, down, *ready = lax.optimization_barrier((up, down, *came.values()))
    came = dict(zip(others, ready))
    rest = jnp.concatenate(ready, axis=0)
    rest = hops(after(rest, own[1][0], own[2][0]), others)

    ups, downs = [], []
    for step in range(1, steps + 1):
        up = shifted(up, "col", 1)
        ups += [up, came[step]]
        if step == 1:
            up = after(up, rest[1][0], rest[2][0])
        if step == steps:
            break
        down = shifted(down, "col", -1)
        downs += [down, came[col_count - step]]
        up = jnp.concatenate([up[:, width:], came[step]], axis=1)
        down = jnp.concatenate([came[col_count - step], down[:, :-width]], axis=1)
    first_shifts = list(range(steps))
    last_shifts = list(range(col_count - 1, steps - 1, -1))
    first_pairs, last_pairs = ups[:-2], downs + ups[-2:]

    cut = len(rest) * 3 // 4
    columns = own + rest
    columns = columns + [swap_cores(own + rest[:cut], 10**9)]
    for piece, held in tied(rest[cut:], keep_cube):
        halves = [
            swap_cores([(piece[:, at : at + width // 2], held)], 0) for at in (0, width // 2)
        ]
        columns.append((jnp.concatenate([piece for piece, _ in halves], axis=1), halves[0][1]))
    part = rows // 2
    flops = 2 * part * order * width
    square_first, half_first, left_first, right = call(
        functools.partial(square_first_kernel, sizes, first_shifts, [held for _, held in columns]),
        "square_first",
        [full(part, width), half(part, width), half(part, order), half(order, width)],
        [keep_square, after(local, last_pairs[0]), *first_pairs, *[piece for piece, _ in columns]],
        10**8,
        limit=12,
    )
    first = hops(half_first, first_shifts, hold=lambda piece: after(piece, last_pairs[-2]))
    square_last, half_last, left = call(
        functools.partial(square_last_kernel, sizes, last_shifts),
        "square_last",
        [full(part, width), half(part, width), half(rows, order)],
        [keep_square, after(right, first[1][0], first[2][0]), left_first, *last_pairs],
        flops,
        limit=12,
    )
    last = hops(half_last, last_shifts)
    halves = first + last
    halves = halves + [swap_cores(items, 10**10) for items in (first, last[:cut], last[cut:])]
    return call(
        functools.partial(
            cube_kernel, sizes, [first_shifts, last_shifts], [held for _, held in halves]
        ),
        "cube",
        full(rows, width),
        [keep_cube, left, square_first, square_last, *[piece for piece, _ in halves]],
        2 * flops,
        [
            pltpu.VMEM((order, width), jnp.bfloat16),
            pltpu.VMEM((rows, width), jnp.float32),
            pltpu.SemaphoreType.DMA((-(-width // (2 * BLK)),)),
        ],
        18,
        target=HBM,
    )


def solution(mesh):
    placed = (P(("row", "col"), None), P(), P(), P())
    return jax.shard_map(
        on_device, mesh=mesh, in_specs=placed, out_specs=P("row", "col"), check_vma=False
    )
```

```python
import functools

import jax
import jax.numpy as jnp
from jax import lax
from jax.experimental import pallas as pl
from jax.experimental.pallas import tpu as pltpu
from jax.sharding import PartitionSpec as P

BLK = 128
VMEM = pl.BlockSpec(memory_space=pltpu.VMEM)


def shifted(block, axis, distance):
    size = lax.axis_size(axis)
    return lax.ppermute(block, axis, [(i, (i + distance) % size) for i in range(size)])


def xor_moved(block, axis, bit_of):
    size = lax.axis_size(axis)
    return lax.ppermute(block, axis, [(i, i ^ bit_of(i)) for i in range(size)])


def hops(block, held, hold_base=lambda piece: piece, hold=lambda piece: piece):
    count = lax.axis_size("row")
    bits = [1 << b for b in range(1, count.bit_length() - 1)]
    items = [(block, 0, 0)]
    for low, high in zip(bits, bits[::-1]):

        def bit_of(i, low=low, high=high):
            return high if i & 1 else low

        items = items + [
            (xor_moved(piece if even == 0 else hold(piece), "row", bit_of), even ^ low, odd ^ high)
            for piece, even, odd in items
        ]
        items[0] = (hold_base(block), 0, 0)
    return [(piece, [(even, odd, held)]) for piece, even, odd in items]


def hint(flops):
    return pl.CostEstimate(flops=flops, bytes_accessed=0, transcendentals=0)


def call(kernel, name, out_shape, inputs, flops, scratch=(), limit=4):
    return pl.pallas_call(
        kernel,
        out_shape=out_shape,
        in_specs=[VMEM] * len(inputs),
        out_specs=jax.tree.map(lambda shape: VMEM, out_shape),
        scratch_shapes=scratch,
        compiler_params=pltpu.CompilerParams(vmem_limit_bytes=limit << 20),
        cost_estimate=hint(flops),
        name=name,
    )(*inputs)


def half(*shape):
    return jax.ShapeDtypeStruct(shape, jnp.bfloat16)


def full(*shape):
    return jax.ShapeDtypeStruct(shape, jnp.float32)


def join_kernel(*refs):
    *piece_refs, out_ref = refs
    row = 0
    for ref in piece_refs:
        out_ref[row : row + ref.shape[0], :] = ref[...]
        row += ref.shape[0]


def swap_cores(items, flops):
    pieces = [piece for piece, _ in items]
    joined = pieces[0]
    if len(pieces) > 1:
        rows = sum(piece.shape[0] for piece in pieces)
        joined = call(join_kernel, "join", half(rows, pieces[0].shape[1]), pieces, flops)
    held = [(odd ^ 1, even ^ 1, shifts) for _, parts in items for even, odd, shifts in parts]
    return xor_moved(joined, "row", lambda i: 1), held


def tied(items, *others):
    ready = lax.optimization_barrier((*[piece for piece, _ in items], *others))
    return [(piece, held) for piece, (_, held) in zip(ready, items)]


def iota(shape, axis):
    return lax.broadcasted_iota(jnp.int32, shape, axis)


def expand(mask, row_start, rows, col_start, cols):
    nblocks = mask.shape[0]
    pick_row = (row_start + iota((rows, nblocks), 0)) // BLK == iota((rows, nblocks), 1)
    pick_col = (col_start + iota((nblocks, cols), 1)) // BLK == iota((nblocks, cols), 0)
    lines = jnp.dot(
        pick_row.astype(jnp.bfloat16),
        mask.astype(jnp.float32).astype(jnp.bfloat16),
        preferred_element_type=jnp.float32,
    )
    return jnp.dot(
        lines.astype(jnp.bfloat16),
        pick_col.astype(jnp.bfloat16),
        preferred_element_type=jnp.float32,
    ).astype(jnp.bfloat16)


def block_at(shift, col_count, width):
    return pl.multiple_of(lax.rem(lax.axis_index("col") + shift, col_count) * width, BLK)


def sub_at(shift, col_count, rows_one):
    return pl.multiple_of(
        lax.rem(lax.axis_index("col") + (col_count - shift), col_count) * rows_one, 16
    )


def cut_kernel(col_count, pattern_ref, density_ref, local_ref, up_ref, down_ref, *piece_refs):
    rows_one, order = density_ref.shape
    width = order // col_count
    first = lax.axis_index("row") * (col_count * rows_one) + sub_at(0, col_count, rows_one)
    local_ref[...] = density_ref[...] * expand(pattern_ref[...], first, rows_one, 0, order)
    for shift, piece_ref in enumerate(piece_refs):
        piece = local_ref[:, pl.ds(block_at(shift, col_count, width), width)]
        piece_ref[...] = piece
        if shift != 1:
            slot = (shift - 2) % col_count
            up_ref[:, slot * width : (slot + 1) * width] = piece
        if shift != col_count - 1:
            down_ref[:, shift * width : (shift + 1) * width] = piece


def keep_kernel(filter_ref, keep_ref):
    rows, width = keep_ref.shape
    row_at, col_at = lax.axis_index("row") * rows, lax.axis_index("col") * width
    keep_ref[...] = expand(filter_ref[...], row_at, rows, col_at, width)


def fill_left(left, first, whole_refs, pair_refs, col_count):
    at = first
    for ref in whole_refs:
        left[at : at + ref.shape[0], :] = ref[...]
        at += ref.shape[0]
    for most_ref, own_ref in zip(pair_refs[::2], pair_refs[1::2]):
        rows_one, width = own_ref.shape
        left[at : at + rows_one, pl.ds(block_at(0, col_count, width), width)] = own_ref[...]
        for slot in range(col_count - 1):
            columns = pl.ds(block_at(slot + 1, col_count, width), width)
            left[at : at + rows_one, columns] = most_ref[:, slot * width : (slot + 1) * width]
        at += rows_one


def fill_right(right, refs, layouts, sizes):
    row_count, col_count = sizes
    rows = right.shape[0] // row_count
    rows_one = rows // col_count
    row_id = lax.axis_index("row")
    odd_core = lax.rem(row_id, 2) == 1
    for ref, held in zip(refs, layouts):
        row = 0
        for even, odd, shifts in held:
            place = pl.multiple_of((row_id ^ jnp.where(odd_core, odd, even)) * rows, BLK)
            for shift in shifts:
                at = pl.multiple_of(place + sub_at(shift, col_count, rows_one), 16)
                right[pl.ds(at, rows_one), :] = ref[row : row + rows_one, :]
                row += rows_one


def split_refs(refs, counts):
    groups = []
    for count in counts:
        groups.append(refs[:count])
        refs = refs[count:]
    return groups + [refs]


def square_part(left, right, shifts, col_count, keep_ref, square_ref, half_ref):
    rows_one = square_ref.shape[0] // len(shifts)
    total = jnp.dot(left, right, preferred_element_type=jnp.float32)
    for slot, shift in enumerate(shifts):
        at = slice(slot * rows_one, (slot + 1) * rows_one)
        keep = keep_ref[pl.ds(sub_at(shift, col_count, rows_one), rows_one), :]
        part = total[at] * keep.astype(jnp.float32)
        square_ref[at, :] = part
        half_ref[at, :] = part.astype(jnp.bfloat16)


def square_first_kernel(sizes, shifts, layouts, keep_ref, local_ref, *refs):
    pair_refs, piece_refs, rest = split_refs(refs, [2 * len(shifts) - 2, len(layouts)])
    square_ref, half_ref, left_ref, right_ref = rest
    fill_left(left_ref, 0, [local_ref], pair_refs, sizes[1])
    fill_right(right_ref, piece_refs, layouts, sizes)
    square_part(left_ref[...], right_ref[...], shifts, sizes[1], keep_ref, square_ref, half_ref)


def stack_kernel(col_count, before_ref, *refs):
    *pair_refs, left_ref = refs
    fill_left(left_ref, 0, [before_ref], pair_refs, col_count)


def square_last_kernel(sizes, shifts, keep_ref, right_ref, left_ref, square_ref, half_ref):
    left = left_ref[-square_ref.shape[0] :, :]
    square_part(left, right_ref[...], shifts, sizes[1], keep_ref, square_ref, half_ref)


def pick_kernel(sizes, shift, left_ref, picked_ref, select):
    row_count, col_count = sizes
    order, count = select.shape
    rows_one = count // row_count
    column = iota((order, count), 1)
    from_row = column + (column // rows_one) * (order // row_count - rows_one)
    from_row = from_row + sub_at(shift, col_count, rows_one)
    select[...] = (iota((order, count), 0) == from_row).astype(jnp.bfloat16)
    picked = jnp.dot(left_ref[...], select[...], preferred_element_type=jnp.float32)
    picked_ref[...] = picked.astype(jnp.bfloat16)


def cube_first_kernel(sizes, shifts, layouts, keep_ref, left_ref, *refs):
    (first_ref, last_ref), piece_refs, (out_ref, right) = split_refs(refs, [2, len(layouts)])
    rows_one = last_ref.shape[0]
    right[...] = jnp.zeros_like(right)
    fill_right(right, piece_refs, layouts, sizes)
    total = jnp.dot(left_ref[...], right[...], preferred_element_type=jnp.float32)
    for slot, shift in enumerate(shifts + [sizes[1] // 2]):
        part = slice(slot * rows_one, (slot + 1) * rows_one)
        keep = keep_ref[pl.ds(sub_at(shift, sizes[1], rows_one), rows_one), :]
        square = last_ref[...] if slot == len(shifts) else first_ref[part, :]
        out_ref[part, :] = 3.0 * square - 2.0 * (total[part] * keep.astype(jnp.float32))


def cube_last_kernel(sizes, shifts, layouts, keep_ref, picked_ref, started_ref, *refs):
    *piece_refs, out_ref, right = refs
    row_count, col_count = sizes
    rows_one = right.shape[0] // row_count
    row_id = lax.axis_index("row")
    odd_core = lax.rem(row_id, 2) == 1
    for ref, held in zip(piece_refs, layouts):
        for slot, (even, odd, _) in enumerate(held):
            place = pl.multiple_of((row_id ^ jnp.where(odd_core, odd, even)) * rows_one, 16)
            right[pl.ds(place, rows_one), :] = ref[slot * rows_one : (slot + 1) * rows_one, :]
    total = jnp.dot(picked_ref[...], right[...], preferred_element_type=jnp.float32)
    for slot, shift in enumerate(shifts + [col_count // 2]):
        part = slice(slot * rows_one, (slot + 1) * rows_one)
        at = pl.ds(sub_at(shift, col_count, rows_one), rows_one)
        out_ref[at, :] = started_ref[part, :] - 2.0 * (
            total[part] * keep_ref[at, :].astype(jnp.float32)
        )


def after(value, *others):
    return lax.optimization_barrier((value, *others))[0]


def on_device(density, pattern, filter_square, filter_cube):
    sizes = (lax.axis_size("row"), lax.axis_size("col"))
    row_count, col_count = sizes
    rows_one, order = density.shape
    rows = order // row_count
    width = order // col_count
    steps = col_count // 2

    local, up, down, *pieces = call(
        functools.partial(cut_kernel, col_count),
        "cut",
        [half(rows_one, order)]
        + [half(rows_one, order - width)] * 2
        + [half(rows_one, width)] * col_count,
        [pattern, density],
        10**9,
    )
    keep_square, keep_cube = (
        call(keep_kernel, "keep", half(rows, width), [mask], 2 * 10**10)
        for mask in (filter_square, filter_cube)
    )
    others = list(range(1, col_count))
    came = {shift: shifted(pieces[shift], "col", shift) for shift in others}
    own = hops(after(pieces[0], keep_square), [0])
    up, down, *ready = lax.optimization_barrier((up, down, *came.values()))
    came = dict(zip(others, ready))
    rest = jnp.concatenate(ready, axis=0)
    rest = hops(after(rest, own[1][0], own[2][0]), others)

    ups, downs = [], []
    for step in range(1, steps + 1):
        up = shifted(up, "col", 1)
        ups += [up, came[step]]
        if step == 1:
            up = after(up, rest[1][0], rest[2][0])
        if step == steps:
            break
        down = shifted(down, "col", -1)
        downs += [down, came[col_count - step]]
        up = jnp.concatenate([up[:, width:], came[step]], axis=1)
        down = jnp.concatenate([came[col_count - step], down[:, :-width]], axis=1)
    first_shifts = list(range(steps)) + list(range(col_count - 1, steps, -1))
    first_pairs, last_pairs = ups[:-2] + downs, ups[-2:]

    cut = len(rest) * 3 // 4
    columns = own + rest
    columns = columns + [
        swap_cores(own, 10**9),
        swap_cores(rest[:cut], 10**9),
        swap_cores(tied(rest[cut:], ups[0], downs[0], keep_cube), 10**9),
    ]
    most = rows - rows_one
    flops = 2 * rows_one * order * width
    square_first, half_first, left_first, right = call(
        functools.partial(square_first_kernel, sizes, first_shifts, [held for _, held in columns]),
        "square_first",
        [full(most, width), half(most, width), half(most, order), half(order, width)],
        [keep_square, local, *first_pairs, *[piece for piece, _ in columns]],
        3 * flops,
        limit=12,
    )
    left = call(
        functools.partial(stack_kernel, col_count),
        "stack",
        half(rows, order),
        [left_first, *last_pairs],
        2 * 10**9,
    )
    first = hops(half_first, first_shifts, hold=lambda piece: after(piece, left))
    square_last, half_last = call(
        functools.partial(square_last_kernel, sizes, [steps]),
        "square_last",
        [full(rows_one, width), half(rows_one, width)],
        [keep_square, after(right, first[1][0], first[2][0]), left],
        flops,
        limit=12,
    )
    picked = call(
        functools.partial(pick_kernel, sizes, steps),
        "pick",
        half(rows, order // col_count),
        [left],
        2 * 10**10,
        [pltpu.VMEM((order, order // col_count), jnp.bfloat16)],
        16,
    )
    last = hops(half_last, [steps], hold=lambda piece: after(piece, picked))
    firsts = first + [
        swap_cores(tied(first[:cut], half_last), 10**9),
        swap_cores(first[cut:], 10**9),
    ]
    started = call(
        functools.partial(cube_first_kernel, sizes, first_shifts, [held for _, held in firsts]),
        "cube_first",
        full(rows, width),
        [after(keep_cube, last[1][0], last[2][0]), left, square_first, square_last]
        + [piece for piece, _ in firsts],
        10**10,
        [pltpu.VMEM((order, width), jnp.bfloat16)],
        16,
    )
    lasts = last + [swap_cores(last[:cut], 10**9), swap_cores(tied(last[cut:], started), 10**9)]
    return call(
        functools.partial(cube_last_kernel, sizes, first_shifts, [held for _, held in lasts]),
        "cube_last",
        full(rows, width),
        [keep_cube, picked, started, *[piece for piece, _ in lasts]],
        flops,
        [pltpu.VMEM((order // col_count, width), jnp.bfloat16)],
        10,
    )


def solution(mesh):
    placed = (P(("row", "col"), None), P(), P(), P())
    return jax.shard_map(
        on_device, mesh=mesh, in_specs=placed, out_specs=P("row", "col"), check_vma=False
    )
```

```python
import functools

import jax
import jax.numpy as jnp
from jax import lax
from jax.experimental import pallas as pl
from jax.experimental.pallas import tpu as pltpu
from jax.sharding import PartitionSpec as P

BLK = 128
VMEM = pl.BlockSpec(memory_space=pltpu.VMEM)


def shifted(block, axis, distance):
    size = lax.axis_size(axis)
    return lax.ppermute(block, axis, [(i, (i + distance) % size) for i in range(size)])


def xor_moved(block, axis, bit_of):
    size = lax.axis_size(axis)
    return lax.ppermute(block, axis, [(i, i ^ bit_of(i)) for i in range(size)])


def hops(block, held, hold_base=lambda piece: piece, hold=lambda piece: piece):
    count = lax.axis_size("row")
    bits = [1 << b for b in range(1, count.bit_length() - 1)]
    items = [(block, 0, 0)]
    for low, high in zip(bits, bits[::-1]):

        def bit_of(i, low=low, high=high):
            return high if i & 1 else low

        items = items + [
            (xor_moved(piece if even == 0 else hold(piece), "row", bit_of), even ^ low, odd ^ high)
            for piece, even, odd in items
        ]
        items[0] = (hold_base(block), 0, 0)
    return [(piece, [(even, odd, held)]) for piece, even, odd in items]


def hint(flops):
    return pl.CostEstimate(flops=flops, bytes_accessed=0, transcendentals=0)


def call(kernel, name, out_shape, inputs, flops, scratch=(), limit=4):
    return pl.pallas_call(
        kernel,
        out_shape=out_shape,
        in_specs=[VMEM] * len(inputs),
        out_specs=jax.tree.map(lambda shape: VMEM, out_shape),
        scratch_shapes=scratch,
        compiler_params=pltpu.CompilerParams(vmem_limit_bytes=limit << 20),
        cost_estimate=hint(flops),
        name=name,
    )(*inputs)


def half(*shape):
    return jax.ShapeDtypeStruct(shape, jnp.bfloat16)


def full(*shape):
    return jax.ShapeDtypeStruct(shape, jnp.float32)


def join_kernel(*refs):
    *piece_refs, out_ref = refs
    row = 0
    for ref in piece_refs:
        out_ref[row : row + ref.shape[0], :] = ref[...]
        row += ref.shape[0]


def swap_cores(items, flops):
    pieces = [piece for piece, _ in items]
    joined = pieces[0]
    if len(pieces) > 1:
        rows = sum(piece.shape[0] for piece in pieces)
        joined = call(join_kernel, "join", half(rows, pieces[0].shape[1]), pieces, flops)
    held = [(odd ^ 1, even ^ 1, shifts) for _, parts in items for even, odd, shifts in parts]
    return xor_moved(joined, "row", lambda i: 1), held


def tied(items, *others):
    ready = lax.optimization_barrier((*[piece for piece, _ in items], *others))
    return [(piece, held) for piece, (_, held) in zip(ready, items)]


def iota(shape, axis):
    return lax.broadcasted_iota(jnp.int32, shape, axis)


def expand(mask, row_start, rows, col_start, cols):
    nblocks = mask.shape[0]
    pick_row = (row_start + iota((rows, nblocks), 0)) // BLK == iota((rows, nblocks), 1)
    pick_col = (col_start + iota((nblocks, cols), 1)) // BLK == iota((nblocks, cols), 0)
    lines = jnp.dot(
        pick_row.astype(jnp.bfloat16),
        mask.astype(jnp.float32).astype(jnp.bfloat16),
        preferred_element_type=jnp.float32,
    )
    return jnp.dot(
        lines.astype(jnp.bfloat16),
        pick_col.astype(jnp.bfloat16),
        preferred_element_type=jnp.float32,
    ).astype(jnp.bfloat16)


def block_at(shift, col_count, width):
    return pl.multiple_of(lax.rem(lax.axis_index("col") + shift, col_count) * width, BLK)


def sub_at(shift, col_count, rows_one):
    return pl.multiple_of(
        lax.rem(lax.axis_index("col") + (col_count - shift), col_count) * rows_one, 16
    )


def cut_kernel(col_count, pattern_ref, density_ref, local_ref, up_ref, down_ref, *piece_refs):
    rows_one, order = density_ref.shape
    width = order // col_count
    first = lax.axis_index("row") * (col_count * rows_one) + sub_at(0, col_count, rows_one)
    local_ref[...] = density_ref[...] * expand(pattern_ref[...], first, rows_one, 0, order)
    for shift, piece_ref in enumerate(piece_refs):
        piece = local_ref[:, pl.ds(block_at(shift, col_count, width), width)]
        piece_ref[...] = piece
        if shift != 1:
            slot = (shift - 2) % col_count
            up_ref[:, slot * width : (slot + 1) * width] = piece
        if shift != col_count - 1:
            down_ref[:, shift * width : (shift + 1) * width] = piece


def keep_kernel(filter_ref, keep_ref):
    rows, width = keep_ref.shape
    row_at, col_at = lax.axis_index("row") * rows, lax.axis_index("col") * width
    keep_ref[...] = expand(filter_ref[...], row_at, rows, col_at, width)


def fill_left(left, first, whole_refs, pair_refs, col_count):
    at = first
    for ref in whole_refs:
        left[at : at + ref.shape[0], :] = ref[...]
        at += ref.shape[0]
    for most_ref, own_ref in zip(pair_refs[::2], pair_refs[1::2]):
        rows_one, width = own_ref.shape
        left[at : at + rows_one, pl.ds(block_at(0, col_count, width), width)] = own_ref[...]
        for slot in range(col_count - 1):
            columns = pl.ds(block_at(slot + 1, col_count, width), width)
            left[at : at + rows_one, columns] = most_ref[:, slot * width : (slot + 1) * width]
        at += rows_one


def fill_right(right, refs, layouts, sizes):
    row_count, col_count = sizes
    rows = right.shape[0] // row_count
    rows_one = rows // col_count
    row_id = lax.axis_index("row")
    odd_core = lax.rem(row_id, 2) == 1
    for ref, held in zip(refs, layouts):
        row = 0
        for even, odd, shifts in held:
            place = pl.multiple_of((row_id ^ jnp.where(odd_core, odd, even)) * rows, BLK)
            for shift in shifts:
                at = pl.multiple_of(place + sub_at(shift, col_count, rows_one), 16)
                right[pl.ds(at, rows_one), :] = ref[row : row + rows_one, :]
                row += rows_one


def split_refs(refs, counts):
    groups = []
    for count in counts:
        groups.append(refs[:count])
        refs = refs[count:]
    return groups + [refs]


def square_part(left, right, shifts, col_count, keep_ref, square_ref, half_ref):
    rows_one = square_ref.shape[0] // len(shifts)
    total = jnp.dot(left, right, preferred_element_type=jnp.float32)
    for slot, shift in enumerate(shifts):
        at = slice(slot * rows_one, (slot + 1) * rows_one)
        keep = keep_ref[pl.ds(sub_at(shift, col_count, rows_one), rows_one), :]
        part = total[at] * keep.astype(jnp.float32)
        square_ref[at, :] = part
        half_ref[at, :] = part.astype(jnp.bfloat16)


def square_first_kernel(sizes, shifts, layouts, keep_ref, local_ref, *refs):
    pair_refs, piece_refs, rest = split_refs(refs, [2 * len(shifts) - 2, len(layouts)])
    square_ref, half_ref, left_ref, right_ref = rest
    fill_left(left_ref, 0, [local_ref], pair_refs, sizes[1])
    fill_right(right_ref, piece_refs, layouts, sizes)
    square_part(left_ref[...], right_ref[...], shifts, sizes[1], keep_ref, square_ref, half_ref)


def stack_kernel(col_count, before_ref, *refs):
    *pair_refs, left_ref = refs
    fill_left(left_ref, 0, [before_ref], pair_refs, col_count)


def square_last_kernel(sizes, shifts, keep_ref, right_ref, left_ref, square_ref, half_ref):
    left = left_ref[-square_ref.shape[0] :, :]
    square_part(left, right_ref[...], shifts, sizes[1], keep_ref, square_ref, half_ref)


def pick_kernel(sizes, shift, left_ref, picked_ref, select):
    row_count, col_count = sizes
    order, count = select.shape
    rows_one = count // row_count
    column = iota((order, count), 1)
    from_row = column + (column // rows_one) * (order // row_count - rows_one)
    from_row = from_row + sub_at(shift, col_count, rows_one)
    select[...] = (iota((order, count), 0) == from_row).astype(jnp.bfloat16)
    picked = jnp.dot(left_ref[...], select[...], preferred_element_type=jnp.float32)
    picked_ref[...] = picked.astype(jnp.bfloat16)


def cube_first_kernel(sizes, shifts, layouts, keep_ref, left_ref, *refs):
    (first_ref, last_ref), piece_refs, (out_ref, right) = split_refs(refs, [2, len(layouts)])
    rows_one = last_ref.shape[0]
    right[...] = jnp.zeros_like(right)
    fill_right(right, piece_refs, layouts, sizes)
    total = jnp.dot(left_ref[...], right[...], preferred_element_type=jnp.float32)
    for slot, shift in enumerate(shifts + [sizes[1] // 2]):
        part = slice(slot * rows_one, (slot + 1) * rows_one)
        keep = keep_ref[pl.ds(sub_at(shift, sizes[1], rows_one), rows_one), :]
        square = last_ref[...] if slot == len(shifts) else first_ref[part, :]
        out_ref[part, :] = 3.0 * square - 2.0 * (total[part] * keep.astype(jnp.float32))


def cube_last_kernel(sizes, shifts, layouts, keep_ref, picked_ref, started_ref, *refs):
    *piece_refs, out_ref, right = refs
    row_count, col_count = sizes
    rows_one = right.shape[0] // row_count
    row_id = lax.axis_index("row")
    odd_core = lax.rem(row_id, 2) == 1
    for ref, held in zip(piece_refs, layouts):
        for slot, (even, odd, _) in enumerate(held):
            place = pl.multiple_of((row_id ^ jnp.where(odd_core, odd, even)) * rows_one, 16)
            right[pl.ds(place, rows_one), :] = ref[slot * rows_one : (slot + 1) * rows_one, :]
    total = jnp.dot(picked_ref[...], right[...], preferred_element_type=jnp.float32)
    for slot, shift in enumerate(shifts + [col_count // 2]):
        part = slice(slot * rows_one, (slot + 1) * rows_one)
        at = pl.ds(sub_at(shift, col_count, rows_one), rows_one)
        out_ref[at, :] = started_ref[part, :] - 2.0 * (
            total[part] * keep_ref[at, :].astype(jnp.float32)
        )


def after(value, *others):
    return lax.optimization_barrier((value, *others))[0]


def on_device(density, pattern, filter_square, filter_cube):
    sizes = (lax.axis_size("row"), lax.axis_size("col"))
    row_count, col_count = sizes
    rows_one, order = density.shape
    rows = order // row_count
    width = order // col_count
    steps = col_count // 2

    local, up, down, *pieces = call(
        functools.partial(cut_kernel, col_count),
        "cut",
        [half(rows_one, order)]
        + [half(rows_one, order - width)] * 2
        + [half(rows_one, width)] * col_count,
        [pattern, density],
        10**9,
    )
    keep_square, keep_cube = (
        call(keep_kernel, "keep", half(rows, width), [mask], 2 * 10**10)
        for mask in (filter_square, filter_cube)
    )
    others = list(range(1, col_count))
    came = {shift: shifted(pieces[shift], "col", shift) for shift in others}
    own = hops(after(pieces[0], keep_square), [0])
    up, down, *ready = lax.optimization_barrier((up, down, *came.values()))
    came = dict(zip(others, ready))
    rest = jnp.concatenate(ready, axis=0)
    rest = hops(
        after(rest, own[1][0], own[2][0]), others, lambda piece: after(piece, own[-1][0])
    )

    ups, downs = [], []
    for step in range(1, steps + 1):
        up = shifted(up, "col", 1)
        ups += [up, came[step]]
        if step == 1:
            up = after(up, rest[1][0], rest[2][0])
        if step == steps:
            break
        down = shifted(down, "col", -1)
        downs += [down, came[col_count - step]]
        up = jnp.concatenate([up[:, width:], came[step]], axis=1)
        down = jnp.concatenate([came[col_count - step], down[:, :-width]], axis=1)
    first_shifts = list(range(steps)) + list(range(col_count - 1, steps, -1))
    first_pairs, last_pairs = ups[:-2] + downs, ups[-2:]

    cut = len(rest) * 3 // 4
    columns = own + rest
    columns = columns + [
        swap_cores(own + rest[:2], 10**9),
        swap_cores(tied(rest[2:], ups[0], downs[0], keep_cube), 10**9),
    ]
    most = rows - rows_one
    flops = 2 * rows_one * order * width
    square_first, half_first, left_first, right = call(
        functools.partial(square_first_kernel, sizes, first_shifts, [held for _, held in columns]),
        "square_first",
        [full(most, width), half(most, width), half(most, order), half(order, width)],
        [keep_square, local, *first_pairs, *[piece for piece, _ in columns]],
        3 * flops,
        limit=12,
    )
    left = call(
        functools.partial(stack_kernel, col_count),
        "stack",
        half(rows, order),
        [left_first, *last_pairs],
        2 * 10**9,
    )
    first = hops(half_first, first_shifts, hold=lambda piece: after(piece, left))
    square_last, half_last = call(
        functools.partial(square_last_kernel, sizes, [steps]),
        "square_last",
        [full(rows_one, width), half(rows_one, width)],
        [keep_square, after(right, first[1][0], first[2][0]), left],
        flops,
        limit=12,
    )
    picked = call(
        functools.partial(pick_kernel, sizes, steps),
        "pick",
        half(rows, order // col_count),
        [left],
        2 * 10**10,
        [pltpu.VMEM((order, order // col_count), jnp.bfloat16)],
        16,
    )
    last = hops(half_last, [steps], hold=lambda piece: after(piece, picked))
    firsts = first + [
        swap_cores(tied(first[:cut], half_last), 10**9),
        swap_cores(first[cut:], 10**9),
    ]
    started = call(
        functools.partial(cube_first_kernel, sizes, first_shifts, [held for _, held in firsts]),
        "cube_first",
        full(rows, width),
        [after(keep_cube, last[1][0], last[2][0]), left, square_first, square_last]
        + [piece for piece, _ in firsts],
        10**10,
        [pltpu.VMEM((order, width), jnp.bfloat16)],
        16,
    )
    lasts = last + [swap_cores(last[:cut], 10**9), swap_cores(tied(last[cut:], started), 10**9)]
    return call(
        functools.partial(cube_last_kernel, sizes, first_shifts, [held for _, held in lasts]),
        "cube_last",
        full(rows, width),
        [keep_cube, picked, started, *[piece for piece, _ in lasts]],
        flops,
        [pltpu.VMEM((order // col_count, width), jnp.bfloat16)],
        10,
    )


def solution(mesh):
    placed = (P(("row", "col"), None), P(), P(), P())
    return jax.shard_map(
        on_device, mesh=mesh, in_specs=placed, out_specs=P("row", "col"), check_vma=False
    )
```

```python
import functools

import jax
import jax.numpy as jnp
from jax import lax
from jax.experimental import pallas as pl
from jax.experimental.pallas import tpu as pltpu
from jax.sharding import PartitionSpec as P

BLK = 128
VMEM = pl.BlockSpec(memory_space=pltpu.VMEM)


def shifted(block, axis, distance):
    size = lax.axis_size(axis)
    return lax.ppermute(block, axis, [(i, (i + distance) % size) for i in range(size)])


def xor_moved(block, axis, bit_of):
    size = lax.axis_size(axis)
    return lax.ppermute(block, axis, [(i, i ^ bit_of(i)) for i in range(size)])


def hops(block, held, hold_base=lambda piece: piece, hold=lambda piece: piece):
    count = lax.axis_size("row")
    bits = [1 << b for b in range(1, count.bit_length() - 1)]
    items = [(block, 0, 0)]
    for low, high in zip(bits, bits[::-1]):

        def bit_of(i, low=low, high=high):
            return high if i & 1 else low

        items = items + [
            (xor_moved(piece if even == 0 else hold(piece), "row", bit_of), even ^ low, odd ^ high)
            for piece, even, odd in items
        ]
        items[0] = (hold_base(block), 0, 0)
    return [(piece, [(even, odd, held)]) for piece, even, odd in items]


def hint(flops):
    return pl.CostEstimate(flops=flops, bytes_accessed=0, transcendentals=0)


def call(kernel, name, out_shape, inputs, flops, scratch=(), limit=4):
    return pl.pallas_call(
        kernel,
        out_shape=out_shape,
        in_specs=[VMEM] * len(inputs),
        out_specs=jax.tree.map(lambda shape: VMEM, out_shape),
        scratch_shapes=scratch,
        compiler_params=pltpu.CompilerParams(vmem_limit_bytes=limit << 20),
        cost_estimate=hint(flops),
        name=name,
    )(*inputs)


def half(*shape):
    return jax.ShapeDtypeStruct(shape, jnp.bfloat16)


def full(*shape):
    return jax.ShapeDtypeStruct(shape, jnp.float32)


def join_kernel(*refs):
    *piece_refs, out_ref = refs
    row = 0
    for ref in piece_refs:
        out_ref[row : row + ref.shape[0], :] = ref[...]
        row += ref.shape[0]


def swap_cores(items, flops):
    pieces = [piece for piece, _ in items]
    joined = pieces[0]
    if len(pieces) > 1:
        rows = sum(piece.shape[0] for piece in pieces)
        joined = call(join_kernel, "join", half(rows, pieces[0].shape[1]), pieces, flops)
    held = [(odd ^ 1, even ^ 1, shifts) for _, parts in items for even, odd, shifts in parts]
    return xor_moved(joined, "row", lambda i: 1), held


def tied(items, *others):
    ready = lax.optimization_barrier((*[piece for piece, _ in items], *others))
    return [(piece, held) for piece, (_, held) in zip(ready, items)]


def iota(shape, axis):
    return lax.broadcasted_iota(jnp.int32, shape, axis)


def expand(mask, row_start, rows, col_start, cols):
    nblocks = mask.shape[0]
    pick_row = (row_start + iota((rows, nblocks), 0)) // BLK == iota((rows, nblocks), 1)
    pick_col = (col_start + iota((nblocks, cols), 1)) // BLK == iota((nblocks, cols), 0)
    lines = jnp.dot(
        pick_row.astype(jnp.bfloat16),
        mask.astype(jnp.float32).astype(jnp.bfloat16),
        preferred_element_type=jnp.float32,
    )
    return jnp.dot(
        lines.astype(jnp.bfloat16),
        pick_col.astype(jnp.bfloat16),
        preferred_element_type=jnp.float32,
    ).astype(jnp.bfloat16)


def block_at(shift, col_count, width):
    return pl.multiple_of(lax.rem(lax.axis_index("col") + shift, col_count) * width, BLK)


def sub_at(shift, col_count, rows_one):
    return pl.multiple_of(
        lax.rem(lax.axis_index("col") + (col_count - shift), col_count) * rows_one, 16
    )


def cut_kernel(col_count, pattern_ref, density_ref, local_ref, up_ref, down_ref, *piece_refs):
    rows_one, order = density_ref.shape
    width = order // col_count
    first = lax.axis_index("row") * (col_count * rows_one) + sub_at(0, col_count, rows_one)
    local_ref[...] = density_ref[...] * expand(pattern_ref[...], first, rows_one, 0, order)
    for shift, piece_ref in enumerate(piece_refs):
        piece = local_ref[:, pl.ds(block_at(shift, col_count, width), width)]
        piece_ref[...] = piece
        if shift != 1:
            slot = (shift - 2) % col_count
            up_ref[:, slot * width : (slot + 1) * width] = piece
        if shift != col_count - 1:
            down_ref[:, shift * width : (shift + 1) * width] = piece


def keep_kernel(filter_ref, keep_ref):
    rows, width = keep_ref.shape
    row_at, col_at = lax.axis_index("row") * rows, lax.axis_index("col") * width
    keep_ref[...] = expand(filter_ref[...], row_at, rows, col_at, width)


def fill_left(left, first, whole_refs, pair_refs, col_count):
    at = first
    for ref in whole_refs:
        left[at : at + ref.shape[0], :] = ref[...]
        at += ref.shape[0]
    for most_ref, own_ref in zip(pair_refs[::2], pair_refs[1::2]):
        rows_one, width = own_ref.shape
        left[at : at + rows_one, pl.ds(block_at(0, col_count, width), width)] = own_ref[...]
        for slot in range(col_count - 1):
            columns = pl.ds(block_at(slot + 1, col_count, width), width)
            left[at : at + rows_one, columns] = most_ref[:, slot * width : (slot + 1) * width]
        at += rows_one


def fill_right(right, refs, layouts, sizes):
    row_count, col_count = sizes
    rows = right.shape[0] // row_count
    rows_one = rows // col_count
    row_id = lax.axis_index("row")
    odd_core = lax.rem(row_id, 2) == 1
    for ref, held in zip(refs, layouts):
        row = 0
        for even, odd, shifts in held:
            place = pl.multiple_of((row_id ^ jnp.where(odd_core, odd, even)) * rows, BLK)
            for shift in shifts:
                at = pl.multiple_of(place + sub_at(shift, col_count, rows_one), 16)
                right[pl.ds(at, rows_one), :] = ref[row : row + rows_one, :]
                row += rows_one


def split_refs(refs, counts):
    groups = []
    for count in counts:
        groups.append(refs[:count])
        refs = refs[count:]
    return groups + [refs]


def square_part(left, right, shifts, col_count, keep_ref, square_ref, half_ref):
    rows_one = square_ref.shape[0] // len(shifts)
    total = jnp.dot(left, right, preferred_element_type=jnp.float32)
    for slot, shift in enumerate(shifts):
        at = slice(slot * rows_one, (slot + 1) * rows_one)
        keep = keep_ref[pl.ds(sub_at(shift, col_count, rows_one), rows_one), :]
        part = total[at] * keep.astype(jnp.float32)
        square_ref[at, :] = part
        half_ref[at, :] = part.astype(jnp.bfloat16)


def square_first_kernel(sizes, shifts, layouts, keep_ref, local_ref, *refs):
    pair_refs, piece_refs, rest = split_refs(refs, [2 * len(shifts) - 2, len(layouts)])
    square_ref, half_ref, left_ref, right_ref = rest
    fill_left(left_ref, 0, [local_ref], pair_refs, sizes[1])
    fill_right(right_ref, piece_refs, layouts, sizes)
    square_part(left_ref[...], right_ref[...], shifts, sizes[1], keep_ref, square_ref, half_ref)


def stack_kernel(col_count, before_ref, *refs):
    *pair_refs, left_ref = refs
    fill_left(left_ref, 0, [before_ref], pair_refs, col_count)


def square_last_kernel(sizes, shifts, keep_ref, right_ref, left_ref, square_ref, half_ref):
    left = left_ref[-square_ref.shape[0] :, :]
    square_part(left, right_ref[...], shifts, sizes[1], keep_ref, square_ref, half_ref)


def pick_kernel(sizes, shift, left_ref, picked_ref, select):
    row_count, col_count = sizes
    order, count = select.shape
    rows_one = count // row_count
    column = iota((order, count), 1)
    from_row = column + (column // rows_one) * (order // row_count - rows_one)
    from_row = from_row + sub_at(shift, col_count, rows_one)
    select[...] = (iota((order, count), 0) == from_row).astype(jnp.bfloat16)
    picked = jnp.dot(left_ref[...], select[...], preferred_element_type=jnp.float32)
    picked_ref[...] = picked.astype(jnp.bfloat16)


def cube_first_kernel(sizes, chunk_shifts, layouts, keep_ref, left_ref, *refs):
    square_refs, piece_refs, rest = split_refs(refs, [len(chunk_shifts), len(layouts)])
    out_ref, right = rest
    rows_one = out_ref.shape[0] // sizes[1]
    right[...] = jnp.zeros_like(right)
    fill_right(right, piece_refs, layouts, sizes)
    total = jnp.dot(left_ref[...], right[...], preferred_element_type=jnp.float32)
    row = 0
    for square_ref, shifts in zip(square_refs, chunk_shifts):
        for slot, shift in enumerate(shifts):
            part = slice(row, row + rows_one)
            keep = keep_ref[pl.ds(sub_at(shift, sizes[1], rows_one), rows_one), :]
            square = square_ref[slot * rows_one : (slot + 1) * rows_one, :]
            out_ref[part, :] = 3.0 * square - 2.0 * (total[part] * keep.astype(jnp.float32))
            row += rows_one


def cube_last_kernel(sizes, shifts, layouts, keep_ref, picked_ref, started_ref, *refs):
    *piece_refs, out_ref, right = refs
    row_count, col_count = sizes
    rows_one = right.shape[0] // row_count
    row_id = lax.axis_index("row")
    odd_core = lax.rem(row_id, 2) == 1
    for ref, held in zip(piece_refs, layouts):
        for slot, (even, odd, _) in enumerate(held):
            place = pl.multiple_of((row_id ^ jnp.where(odd_core, odd, even)) * rows_one, 16)
            right[pl.ds(place, rows_one), :] = ref[slot * rows_one : (slot + 1) * rows_one, :]
    total = jnp.dot(picked_ref[...], right[...], preferred_element_type=jnp.float32)
    for slot, shift in enumerate(shifts + [col_count // 2]):
        part = slice(slot * rows_one, (slot + 1) * rows_one)
        at = pl.ds(sub_at(shift, col_count, rows_one), rows_one)
        out_ref[at, :] = started_ref[part, :] - 2.0 * (
            total[part] * keep_ref[at, :].astype(jnp.float32)
        )


def after(value, *others):
    return lax.optimization_barrier((value, *others))[0]


def on_device(density, pattern, filter_square, filter_cube):
    sizes = (lax.axis_size("row"), lax.axis_size("col"))
    row_count, col_count = sizes
    rows_one, order = density.shape
    rows = order // row_count
    width = order // col_count
    steps = col_count // 2

    local, up, down, *pieces = call(
        functools.partial(cut_kernel, col_count),
        "cut",
        [half(rows_one, order)]
        + [half(rows_one, order - width)] * 2
        + [half(rows_one, width)] * col_count,
        [pattern, density],
        10**9,
    )
    keep_square, keep_cube = (
        call(keep_kernel, "keep", half(rows, width), [mask], 2 * 10**10)
        for mask in (filter_square, filter_cube)
    )
    others = list(range(1, col_count))
    came = {shift: shifted(pieces[shift], "col", shift) for shift in others}
    own = hops(after(pieces[0], keep_square), [0])
    up, down, *ready = lax.optimization_barrier((up, down, *came.values()))
    came = dict(zip(others, ready))
    rest = jnp.concatenate(ready, axis=0)
    rest = hops(
        after(rest, own[1][0], own[2][0]), others, lambda piece: after(piece, own[-1][0])
    )

    ups, downs = [shifted(up, "col", 1), came[1]], [shifted(down, "col", -1), came[col_count - 1]]
    first_shifts = [0, 1]
    middle_shifts = list(range(2, steps)) + list(range(col_count - 1, steps, -1))

    cut = len(rest) * 3 // 4
    columns = own + rest + [swap_cores(own + rest[:2], 10**9)]
    columns.append(swap_cores(rest[2:cut], 0) if cut == 3 else swap_cores(rest[2:cut], 10**9))
    for piece, held in tied(rest[cut:], ups[0], keep_cube):
        parts = [swap_cores([(piece[:, at : at + width // 2], held)], 0) for at in (0, width // 2)]
        columns.append((jnp.concatenate([piece for piece, _ in parts], axis=1), parts[0][1]))
    flops = 2 * rows_one * order * width

    def square_call(name, count, filled, extra, inputs, kernel):
        return call(
            kernel,
            name,
            [full(count * rows_one, width), half(count * rows_one, width)] + extra,
            inputs,
            filled,
            limit=12,
        )

    square_first, half_first, left_first, right = square_call(
        "square_first",
        2,
        0,
        [half(2 * rows_one, order), half(order, width)],
        [keep_square, local, *ups, *[piece for piece, _ in columns]],
        functools.partial(square_first_kernel, sizes, first_shifts, [held for _, held in columns]),
    )
    for step in range(2, steps + 1):
        up = after(ups[-2], downs[-2], half_first)
        up = jnp.concatenate([up[:, width:], came[step - 1]], axis=1)
        ups += [shifted(up, "col", 1), came[step]]
        if step < steps:
            back = col_count - step
            down = jnp.concatenate([came[back + 1], downs[-2][:, :-width]], axis=1)
            downs += [shifted(down, "col", -1), came[back]]
    left_middle = call(
        functools.partial(stack_kernel, col_count),
        "stack",
        half(rows - rows_one, order),
        [left_first, *ups[2:-2], *downs],
        10**8,
    )
    first = hops(half_first, first_shifts)
    square_middle, half_middle = square_call(
        "square_middle",
        len(middle_shifts),
        0,
        [],
        [keep_square, right, left_middle],
        functools.partial(square_last_kernel, sizes, middle_shifts),
    )
    left = call(
        functools.partial(stack_kernel, col_count),
        "stack",
        half(rows, order),
        [left_middle, *ups[-2:]],
        2 * 10**9,
    )
    middle = hops(half_middle, middle_shifts)
    square_last, half_last = square_call(
        "square_last",
        1,
        flops,
        [],
        [keep_square, after(right, first[-1][0], middle[-1][0]), left],
        functools.partial(square_last_kernel, sizes, [steps]),
    )
    picked = call(
        functools.partial(pick_kernel, sizes, steps),
        "pick",
        half(rows, order // col_count),
        [left],
        2 * 10**10,
        [pltpu.VMEM((order, order // col_count), jnp.bfloat16)],
        16,
    )
    last = hops(half_last, [steps], hold=lambda piece: after(piece, picked))
    firsts = first + middle
    firsts = firsts + [
        swap_cores(tied(first, half_last), 10**9),
        swap_cores(tied(middle, half_last), 10**9),
    ]
    started = call(
        functools.partial(
            cube_first_kernel,
            sizes,
            [first_shifts, middle_shifts, [steps]],
            [held for _, held in firsts],
        ),
        "cube_first",
        full(rows, width),
        [after(keep_cube, last[1][0], last[2][0]), left, square_first, square_middle, square_last]
        + [piece for piece, _ in firsts],
        10**10,
        [pltpu.VMEM((order, width), jnp.bfloat16)],
        16,
    )
    lasts = last + [swap_cores(last[:cut], 10**9), swap_cores(tied(last[cut:], started), 10**9)]
    return call(
        functools.partial(cube_last_kernel, sizes, first_shifts + middle_shifts, [held for _, held in lasts]),
        "cube_last",
        full(rows, width),
        [keep_cube, picked, started, *[piece for piece, _ in lasts]],
        flops,
        [pltpu.VMEM((order // col_count, width), jnp.bfloat16)],
        10,
    )


def solution(mesh):
    placed = (P(("row", "col"), None), P(), P(), P())
    return jax.shard_map(
        on_device, mesh=mesh, in_specs=placed, out_specs=P("row", "col"), check_vma=False
    )
```

```python
import functools

import jax
import jax.numpy as jnp
from jax import lax
from jax.experimental import pallas as pl
from jax.experimental.pallas import tpu as pltpu
from jax.sharding import PartitionSpec as P

BLK = 128
VMEM = pl.BlockSpec(memory_space=pltpu.VMEM)


def shifted(block, axis, distance):
    size = lax.axis_size(axis)
    return lax.ppermute(block, axis, [(i, (i + distance) % size) for i in range(size)])


def xor_moved(block, axis, bit_of):
    size = lax.axis_size(axis)
    return lax.ppermute(block, axis, [(i, i ^ bit_of(i)) for i in range(size)])


def hops(block, held, hold_base=lambda piece: piece, hold=lambda piece: piece):
    count = lax.axis_size("row")
    bits = [1 << b for b in range(1, count.bit_length() - 1)]
    items = [(block, 0, 0)]
    for low, high in zip(bits, bits[::-1]):

        def bit_of(i, low=low, high=high):
            return high if i & 1 else low

        items = items + [
            (xor_moved(piece if even == 0 else hold(piece), "row", bit_of), even ^ low, odd ^ high)
            for piece, even, odd in items
        ]
        items[0] = (hold_base(block), 0, 0)
    return [(piece, [(even, odd, held)]) for piece, even, odd in items]


def hint(flops):
    return pl.CostEstimate(flops=flops, bytes_accessed=0, transcendentals=0)


def call(kernel, name, out_shape, inputs, flops, scratch=(), limit=4):
    return pl.pallas_call(
        kernel,
        out_shape=out_shape,
        in_specs=[VMEM] * len(inputs),
        out_specs=jax.tree.map(lambda shape: VMEM, out_shape),
        scratch_shapes=scratch,
        compiler_params=pltpu.CompilerParams(vmem_limit_bytes=limit << 20),
        cost_estimate=hint(flops),
        name=name,
    )(*inputs)


def half(*shape):
    return jax.ShapeDtypeStruct(shape, jnp.bfloat16)


def full(*shape):
    return jax.ShapeDtypeStruct(shape, jnp.float32)


def join_kernel(*refs):
    *piece_refs, out_ref = refs
    row = 0
    for ref in piece_refs:
        out_ref[row : row + ref.shape[0], :] = ref[...]
        row += ref.shape[0]


def swap_cores(items, flops):
    pieces = [piece for piece, _ in items]
    joined = pieces[0]
    if len(pieces) > 1:
        rows = sum(piece.shape[0] for piece in pieces)
        joined = call(join_kernel, "join", half(rows, pieces[0].shape[1]), pieces, flops)
    held = [(odd ^ 1, even ^ 1, shifts) for _, parts in items for even, odd, shifts in parts]
    return xor_moved(joined, "row", lambda i: 1), held


def tied(items, *others):
    ready = lax.optimization_barrier((*[piece for piece, _ in items], *others))
    return [(piece, held) for piece, (_, held) in zip(ready, items)]


def iota(shape, axis):
    return lax.broadcasted_iota(jnp.int32, shape, axis)


def expand(mask, row_start, rows, col_start, cols):
    nblocks = mask.shape[0]
    pick_row = (row_start + iota((rows, nblocks), 0)) // BLK == iota((rows, nblocks), 1)
    pick_col = (col_start + iota((nblocks, cols), 1)) // BLK == iota((nblocks, cols), 0)
    lines = jnp.dot(
        pick_row.astype(jnp.bfloat16),
        mask.astype(jnp.float32).astype(jnp.bfloat16),
        preferred_element_type=jnp.float32,
    )
    return jnp.dot(
        lines.astype(jnp.bfloat16),
        pick_col.astype(jnp.bfloat16),
        preferred_element_type=jnp.float32,
    ).astype(jnp.bfloat16)


def block_at(shift, col_count, width):
    return pl.multiple_of(lax.rem(lax.axis_index("col") + shift, col_count) * width, BLK)


def sub_at(shift, col_count, rows_one):
    return pl.multiple_of(
        lax.rem(lax.axis_index("col") + (col_count - shift), col_count) * rows_one, 16
    )


def cut_kernel(col_count, pattern_ref, density_ref, local_ref, up_ref, down_ref, *piece_refs):
    rows_one, order = density_ref.shape
    width = order // col_count
    first = lax.axis_index("row") * (col_count * rows_one) + sub_at(0, col_count, rows_one)
    local_ref[...] = density_ref[...] * expand(pattern_ref[...], first, rows_one, 0, order)
    for shift, piece_ref in enumerate(piece_refs):
        piece = local_ref[:, pl.ds(block_at(shift, col_count, width), width)]
        piece_ref[...] = piece
        if shift != 1:
            slot = (shift - 2) % col_count
            up_ref[:, slot * width : (slot + 1) * width] = piece
        if shift != col_count - 1:
            down_ref[:, shift * width : (shift + 1) * width] = piece


def keep_kernel(filter_ref, keep_ref):
    rows, width = keep_ref.shape
    row_at, col_at = lax.axis_index("row") * rows, lax.axis_index("col") * width
    keep_ref[...] = expand(filter_ref[...], row_at, rows, col_at, width)


def fill_left(left, first, whole_refs, pair_refs, col_count):
    at = first
    for ref in whole_refs:
        left[at : at + ref.shape[0], :] = ref[...]
        at += ref.shape[0]
    for most_ref, own_ref in zip(pair_refs[::2], pair_refs[1::2]):
        rows_one, width = own_ref.shape
        left[at : at + rows_one, pl.ds(block_at(0, col_count, width), width)] = own_ref[...]
        for slot in range(col_count - 1):
            columns = pl.ds(block_at(slot + 1, col_count, width), width)
            left[at : at + rows_one, columns] = most_ref[:, slot * width : (slot + 1) * width]
        at += rows_one


def fill_right(right, refs, layouts, sizes):
    row_count, col_count = sizes
    rows = right.shape[0] // row_count
    rows_one = rows // col_count
    row_id = lax.axis_index("row")
    odd_core = lax.rem(row_id, 2) == 1
    for ref, held in zip(refs, layouts):
        row = 0
        for even, odd, shifts in held:
            place = pl.multiple_of((row_id ^ jnp.where(odd_core, odd, even)) * rows, BLK)
            for shift in shifts:
                at = pl.multiple_of(place + sub_at(shift, col_count, rows_one), 16)
                right[pl.ds(at, rows_one), :] = ref[row : row + rows_one, :]
                row += rows_one


def split_refs(refs, counts):
    groups = []
    for count in counts:
        groups.append(refs[:count])
        refs = refs[count:]
    return groups + [refs]


def square_part(left, right, shifts, col_count, keep_ref, square_ref, half_ref):
    rows_one = square_ref.shape[0] // len(shifts)
    total = jnp.dot(left, right, preferred_element_type=jnp.float32)
    for slot, shift in enumerate(shifts):
        at = slice(slot * rows_one, (slot + 1) * rows_one)
        keep = keep_ref[pl.ds(sub_at(shift, col_count, rows_one), rows_one), :]
        part = total[at] * keep.astype(jnp.float32)
        square_ref[at, :] = part
        half_ref[at, :] = part.astype(jnp.bfloat16)


def square_first_kernel(sizes, shifts, layouts, keep_ref, local_ref, *refs):
    pair_refs, piece_refs, rest = split_refs(refs, [2 * len(shifts) - 2, len(layouts)])
    square_ref, half_ref, left_ref, right_ref = rest
    fill_left(left_ref, 0, [local_ref], pair_refs, sizes[1])
    fill_right(right_ref, piece_refs, layouts, sizes)
    square_part(left_ref[...], right_ref[...], shifts, sizes[1], keep_ref, square_ref, half_ref)


def stack_kernel(col_count, before_ref, *refs):
    *pair_refs, left_ref = refs
    fill_left(left_ref, 0, [before_ref], pair_refs, col_count)


def square_last_kernel(sizes, shifts, keep_ref, right_ref, left_ref, square_ref, half_ref):
    left = left_ref[-square_ref.shape[0] :, :]
    square_part(left, right_ref[...], shifts, sizes[1], keep_ref, square_ref, half_ref)


def pick_kernel(sizes, shift, left_ref, picked_ref, select):
    row_count, col_count = sizes
    order, count = select.shape
    rows_one = count // row_count
    column = iota((order, count), 1)
    from_row = column + (column // rows_one) * (order // row_count - rows_one)
    from_row = from_row + sub_at(shift, col_count, rows_one)
    select[...] = (iota((order, count), 0) == from_row).astype(jnp.bfloat16)
    picked = jnp.dot(left_ref[...], select[...], preferred_element_type=jnp.float32)
    picked_ref[...] = picked.astype(jnp.bfloat16)


def cube_first_kernel(sizes, chunk_shifts, layouts, keep_ref, left_ref, *refs):
    square_refs, piece_refs, rest = split_refs(refs, [len(chunk_shifts), len(layouts)])
    out_ref, right = rest
    rows_one = out_ref.shape[0] // sizes[1]
    right[...] = jnp.zeros_like(right)
    fill_right(right, piece_refs, layouts, sizes)
    total = jnp.dot(left_ref[...], right[...], preferred_element_type=jnp.float32)
    row = 0
    for square_ref, shifts in zip(square_refs, chunk_shifts):
        for slot, shift in enumerate(shifts):
            part = slice(row, row + rows_one)
            keep = keep_ref[pl.ds(sub_at(shift, sizes[1], rows_one), rows_one), :]
            square = square_ref[slot * rows_one : (slot + 1) * rows_one, :]
            out_ref[part, :] = 3.0 * square - 2.0 * (total[part] * keep.astype(jnp.float32))
            row += rows_one


def cube_last_kernel(sizes, shifts, layouts, keep_ref, picked_ref, started_ref, *refs):
    *piece_refs, out_ref, right = refs
    row_count, col_count = sizes
    rows_one = right.shape[0] // row_count
    row_id = lax.axis_index("row")
    odd_core = lax.rem(row_id, 2) == 1
    for ref, held in zip(piece_refs, layouts):
        for slot, (even, odd, _) in enumerate(held):
            place = pl.multiple_of((row_id ^ jnp.where(odd_core, odd, even)) * rows_one, 16)
            right[pl.ds(place, rows_one), :] = ref[slot * rows_one : (slot + 1) * rows_one, :]
    total = jnp.dot(picked_ref[...], right[...], preferred_element_type=jnp.float32)
    for slot, shift in enumerate(shifts + [col_count // 2]):
        part = slice(slot * rows_one, (slot + 1) * rows_one)
        at = pl.ds(sub_at(shift, col_count, rows_one), rows_one)
        out_ref[at, :] = started_ref[part, :] - 2.0 * (
            total[part] * keep_ref[at, :].astype(jnp.float32)
        )


def after(value, *others):
    return lax.optimization_barrier((value, *others))[0]


def on_device(density, pattern, filter_square, filter_cube):
    sizes = (lax.axis_size("row"), lax.axis_size("col"))
    row_count, col_count = sizes
    rows_one, order = density.shape
    rows = order // row_count
    width = order // col_count
    steps = col_count // 2

    local, up, down, *pieces = call(
        functools.partial(cut_kernel, col_count),
        "cut",
        [half(rows_one, order)]
        + [half(rows_one, order - width)] * 2
        + [half(rows_one, width)] * col_count,
        [pattern, density],
        10**9,
    )
    keep_square, keep_cube = (
        call(keep_kernel, "keep", half(rows, width), [mask], 2 * 10**10)
        for mask in (filter_square, filter_cube)
    )
    others = list(range(1, col_count))
    came = {shift: shifted(pieces[shift], "col", shift) for shift in others}
    own = hops(after(pieces[0], keep_square), [0])
    up, down, *ready = lax.optimization_barrier((up, down, *came.values()))
    came = dict(zip(others, ready))
    rest = jnp.concatenate(ready, axis=0)
    rest = hops(
        after(rest, own[1][0], own[2][0]), others, lambda piece: after(piece, own[-1][0])
    )

    ups, downs = [shifted(up, "col", 1), came[1]], [shifted(down, "col", -1), came[col_count - 1]]
    first_shifts = [0, 1]
    middle_shifts = list(range(2, steps)) + list(range(col_count - 1, steps, -1))

    cut = len(rest) * 3 // 4
    columns = own + rest + [swap_cores(own + rest[:2], 10**9)]
    columns.append(swap_cores(rest[2:cut], 0) if cut == 3 else swap_cores(rest[2:cut], 10**9))
    for piece, held in tied(rest[cut:], ups[0], keep_cube):
        parts = [swap_cores([(piece[:, at : at + width // 2], held)], 0) for at in (0, width // 2)]
        columns.append((jnp.concatenate([piece for piece, _ in parts], axis=1), parts[0][1]))
    flops = 2 * rows_one * order * width

    def square_call(name, count, filled, extra, inputs, kernel):
        return call(
            kernel,
            name,
            [full(count * rows_one, width), half(count * rows_one, width)] + extra,
            inputs,
            filled,
            limit=12,
        )

    square_first, half_first, left_first, right = square_call(
        "square_first",
        2,
        0,
        [half(2 * rows_one, order), half(order, width)],
        [keep_square, local, *ups, *[piece for piece, _ in columns]],
        functools.partial(square_first_kernel, sizes, first_shifts, [held for _, held in columns]),
    )
    for step in range(2, steps + 1):
        up = after(ups[-2], downs[-2], half_first)
        up = jnp.concatenate([up[:, width:], came[step - 1]], axis=1)
        ups += [shifted(up, "col", 1), came[step]]
        if step < steps:
            back = col_count - step
            down = jnp.concatenate([came[back + 1], downs[-2][:, :-width]], axis=1)
            downs += [shifted(down, "col", -1), came[back]]
    left_middle = call(
        functools.partial(stack_kernel, col_count),
        "stack",
        half(rows - rows_one, order),
        [left_first, *ups[2:-2], *downs],
        10**8,
    )
    first = hops(half_first, first_shifts)
    square_middle, half_middle = square_call(
        "square_middle",
        len(middle_shifts),
        0,
        [],
        [keep_square, after(right, first[1][0]), left_middle],
        functools.partial(square_last_kernel, sizes, middle_shifts),
    )
    left = call(
        functools.partial(stack_kernel, col_count),
        "stack",
        half(rows, order),
        [left_middle, *ups[-2:]],
        2 * 10**9,
    )
    middle = hops(half_middle, middle_shifts)
    square_last, half_last = square_call(
        "square_last",
        1,
        2 * 10**10,
        [],
        [keep_square, after(right, middle[1][0]), left],
        functools.partial(square_last_kernel, sizes, [steps]),
    )
    picked = call(
        functools.partial(pick_kernel, sizes, steps),
        "pick",
        half(rows, order // col_count),
        [left],
        2 * 10**10,
        [pltpu.VMEM((order, order // col_count), jnp.bfloat16)],
        16,
    )
    last = hops(half_last, [steps], hold=lambda piece: after(piece, picked))
    firsts = first + middle
    firsts = firsts + [
        swap_cores(tied(first, half_last), 10**9),
        swap_cores(tied(middle, half_last), 10**9),
    ]
    started = call(
        functools.partial(
            cube_first_kernel,
            sizes,
            [first_shifts, middle_shifts, [steps]],
            [held for _, held in firsts],
        ),
        "cube_first",
        full(rows, width),
        [after(keep_cube, last[1][0], last[2][0]), left, square_first, square_middle, square_last]
        + [piece for piece, _ in firsts],
        10**10,
        [pltpu.VMEM((order, width), jnp.bfloat16)],
        16,
    )
    lasts = last + [swap_cores(last[:cut], 10**9), swap_cores(tied(last[cut:], started), 10**9)]
    return call(
        functools.partial(cube_last_kernel, sizes, first_shifts + middle_shifts, [held for _, held in lasts]),
        "cube_last",
        full(rows, width),
        [keep_cube, picked, started, *[piece for piece, _ in lasts]],
        flops,
        [pltpu.VMEM((order // col_count, width), jnp.bfloat16)],
        10,
    )


def solution(mesh):
    placed = (P(("row", "col"), None), P(), P(), P())
    return jax.shard_map(
        on_device, mesh=mesh, in_specs=placed, out_specs=P("row", "col"), check_vma=False
    )
```

```python
import functools

import jax
import jax.numpy as jnp
from jax import lax
from jax.experimental import pallas as pl
from jax.experimental.pallas import tpu as pltpu
from jax.sharding import PartitionSpec as P

BLK = 128
VMEM = pl.BlockSpec(memory_space=pltpu.VMEM)


def shifted(block, axis, distance):
    size = lax.axis_size(axis)
    return lax.ppermute(block, axis, [(i, (i + distance) % size) for i in range(size)])


def xor_moved(block, axis, bit_of):
    size = lax.axis_size(axis)
    return lax.ppermute(block, axis, [(i, i ^ bit_of(i)) for i in range(size)])


def hops(block, held, hold_base=lambda piece: piece, hold=lambda piece: piece):
    count = lax.axis_size("row")
    bits = [1 << b for b in range(1, count.bit_length() - 1)]
    items = [(block, 0, 0)]
    for low, high in zip(bits, bits[::-1]):

        def bit_of(i, low=low, high=high):
            return high if i & 1 else low

        items = items + [
            (xor_moved(piece if even == 0 else hold(piece), "row", bit_of), even ^ low, odd ^ high)
            for piece, even, odd in items
        ]
        items[0] = (hold_base(block), 0, 0)
    return [(piece, [(even, odd, held)]) for piece, even, odd in items]


def hint(flops):
    return pl.CostEstimate(flops=flops, bytes_accessed=0, transcendentals=0)


def call(kernel, name, out_shape, inputs, flops, scratch=(), limit=4):
    return pl.pallas_call(
        kernel,
        out_shape=out_shape,
        in_specs=[VMEM] * len(inputs),
        out_specs=jax.tree.map(lambda shape: VMEM, out_shape),
        scratch_shapes=scratch,
        compiler_params=pltpu.CompilerParams(vmem_limit_bytes=limit << 20),
        cost_estimate=hint(flops),
        name=name,
    )(*inputs)


def half(*shape):
    return jax.ShapeDtypeStruct(shape, jnp.bfloat16)


def full(*shape):
    return jax.ShapeDtypeStruct(shape, jnp.float32)


def join_kernel(*refs):
    *piece_refs, out_ref = refs
    row = 0
    for ref in piece_refs:
        out_ref[row : row + ref.shape[0], :] = ref[...]
        row += ref.shape[0]


def swap_cores(items, flops):
    pieces = [piece for piece, _ in items]
    joined = pieces[0]
    if len(pieces) > 1:
        rows = sum(piece.shape[0] for piece in pieces)
        joined = call(join_kernel, "join", half(rows, pieces[0].shape[1]), pieces, flops)
    held = [(odd ^ 1, even ^ 1, shifts) for _, parts in items for even, odd, shifts in parts]
    return xor_moved(joined, "row", lambda i: 1), held


def tied(items, *others):
    ready = lax.optimization_barrier((*[piece for piece, _ in items], *others))
    return [(piece, held) for piece, (_, held) in zip(ready, items)]


def iota(shape, axis):
    return lax.broadcasted_iota(jnp.int32, shape, axis)


def expand(mask, row_start, rows, col_start, cols):
    nblocks = mask.shape[0]
    pick_row = (row_start + iota((rows, nblocks), 0)) // BLK == iota((rows, nblocks), 1)
    pick_col = (col_start + iota((nblocks, cols), 1)) // BLK == iota((nblocks, cols), 0)
    lines = jnp.dot(
        pick_row.astype(jnp.bfloat16),
        mask.astype(jnp.float32).astype(jnp.bfloat16),
        preferred_element_type=jnp.float32,
    )
    return jnp.dot(
        lines.astype(jnp.bfloat16),
        pick_col.astype(jnp.bfloat16),
        preferred_element_type=jnp.float32,
    ).astype(jnp.bfloat16)


def block_at(shift, col_count, width):
    return pl.multiple_of(lax.rem(lax.axis_index("col") + shift, col_count) * width, BLK)


def sub_at(shift, col_count, rows_one):
    return pl.multiple_of(
        lax.rem(lax.axis_index("col") + (col_count - shift), col_count) * rows_one, 16
    )


def cut_kernel(col_count, pattern_ref, density_ref, local_ref, up_ref, down_ref, *piece_refs):
    rows_one, order = density_ref.shape
    width = order // col_count
    first = lax.axis_index("row") * (col_count * rows_one) + sub_at(0, col_count, rows_one)
    local_ref[...] = density_ref[...] * expand(pattern_ref[...], first, rows_one, 0, order)
    for shift, piece_ref in enumerate(piece_refs):
        piece = local_ref[:, pl.ds(block_at(shift, col_count, width), width)]
        piece_ref[...] = piece
        if shift != 1:
            slot = (shift - 2) % col_count
            up_ref[:, slot * width : (slot + 1) * width] = piece
        if shift != col_count - 1:
            down_ref[:, shift * width : (shift + 1) * width] = piece


def keep_kernel(filter_ref, keep_ref):
    rows, width = keep_ref.shape
    row_at, col_at = lax.axis_index("row") * rows, lax.axis_index("col") * width
    keep_ref[...] = expand(filter_ref[...], row_at, rows, col_at, width)


def fill_left(left, first, whole_refs, pair_refs, col_count):
    at = first
    for ref in whole_refs:
        left[at : at + ref.shape[0], :] = ref[...]
        at += ref.shape[0]
    for most_ref, own_ref in zip(pair_refs[::2], pair_refs[1::2]):
        rows_one, width = own_ref.shape
        left[at : at + rows_one, pl.ds(block_at(0, col_count, width), width)] = own_ref[...]
        for slot in range(col_count - 1):
            columns = pl.ds(block_at(slot + 1, col_count, width), width)
            left[at : at + rows_one, columns] = most_ref[:, slot * width : (slot + 1) * width]
        at += rows_one


def fill_right(right, refs, layouts, sizes):
    row_count, col_count = sizes
    rows = right.shape[0] // row_count
    rows_one = rows // col_count
    row_id = lax.axis_index("row")
    odd_core = lax.rem(row_id, 2) == 1
    for ref, held in zip(refs, layouts):
        row = 0
        for even, odd, shifts in held:
            place = pl.multiple_of((row_id ^ jnp.where(odd_core, odd, even)) * rows, BLK)
            for shift in shifts:
                at = pl.multiple_of(place + sub_at(shift, col_count, rows_one), 16)
                right[pl.ds(at, rows_one), :] = ref[row : row + rows_one, :]
                row += rows_one


def split_refs(refs, counts):
    groups = []
    for count in counts:
        groups.append(refs[:count])
        refs = refs[count:]
    return groups + [refs]


def square_part(left, right, shifts, col_count, keep_ref, square_ref, half_ref):
    rows_one = square_ref.shape[0] // len(shifts)
    total = jnp.dot(left, right, preferred_element_type=jnp.float32)
    for slot, shift in enumerate(shifts):
        at = slice(slot * rows_one, (slot + 1) * rows_one)
        keep = keep_ref[pl.ds(sub_at(shift, col_count, rows_one), rows_one), :]
        part = total[at] * keep.astype(jnp.float32)
        square_ref[at, :] = part
        half_ref[at, :] = part.astype(jnp.bfloat16)


def square_first_kernel(sizes, shifts, layouts, keep_ref, local_ref, *refs):
    pair_refs, piece_refs, rest = split_refs(refs, [2 * len(shifts) - 2, len(layouts)])
    square_ref, half_ref, left_ref, right_ref = rest
    fill_left(left_ref, 0, [local_ref], pair_refs, sizes[1])
    fill_right(right_ref, piece_refs, layouts, sizes)
    square_part(left_ref[...], right_ref[...], shifts, sizes[1], keep_ref, square_ref, half_ref)


def stack_kernel(col_count, before_ref, *refs):
    *pair_refs, left_ref = refs
    fill_left(left_ref, 0, [before_ref], pair_refs, col_count)


def square_last_kernel(sizes, shifts, keep_ref, right_ref, left_ref, square_ref, half_ref):
    left = left_ref[-square_ref.shape[0] :, :]
    square_part(left, right_ref[...], shifts, sizes[1], keep_ref, square_ref, half_ref)


def pick_kernel(sizes, shift, left_ref, picked_ref, select):
    row_count, col_count = sizes
    order, count = select.shape
    rows_one = count // row_count
    column = iota((order, count), 1)
    from_row = column + (column // rows_one) * (order // row_count - rows_one)
    from_row = from_row + sub_at(shift, col_count, rows_one)
    select[...] = (iota((order, count), 0) == from_row).astype(jnp.bfloat16)
    picked = jnp.dot(left_ref[...], select[...], preferred_element_type=jnp.float32)
    picked_ref[...] = picked.astype(jnp.bfloat16)


def cube_first_kernel(sizes, chunk_shifts, layouts, keep_ref, left_ref, *refs):
    square_refs, piece_refs, rest = split_refs(refs, [len(chunk_shifts), len(layouts)])
    out_ref, right = rest
    rows_one = out_ref.shape[0] // sizes[1]
    right[...] = jnp.zeros_like(right)
    fill_right(right, piece_refs, layouts, sizes)
    total = jnp.dot(left_ref[...], right[...], preferred_element_type=jnp.float32)
    row = 0
    for square_ref, shifts in zip(square_refs, chunk_shifts):
        for slot, shift in enumerate(shifts):
            part = slice(row, row + rows_one)
            keep = keep_ref[pl.ds(sub_at(shift, sizes[1], rows_one), rows_one), :]
            square = square_ref[slot * rows_one : (slot + 1) * rows_one, :]
            out_ref[part, :] = 3.0 * square - 2.0 * (total[part] * keep.astype(jnp.float32))
            row += rows_one


def cube_last_kernel(sizes, shifts, layouts, keep_ref, picked_ref, started_ref, *refs):
    *piece_refs, out_ref, right = refs
    row_count, col_count = sizes
    rows_one = right.shape[0] // row_count
    row_id = lax.axis_index("row")
    odd_core = lax.rem(row_id, 2) == 1
    for ref, held in zip(piece_refs, layouts):
        for slot, (even, odd, _) in enumerate(held):
            place = pl.multiple_of((row_id ^ jnp.where(odd_core, odd, even)) * rows_one, 16)
            right[pl.ds(place, rows_one), :] = ref[slot * rows_one : (slot + 1) * rows_one, :]
    total = jnp.dot(picked_ref[...], right[...], preferred_element_type=jnp.float32)
    for slot, shift in enumerate(shifts + [col_count // 2]):
        part = slice(slot * rows_one, (slot + 1) * rows_one)
        at = pl.ds(sub_at(shift, col_count, rows_one), rows_one)
        out_ref[at, :] = started_ref[part, :] - 2.0 * (
            total[part] * keep_ref[at, :].astype(jnp.float32)
        )


def after(value, *others):
    return lax.optimization_barrier((value, *others))[0]


def on_device(density, pattern, filter_square, filter_cube):
    sizes = (lax.axis_size("row"), lax.axis_size("col"))
    row_count, col_count = sizes
    rows_one, order = density.shape
    rows = order // row_count
    width = order // col_count
    steps = col_count // 2

    local, up, down, *pieces = call(
        functools.partial(cut_kernel, col_count),
        "cut",
        [half(rows_one, order)]
        + [half(rows_one, order - width)] * 2
        + [half(rows_one, width)] * col_count,
        [pattern, density],
        10**9,
    )
    keep_square, keep_cube = (
        call(keep_kernel, "keep", half(rows, width), [mask], 2 * 10**10)
        for mask in (filter_square, filter_cube)
    )
    others = list(range(1, col_count))
    came = {shift: shifted(pieces[shift], "col", shift) for shift in others}
    own = hops(after(pieces[0], keep_square), [0])
    up, down, *ready = lax.optimization_barrier((up, down, *came.values()))
    came = dict(zip(others, ready))
    rest = jnp.concatenate(ready, axis=0)
    rest = hops(
        after(rest, own[1][0], own[2][0]), others, lambda piece: after(piece, own[-1][0])
    )

    ups, downs = [shifted(up, "col", 1), came[1]], [shifted(down, "col", -1), came[col_count - 1]]
    first_shifts = [0, 1]
    middle_shifts = list(range(2, steps)) + list(range(col_count - 1, steps, -1))

    cut = len(rest) * 3 // 4
    columns = own + rest + [swap_cores(own + rest[:2], 10**9)]
    columns.append(swap_cores(rest[2:cut], 0) if cut == 3 else swap_cores(rest[2:cut], 10**9))
    for piece, held in tied(rest[cut:], ups[0], keep_cube):
        parts = [swap_cores([(piece[:, at : at + width // 2], held)], 0) for at in (0, width // 2)]
        columns.append((jnp.concatenate([piece for piece, _ in parts], axis=1), parts[0][1]))
    flops = 2 * rows_one * order * width

    def square_call(name, count, filled, extra, inputs, kernel):
        return call(
            kernel,
            name,
            [full(count * rows_one, width), half(count * rows_one, width)] + extra,
            inputs,
            filled,
            limit=12,
        )

    square_first, half_first, left_first, right = square_call(
        "square_first",
        2,
        0,
        [half(2 * rows_one, order), half(order, width)],
        [keep_square, local, *ups, *[piece for piece, _ in columns]],
        functools.partial(square_first_kernel, sizes, first_shifts, [held for _, held in columns]),
    )
    for step in range(2, steps + 1):
        up = after(ups[-2], downs[-2], half_first)
        up = jnp.concatenate([up[:, width:], came[step - 1]], axis=1)
        ups += [shifted(up, "col", 1), came[step]]
        if step < steps:
            back = col_count - step
            down = jnp.concatenate([came[back + 1], downs[-2][:, :-width]], axis=1)
            downs += [shifted(down, "col", -1), came[back]]
    left_middle = call(
        functools.partial(stack_kernel, col_count),
        "stack",
        half(rows - rows_one, order),
        [left_first, *ups[2:-2], *downs],
        10**8,
    )
    first = hops(half_first, first_shifts)
    square_middle, half_middle = square_call(
        "square_middle",
        len(middle_shifts),
        0,
        [],
        [keep_square, after(right, first[1][0]), left_middle],
        functools.partial(square_last_kernel, sizes, middle_shifts),
    )
    left = call(
        functools.partial(stack_kernel, col_count),
        "stack",
        half(rows, order),
        [left_middle, *ups[-2:]],
        2 * 10**9,
    )
    middle = hops(half_middle, middle_shifts, hold=lambda piece: after(piece, first[2][0]))
    square_last, half_last = square_call(
        "square_last",
        1,
        2 * 10**10,
        [],
        [keep_square, after(right, middle[1][0]), left],
        functools.partial(square_last_kernel, sizes, [steps]),
    )
    picked = call(
        functools.partial(pick_kernel, sizes, steps),
        "pick",
        half(rows, order // col_count),
        [left],
        2 * 10**10,
        [pltpu.VMEM((order, order // col_count), jnp.bfloat16)],
        16,
    )
    last = hops(half_last, [steps], hold=lambda piece: after(piece, picked))
    firsts = first + middle
    firsts = firsts + [
        swap_cores(tied(first, half_last), 10**9),
        swap_cores(tied(middle, half_last), 10**9),
    ]
    started = call(
        functools.partial(
            cube_first_kernel,
            sizes,
            [first_shifts, middle_shifts, [steps]],
            [held for _, held in firsts],
        ),
        "cube_first",
        full(rows, width),
        [after(keep_cube, last[1][0], last[2][0]), left, square_first, square_middle, square_last]
        + [piece for piece, _ in firsts],
        10**10,
        [pltpu.VMEM((order, width), jnp.bfloat16)],
        16,
    )
    lasts = last + [swap_cores(last[:cut], 10**9), swap_cores(tied(last[cut:], started), 10**9)]
    return call(
        functools.partial(cube_last_kernel, sizes, first_shifts + middle_shifts, [held for _, held in lasts]),
        "cube_last",
        full(rows, width),
        [keep_cube, picked, started, *[piece for piece, _ in lasts]],
        flops,
        [pltpu.VMEM((order // col_count, width), jnp.bfloat16)],
        10,
    )


def solution(mesh):
    placed = (P(("row", "col"), None), P(), P(), P())
    return jax.shard_map(
        on_device, mesh=mesh, in_specs=placed, out_specs=P("row", "col"), check_vma=False
    )
```

```python
import functools

import jax
import jax.numpy as jnp
from jax import lax
from jax.experimental import pallas as pl
from jax.experimental.pallas import tpu as pltpu
from jax.sharding import PartitionSpec as P

BLK = 128
VMEM = pl.BlockSpec(memory_space=pltpu.VMEM)


def shifted(block, axis, distance):
    size = lax.axis_size(axis)
    return lax.ppermute(block, axis, [(i, (i + distance) % size) for i in range(size)])


def xor_moved(block, axis, bit_of):
    size = lax.axis_size(axis)
    return lax.ppermute(block, axis, [(i, i ^ bit_of(i)) for i in range(size)])


def hops(block, held, hold_base=lambda piece: piece, hold=lambda piece: piece):
    count = lax.axis_size("row")
    bits = [1 << b for b in range(1, count.bit_length() - 1)]
    items = [(block, 0, 0)]
    for low, high in zip(bits, bits[::-1]):

        def bit_of(i, low=low, high=high):
            return high if i & 1 else low

        items = items + [
            (xor_moved(piece if even == 0 else hold(piece), "row", bit_of), even ^ low, odd ^ high)
            for piece, even, odd in items
        ]
        items[0] = (hold_base(block), 0, 0)
    return [(piece, [(even, odd, held)]) for piece, even, odd in items]


def direct(block, held):
    count = lax.axis_size("row")
    moved = [(xor_moved(block, "row", lambda i, bits=bits: bits), bits) for bits in range(2, count, 2)]
    return [(block, [(0, 0, held)])] + [(piece, [(bits, bits, held)]) for piece, bits in moved]


def hint(flops):
    return pl.CostEstimate(flops=flops, bytes_accessed=0, transcendentals=0)


def call(kernel, name, out_shape, inputs, flops, scratch=(), limit=4):
    return pl.pallas_call(
        kernel,
        out_shape=out_shape,
        in_specs=[VMEM] * len(inputs),
        out_specs=jax.tree.map(lambda shape: VMEM, out_shape),
        scratch_shapes=scratch,
        compiler_params=pltpu.CompilerParams(vmem_limit_bytes=limit << 20),
        cost_estimate=hint(flops),
        name=name,
    )(*inputs)


def half(*shape):
    return jax.ShapeDtypeStruct(shape, jnp.bfloat16)


def full(*shape):
    return jax.ShapeDtypeStruct(shape, jnp.float32)


def join_kernel(*refs):
    *piece_refs, out_ref = refs
    row = 0
    for ref in piece_refs:
        out_ref[row : row + ref.shape[0], :] = ref[...]
        row += ref.shape[0]


def swap_cores(items, flops):
    pieces = [piece for piece, _ in items]
    joined = pieces[0]
    if len(pieces) > 1:
        rows = sum(piece.shape[0] for piece in pieces)
        joined = call(join_kernel, "join", half(rows, pieces[0].shape[1]), pieces, flops)
    held = [(odd ^ 1, even ^ 1, shifts) for _, parts in items for even, odd, shifts in parts]
    return xor_moved(joined, "row", lambda i: 1), held


def tied(items, *others):
    ready = lax.optimization_barrier((*[piece for piece, _ in items], *others))
    return [(piece, held) for piece, (_, held) in zip(ready, items)]


def iota(shape, axis):
    return lax.broadcasted_iota(jnp.int32, shape, axis)


def expand(mask, row_start, rows, col_start, cols):
    nblocks = mask.shape[0]
    pick_row = (row_start + iota((rows, nblocks), 0)) // BLK == iota((rows, nblocks), 1)
    pick_col = (col_start + iota((nblocks, cols), 1)) // BLK == iota((nblocks, cols), 0)
    lines = jnp.dot(
        pick_row.astype(jnp.bfloat16),
        mask.astype(jnp.float32).astype(jnp.bfloat16),
        preferred_element_type=jnp.float32,
    )
    return jnp.dot(
        lines.astype(jnp.bfloat16),
        pick_col.astype(jnp.bfloat16),
        preferred_element_type=jnp.float32,
    ).astype(jnp.bfloat16)


def block_at(shift, col_count, width):
    return pl.multiple_of(lax.rem(lax.axis_index("col") + shift, col_count) * width, BLK)


def sub_at(shift, col_count, rows_one):
    return pl.multiple_of(
        lax.rem(lax.axis_index("col") + (col_count - shift), col_count) * rows_one, 16
    )


def cut_kernel(col_count, pattern_ref, density_ref, local_ref, up_ref, down_ref, *piece_refs):
    rows_one, order = density_ref.shape
    width = order // col_count
    first = lax.axis_index("row") * (col_count * rows_one) + sub_at(0, col_count, rows_one)
    local_ref[...] = density_ref[...] * expand(pattern_ref[...], first, rows_one, 0, order)
    for shift, piece_ref in enumerate(piece_refs):
        piece = local_ref[:, pl.ds(block_at(shift, col_count, width), width)]
        piece_ref[...] = piece
        if shift != 1:
            slot = (shift - 2) % col_count
            up_ref[:, slot * width : (slot + 1) * width] = piece
        if shift != col_count - 1:
            down_ref[:, shift * width : (shift + 1) * width] = piece


def keep_kernel(filter_ref, keep_ref):
    rows, width = keep_ref.shape
    row_at, col_at = lax.axis_index("row") * rows, lax.axis_index("col") * width
    keep_ref[...] = expand(filter_ref[...], row_at, rows, col_at, width)


def fill_left(left, first, whole_refs, pair_refs, col_count):
    at = first
    for ref in whole_refs:
        left[at : at + ref.shape[0], :] = ref[...]
        at += ref.shape[0]
    for most_ref, own_ref in zip(pair_refs[::2], pair_refs[1::2]):
        rows_one, width = own_ref.shape
        left[at : at + rows_one, pl.ds(block_at(0, col_count, width), width)] = own_ref[...]
        for slot in range(col_count - 1):
            columns = pl.ds(block_at(slot + 1, col_count, width), width)
            left[at : at + rows_one, columns] = most_ref[:, slot * width : (slot + 1) * width]
        at += rows_one


def fill_right(right, refs, layouts, sizes):
    row_count, col_count = sizes
    rows = right.shape[0] // row_count
    rows_one = rows // col_count
    row_id = lax.axis_index("row")
    odd_core = lax.rem(row_id, 2) == 1
    for ref, held in zip(refs, layouts):
        row = 0
        for even, odd, shifts in held:
            place = pl.multiple_of((row_id ^ jnp.where(odd_core, odd, even)) * rows, BLK)
            for shift in shifts:
                at = pl.multiple_of(place + sub_at(shift, col_count, rows_one), 16)
                right[pl.ds(at, rows_one), :] = ref[row : row + rows_one, :]
                row += rows_one


def split_refs(refs, counts):
    groups = []
    for count in counts:
        groups.append(refs[:count])
        refs = refs[count:]
    return groups + [refs]


def square_part(left, right, shifts, col_count, keep_ref, square_ref, half_ref):
    rows_one = square_ref.shape[0] // len(shifts)
    total = jnp.dot(left, right, preferred_element_type=jnp.float32)
    for slot, shift in enumerate(shifts):
        at = slice(slot * rows_one, (slot + 1) * rows_one)
        keep = keep_ref[pl.ds(sub_at(shift, col_count, rows_one), rows_one), :]
        part = total[at] * keep.astype(jnp.float32)
        square_ref[at, :] = part
        half_ref[at, :] = part.astype(jnp.bfloat16)


def square_first_kernel(sizes, shifts, layouts, keep_ref, local_ref, *refs):
    pair_refs, piece_refs, rest = split_refs(refs, [2 * len(shifts) - 2, len(layouts)])
    square_ref, half_ref, left_ref, right_ref = rest
    fill_left(left_ref, 0, [local_ref], pair_refs, sizes[1])
    fill_right(right_ref, piece_refs, layouts, sizes)
    square_part(left_ref[...], right_ref[...], shifts, sizes[1], keep_ref, square_ref, half_ref)


def stack_kernel(col_count, before_ref, *refs):
    *pair_refs, left_ref = refs
    fill_left(left_ref, 0, [before_ref], pair_refs, col_count)


def square_last_kernel(sizes, shifts, keep_ref, right_ref, left_ref, square_ref, half_ref):
    left = left_ref[-square_ref.shape[0] :, :]
    square_part(left, right_ref[...], shifts, sizes[1], keep_ref, square_ref, half_ref)


def pick_kernel(sizes, shift, left_ref, picked_ref, select):
    row_count, col_count = sizes
    order, count = select.shape
    rows_one = count // row_count
    column = iota((order, count), 1)
    from_row = column + (column // rows_one) * (order // row_count - rows_one)
    from_row = from_row + sub_at(shift, col_count, rows_one)
    select[...] = (iota((order, count), 0) == from_row).astype(jnp.bfloat16)
    picked = jnp.dot(left_ref[...], select[...], preferred_element_type=jnp.float32)
    picked_ref[...] = picked.astype(jnp.bfloat16)


def cube_first_kernel(sizes, chunk_shifts, layouts, keep_ref, left_ref, *refs):
    square_refs, piece_refs, rest = split_refs(refs, [len(chunk_shifts), len(layouts)])
    out_ref, right = rest
    rows_one = out_ref.shape[0] // sizes[1]
    right[...] = jnp.zeros_like(right)
    fill_right(right, piece_refs, layouts, sizes)
    total = jnp.dot(left_ref[...], right[...], preferred_element_type=jnp.float32)
    row = 0
    for square_ref, shifts in zip(square_refs, chunk_shifts):
        for slot, shift in enumerate(shifts):
            part = slice(row, row + rows_one)
            keep = keep_ref[pl.ds(sub_at(shift, sizes[1], rows_one), rows_one), :]
            square = square_ref[slot * rows_one : (slot + 1) * rows_one, :]
            out_ref[part, :] = 3.0 * square - 2.0 * (total[part] * keep.astype(jnp.float32))
            row += rows_one


def cube_last_kernel(sizes, shifts, layouts, keep_ref, picked_ref, started_ref, *refs):
    *piece_refs, out_ref, right = refs
    row_count, col_count = sizes
    rows_one = right.shape[0] // row_count
    row_id = lax.axis_index("row")
    odd_core = lax.rem(row_id, 2) == 1
    for ref, held in zip(piece_refs, layouts):
        for slot, (even, odd, _) in enumerate(held):
            place = pl.multiple_of((row_id ^ jnp.where(odd_core, odd, even)) * rows_one, 16)
            right[pl.ds(place, rows_one), :] = ref[slot * rows_one : (slot + 1) * rows_one, :]
    total = jnp.dot(picked_ref[...], right[...], preferred_element_type=jnp.float32)
    for slot, shift in enumerate(shifts + [col_count // 2]):
        part = slice(slot * rows_one, (slot + 1) * rows_one)
        at = pl.ds(sub_at(shift, col_count, rows_one), rows_one)
        out_ref[at, :] = started_ref[part, :] - 2.0 * (
            total[part] * keep_ref[at, :].astype(jnp.float32)
        )


def after(value, *others):
    return lax.optimization_barrier((value, *others))[0]


def on_device(density, pattern, filter_square, filter_cube):
    sizes = (lax.axis_size("row"), lax.axis_size("col"))
    row_count, col_count = sizes
    rows_one, order = density.shape
    rows = order // row_count
    width = order // col_count
    steps = col_count // 2

    local, up, down, *pieces = call(
        functools.partial(cut_kernel, col_count),
        "cut",
        [half(rows_one, order)]
        + [half(rows_one, order - width)] * 2
        + [half(rows_one, width)] * col_count,
        [pattern, density],
        10**9,
    )
    keep_square, keep_cube = (
        call(keep_kernel, "keep", half(rows, width), [mask], 2 * 10**10)
        for mask in (filter_square, filter_cube)
    )
    others = list(range(1, col_count))
    came = {shift: shifted(pieces[shift], "col", shift) for shift in others}
    own = hops(after(pieces[0], keep_square), [0])
    up, down, *ready = lax.optimization_barrier((up, down, *came.values()))
    came = dict(zip(others, ready))
    rest = jnp.concatenate(ready, axis=0)
    rest = hops(
        after(rest, own[1][0], own[2][0]), others, lambda piece: after(piece, own[-1][0])
    )

    ups, downs = [shifted(up, "col", 1), came[1]], [shifted(down, "col", -1), came[col_count - 1]]
    first_shifts = [0, 1]
    middle_shifts = list(range(2, steps)) + list(range(col_count - 1, steps, -1))

    cut = len(rest) * 3 // 4
    columns = own + rest + [swap_cores(own + rest[:2], 10**9)]
    columns.append(swap_cores(rest[2:cut], 0) if cut == 3 else swap_cores(rest[2:cut], 10**9))
    for piece, held in tied(rest[cut:], ups[0], keep_cube):
        parts = [swap_cores([(piece[:, at : at + width // 2], held)], 0) for at in (0, width // 2)]
        columns.append((jnp.concatenate([piece for piece, _ in parts], axis=1), parts[0][1]))
    flops = 2 * rows_one * order * width

    def square_call(name, count, filled, extra, inputs, kernel):
        return call(
            kernel,
            name,
            [full(count * rows_one, width), half(count * rows_one, width)] + extra,
            inputs,
            filled,
            limit=12,
        )

    square_first, half_first, left_first, right = square_call(
        "square_first",
        2,
        0,
        [half(2 * rows_one, order), half(order, width)],
        [keep_square, local, *ups, *[piece for piece, _ in columns]],
        functools.partial(square_first_kernel, sizes, first_shifts, [held for _, held in columns]),
    )
    for step in range(2, steps + 1):
        up = after(ups[-2], downs[-2], half_first)
        up = jnp.concatenate([up[:, width:], came[step - 1]], axis=1)
        ups += [shifted(up, "col", 1), came[step]]
        if step < steps:
            back = col_count - step
            down = jnp.concatenate([came[back + 1], downs[-2][:, :-width]], axis=1)
            downs += [shifted(down, "col", -1), came[back]]
    left_middle = call(
        functools.partial(stack_kernel, col_count),
        "stack",
        half(rows - rows_one, order),
        [left_first, *ups[2:-2], *downs],
        10**8,
    )
    first = hops(half_first, first_shifts)
    square_middle, half_middle = square_call(
        "square_middle",
        len(middle_shifts),
        0,
        [],
        [keep_square, after(right, first[1][0]), left_middle],
        functools.partial(square_last_kernel, sizes, middle_shifts),
    )
    left = call(
        functools.partial(stack_kernel, col_count),
        "stack",
        half(rows, order),
        [left_middle, *ups[-2:]],
        2 * 10**9,
    )
    middle = hops(half_middle, middle_shifts, hold=lambda piece: after(piece, first[2][0]))
    square_last, half_last = square_call(
        "square_last",
        1,
        2 * 10**10,
        [],
        [keep_square, after(right, middle[1][0]), left],
        functools.partial(square_last_kernel, sizes, [steps]),
    )
    picked = call(
        functools.partial(pick_kernel, sizes, steps),
        "pick",
        half(rows, order // col_count),
        [left],
        2 * 10**10,
        [pltpu.VMEM((order, order // col_count), jnp.bfloat16)],
        16,
    )
    last = direct(half_last, [steps])
    firsts = first + middle
    firsts = firsts + [
        swap_cores(tied(first, half_last), 10**9),
        swap_cores(tied(middle, half_last), 10**9),
    ]
    started = call(
        functools.partial(
            cube_first_kernel,
            sizes,
            [first_shifts, middle_shifts, [steps]],
            [held for _, held in firsts],
        ),
        "cube_first",
        full(rows, width),
        [after(keep_cube, picked), left, square_first, square_middle, square_last]
        + [piece for piece, _ in firsts],
        10**10,
        [pltpu.VMEM((order, width), jnp.bfloat16)],
        16,
    )
    lasts = last + [swap_cores(last[:cut], 10**9), swap_cores(tied(last[cut:], started), 10**9)]
    return call(
        functools.partial(cube_last_kernel, sizes, first_shifts + middle_shifts, [held for _, held in lasts]),
        "cube_last",
        full(rows, width),
        [keep_cube, picked, started, *[piece for piece, _ in lasts]],
        flops,
        [pltpu.VMEM((order // col_count, width), jnp.bfloat16)],
        10,
    )


def solution(mesh):
    placed = (P(("row", "col"), None), P(), P(), P())
    return jax.shard_map(
        on_device, mesh=mesh, in_specs=placed, out_specs=P("row", "col"), check_vma=False
    )
```

```python
import functools

import jax
import jax.numpy as jnp
from jax import lax
from jax.experimental import pallas as pl
from jax.experimental.pallas import tpu as pltpu
from jax.sharding import PartitionSpec as P

BLK = 128
VMEM = pl.BlockSpec(memory_space=pltpu.VMEM)


def shifted(block, axis, distance):
    size = lax.axis_size(axis)
    return lax.ppermute(block, axis, [(i, (i + distance) % size) for i in range(size)])


def xor_moved(block, axis, bit_of):
    size = lax.axis_size(axis)
    return lax.ppermute(block, axis, [(i, i ^ bit_of(i)) for i in range(size)])


def hops(block, held, hold_base=lambda piece: piece, hold=lambda piece: piece):
    count = lax.axis_size("row")
    bits = [1 << b for b in range(1, count.bit_length() - 1)]
    items = [(block, 0, 0)]
    for low, high in zip(bits, bits[::-1]):

        def bit_of(i, low=low, high=high):
            return high if i & 1 else low

        items = items + [
            (xor_moved(piece if even == 0 else hold(piece), "row", bit_of), even ^ low, odd ^ high)
            for piece, even, odd in items
        ]
        items[0] = (hold_base(block), 0, 0)
    return [(piece, [(even, odd, held)]) for piece, even, odd in items]


def direct(block, held):
    count = lax.axis_size("row")
    moved = [(xor_moved(block, "row", lambda i, bits=bits: bits), bits) for bits in range(2, count, 2)]
    return [(block, [(0, 0, held)])] + [(piece, [(bits, bits, held)]) for piece, bits in moved]


def hint(flops):
    return pl.CostEstimate(flops=flops, bytes_accessed=0, transcendentals=0)


def call(kernel, name, out_shape, inputs, flops, scratch=(), limit=4):
    return pl.pallas_call(
        kernel,
        out_shape=out_shape,
        in_specs=[VMEM] * len(inputs),
        out_specs=jax.tree.map(lambda shape: VMEM, out_shape),
        scratch_shapes=scratch,
        compiler_params=pltpu.CompilerParams(vmem_limit_bytes=limit << 20),
        cost_estimate=hint(flops),
        name=name,
    )(*inputs)


def half(*shape):
    return jax.ShapeDtypeStruct(shape, jnp.bfloat16)


def full(*shape):
    return jax.ShapeDtypeStruct(shape, jnp.float32)


def join_kernel(*refs):
    *piece_refs, out_ref = refs
    row = 0
    for ref in piece_refs:
        out_ref[row : row + ref.shape[0], :] = ref[...]
        row += ref.shape[0]


def swap_cores(items, flops):
    pieces = [piece for piece, _ in items]
    joined = pieces[0]
    if len(pieces) > 1:
        rows = sum(piece.shape[0] for piece in pieces)
        joined = call(join_kernel, "join", half(rows, pieces[0].shape[1]), pieces, flops)
    held = [(odd ^ 1, even ^ 1, shifts) for _, parts in items for even, odd, shifts in parts]
    return xor_moved(joined, "row", lambda i: 1), held


def tied(items, *others):
    ready = lax.optimization_barrier((*[piece for piece, _ in items], *others))
    return [(piece, held) for piece, (_, held) in zip(ready, items)]


def iota(shape, axis):
    return lax.broadcasted_iota(jnp.int32, shape, axis)


def expand(mask, row_start, rows, col_start, cols):
    nblocks = mask.shape[0]
    pick_row = (row_start + iota((rows, nblocks), 0)) // BLK == iota((rows, nblocks), 1)
    pick_col = (col_start + iota((nblocks, cols), 1)) // BLK == iota((nblocks, cols), 0)
    lines = jnp.dot(
        pick_row.astype(jnp.bfloat16),
        mask.astype(jnp.float32).astype(jnp.bfloat16),
        preferred_element_type=jnp.float32,
    )
    return jnp.dot(
        lines.astype(jnp.bfloat16),
        pick_col.astype(jnp.bfloat16),
        preferred_element_type=jnp.float32,
    ).astype(jnp.bfloat16)


def block_at(shift, col_count, width):
    return pl.multiple_of(lax.rem(lax.axis_index("col") + shift, col_count) * width, BLK)


def sub_at(shift, col_count, rows_one):
    return pl.multiple_of(
        lax.rem(lax.axis_index("col") + (col_count - shift), col_count) * rows_one, 16
    )


def cut_kernel(col_count, pattern_ref, density_ref, local_ref, up_ref, down_ref, *piece_refs):
    rows_one, order = density_ref.shape
    width = order // col_count
    first = lax.axis_index("row") * (col_count * rows_one) + sub_at(0, col_count, rows_one)
    local_ref[...] = density_ref[...] * expand(pattern_ref[...], first, rows_one, 0, order)
    for shift, piece_ref in enumerate(piece_refs):
        piece = local_ref[:, pl.ds(block_at(shift, col_count, width), width)]
        piece_ref[...] = piece
        if shift != 1:
            slot = (shift - 2) % col_count
            up_ref[:, slot * width : (slot + 1) * width] = piece
        if shift != col_count - 1:
            down_ref[:, shift * width : (shift + 1) * width] = piece


def keep_kernel(filter_ref, keep_ref):
    rows, width = keep_ref.shape
    row_at, col_at = lax.axis_index("row") * rows, lax.axis_index("col") * width
    keep_ref[...] = expand(filter_ref[...], row_at, rows, col_at, width)


def fill_left(left, first, whole_refs, pair_refs, col_count):
    at = first
    for ref in whole_refs:
        left[at : at + ref.shape[0], :] = ref[...]
        at += ref.shape[0]
    for most_ref, own_ref in zip(pair_refs[::2], pair_refs[1::2]):
        rows_one, width = own_ref.shape
        left[at : at + rows_one, pl.ds(block_at(0, col_count, width), width)] = own_ref[...]
        for slot in range(col_count - 1):
            columns = pl.ds(block_at(slot + 1, col_count, width), width)
            left[at : at + rows_one, columns] = most_ref[:, slot * width : (slot + 1) * width]
        at += rows_one


def fill_right(right, refs, layouts, sizes):
    row_count, col_count = sizes
    rows = right.shape[0] // row_count
    rows_one = rows // col_count
    row_id = lax.axis_index("row")
    odd_core = lax.rem(row_id, 2) == 1
    for ref, held in zip(refs, layouts):
        row = 0
        for even, odd, shifts in held:
            place = pl.multiple_of((row_id ^ jnp.where(odd_core, odd, even)) * rows, BLK)
            for shift in shifts:
                at = pl.multiple_of(place + sub_at(shift, col_count, rows_one), 16)
                right[pl.ds(at, rows_one), :] = ref[row : row + rows_one, :]
                row += rows_one


def split_refs(refs, counts):
    groups = []
    for count in counts:
        groups.append(refs[:count])
        refs = refs[count:]
    return groups + [refs]


def square_part(left, right, shifts, col_count, keep_ref, square_ref, half_ref):
    rows_one = square_ref.shape[0] // len(shifts)
    total = jnp.dot(left, right, preferred_element_type=jnp.float32)
    for slot, shift in enumerate(shifts):
        at = slice(slot * rows_one, (slot + 1) * rows_one)
        keep = keep_ref[pl.ds(sub_at(shift, col_count, rows_one), rows_one), :]
        part = total[at] * keep.astype(jnp.float32)
        square_ref[at, :] = part
        half_ref[at, :] = part.astype(jnp.bfloat16)


def square_first_kernel(sizes, shifts, layouts, keep_ref, local_ref, *refs):
    pair_refs, piece_refs, rest = split_refs(refs, [2 * len(shifts) - 2, len(layouts)])
    square_ref, half_ref, left_ref, right_ref = rest
    fill_left(left_ref, 0, [local_ref], pair_refs, sizes[1])
    fill_right(right_ref, piece_refs, layouts, sizes)
    square_part(left_ref[...], right_ref[...], shifts, sizes[1], keep_ref, square_ref, half_ref)


def stack_kernel(col_count, before_ref, *refs):
    *pair_refs, left_ref = refs
    fill_left(left_ref, 0, [before_ref], pair_refs, col_count)


def square_last_kernel(sizes, shifts, keep_ref, right_ref, left_ref, square_ref, half_ref):
    left = left_ref[-square_ref.shape[0] :, :]
    square_part(left, right_ref[...], shifts, sizes[1], keep_ref, square_ref, half_ref)


def pick_kernel(sizes, shift, left_ref, picked_ref, select):
    row_count, col_count = sizes
    order, count = select.shape
    rows_one = count // row_count
    column = iota((order, count), 1)
    from_row = column + (column // rows_one) * (order // row_count - rows_one)
    from_row = from_row + sub_at(shift, col_count, rows_one)
    select[...] = (iota((order, count), 0) == from_row).astype(jnp.bfloat16)
    picked = jnp.dot(left_ref[...], select[...], preferred_element_type=jnp.float32)
    picked_ref[...] = picked.astype(jnp.bfloat16)


def cube_first_kernel(sizes, chunk_shifts, layouts, keep_ref, left_ref, *refs):
    square_refs, piece_refs, rest = split_refs(refs, [len(chunk_shifts), len(layouts)])
    out_ref, right = rest
    rows_one = out_ref.shape[0] // sizes[1]
    right[...] = jnp.zeros_like(right)
    fill_right(right, piece_refs, layouts, sizes)
    total = jnp.dot(left_ref[...], right[...], preferred_element_type=jnp.float32)
    row = 0
    for square_ref, shifts in zip(square_refs, chunk_shifts):
        for slot, shift in enumerate(shifts):
            part = slice(row, row + rows_one)
            keep = keep_ref[pl.ds(sub_at(shift, sizes[1], rows_one), rows_one), :]
            square = square_ref[slot * rows_one : (slot + 1) * rows_one, :]
            out_ref[part, :] = 3.0 * square - 2.0 * (total[part] * keep.astype(jnp.float32))
            row += rows_one


def cube_last_kernel(sizes, shifts, layouts, keep_ref, picked_ref, started_ref, *refs):
    *piece_refs, out_ref, right = refs
    row_count, col_count = sizes
    rows_one = right.shape[0] // row_count
    row_id = lax.axis_index("row")
    odd_core = lax.rem(row_id, 2) == 1
    for ref, held in zip(piece_refs, layouts):
        for slot, (even, odd, _) in enumerate(held):
            place = pl.multiple_of((row_id ^ jnp.where(odd_core, odd, even)) * rows_one, 16)
            right[pl.ds(place, rows_one), :] = ref[slot * rows_one : (slot + 1) * rows_one, :]
    total = jnp.dot(picked_ref[...], right[...], preferred_element_type=jnp.float32)
    for slot, shift in enumerate(shifts + [col_count // 2]):
        part = slice(slot * rows_one, (slot + 1) * rows_one)
        at = pl.ds(sub_at(shift, col_count, rows_one), rows_one)
        out_ref[at, :] = started_ref[part, :] - 2.0 * (
            total[part] * keep_ref[at, :].astype(jnp.float32)
        )


def after(value, *others):
    return lax.optimization_barrier((value, *others))[0]


def on_device(density, pattern, filter_square, filter_cube):
    sizes = (lax.axis_size("row"), lax.axis_size("col"))
    row_count, col_count = sizes
    rows_one, order = density.shape
    rows = order // row_count
    width = order // col_count
    steps = col_count // 2

    local, up, down, *pieces = call(
        functools.partial(cut_kernel, col_count),
        "cut",
        [half(rows_one, order)]
        + [half(rows_one, order - width)] * 2
        + [half(rows_one, width)] * col_count,
        [pattern, density],
        10**9,
    )
    keep_square, keep_cube = (
        call(keep_kernel, "keep", half(rows, width), [mask], 2 * 10**10)
        for mask in (filter_square, filter_cube)
    )
    others = list(range(1, col_count))
    came = {shift: shifted(pieces[shift], "col", shift) for shift in others}
    own = hops(after(pieces[0], keep_square), [0])
    up, down, *ready = lax.optimization_barrier((up, down, *came.values()))
    came = dict(zip(others, ready))
    rest = jnp.concatenate(ready, axis=0)
    rest = hops(
        after(rest, own[1][0], own[2][0]), others, lambda piece: after(piece, own[-1][0])
    )

    ups, downs = [shifted(up, "col", 1), came[1]], [shifted(down, "col", -1), came[col_count - 1]]
    first_shifts = [0, 1]
    middle_shifts = list(range(2, steps)) + list(range(col_count - 1, steps, -1))

    cut = len(rest) * 3 // 4
    columns = own + rest + [swap_cores(own + rest[:2], 10**9)]
    columns.append(swap_cores(rest[2:cut], 0) if cut == 3 else swap_cores(rest[2:cut], 10**9))
    for piece, held in tied(rest[cut:], ups[0], keep_cube):
        parts = [swap_cores([(piece[:, at : at + width // 2], held)], 0) for at in (0, width // 2)]
        columns.append((jnp.concatenate([piece for piece, _ in parts], axis=1), parts[0][1]))
    flops = 2 * rows_one * order * width

    def square_call(name, count, filled, extra, inputs, kernel):
        return call(
            kernel,
            name,
            [full(count * rows_one, width), half(count * rows_one, width)] + extra,
            inputs,
            filled,
            limit=12,
        )

    square_first, half_first, left_first, right = square_call(
        "square_first",
        2,
        0,
        [half(2 * rows_one, order), half(order, width)],
        [keep_square, local, *ups, *[piece for piece, _ in columns]],
        functools.partial(square_first_kernel, sizes, first_shifts, [held for _, held in columns]),
    )
    for step in range(2, steps + 1):
        up = after(ups[-2], downs[-2], half_first)
        up = jnp.concatenate([up[:, width:], came[step - 1]], axis=1)
        ups += [shifted(up, "col", 1), came[step]]
        if step < steps:
            back = col_count - step
            down = jnp.concatenate([came[back + 1], downs[-2][:, :-width]], axis=1)
            downs += [shifted(down, "col", -1), came[back]]
    left_middle = call(
        functools.partial(stack_kernel, col_count),
        "stack",
        half(rows - rows_one, order),
        [left_first, *ups[2:-2], *downs],
        10**8,
    )
    first = hops(half_first, first_shifts)
    square_middle, half_middle = square_call(
        "square_middle",
        len(middle_shifts),
        0,
        [],
        [keep_square, after(right, first[1][0]), left_middle],
        functools.partial(square_last_kernel, sizes, middle_shifts),
    )
    left = call(
        functools.partial(stack_kernel, col_count),
        "stack",
        half(rows, order),
        [left_middle, *ups[-2:]],
        2 * 10**9,
    )
    middle = hops(half_middle, middle_shifts, hold=lambda piece: after(piece, first[2][0]))
    square_last, half_last = square_call(
        "square_last",
        1,
        2 * 10**10,
        [],
        [keep_square, after(right, middle[1][0]), left],
        functools.partial(square_last_kernel, sizes, [steps]),
    )
    picked = call(
        functools.partial(pick_kernel, sizes, steps),
        "pick",
        half(rows, order // col_count),
        [left],
        2 * 10**10,
        [pltpu.VMEM((order, order // col_count), jnp.bfloat16)],
        16,
    )
    last = direct(half_last, [steps])
    firsts = first + middle
    firsts = firsts + [
        swap_cores(tied(first, half_last), 10**9),
        swap_cores(tied(middle, half_last), 10**9),
    ]
    started = call(
        functools.partial(
            cube_first_kernel,
            sizes,
            [first_shifts, middle_shifts, [steps]],
            [held for _, held in firsts],
        ),
        "cube_first",
        full(rows, width),
        [after(keep_cube, picked), left, square_first, square_middle, square_last]
        + [piece for piece, _ in firsts],
        10**10,
        [pltpu.VMEM((order, width), jnp.bfloat16)],
        16,
    )
    lasts = last + [swap_cores(tied(last, started), 10**9)]
    return call(
        functools.partial(cube_last_kernel, sizes, first_shifts + middle_shifts, [held for _, held in lasts]),
        "cube_last",
        full(rows, width),
        [keep_cube, picked, started, *[piece for piece, _ in lasts]],
        flops,
        [pltpu.VMEM((order // col_count, width), jnp.bfloat16)],
        10,
    )


def solution(mesh):
    placed = (P(("row", "col"), None), P(), P(), P())
    return jax.shard_map(
        on_device, mesh=mesh, in_specs=placed, out_specs=P("row", "col"), check_vma=False
    )
```
